32 devices in a mesh: dp: 16 (over z, y, core), seq: 2 (over x).
Axes of the slice: x: 2, y: 2, z: 4, core: 2. Of those that a mesh axis runs over, the one named last changes fastest.
Arguments:
- tile_feats: bfloat16 [8192, 2048], P('dp'), may hold values from -6 to 6
- tile_pos: int32 [16, 512], P('dp'), may hold values from -1 to 511, as said below
- slide_count: int32 [16], P('dp'), may hold values from 128 to 512, as said below
- w_proj: bfloat16 [2048, 768], P(None, 'seq'), may hold values from -0.125 to 0.125
- emb_grad: bfloat16 [16, 512, 768], P('dp', 'seq'), may hold values from -6 to 6
- ln_gain: float32 [768], replicated, may hold values from 0.25 to 1.75
- w_qkv: bfloat16 [768, 2304], P('dp'), may hold values from -1.5 to 1.5
- w_out: bfloat16 [768, 768], P('dp'), may hold values from -0.21875 to 0.21875
Outputs:
- slide_emb: bfloat16 [16, 512, 768], P('dp', 'seq')
- attn_branch: bfloat16 [16, 512, 768], P('dp', 'seq')
- proj_grad: float32 [2048, 768], P(None, 'seq')
The draws below stay inside these ranges and needn't reach their ends.
Inputs may be any that keep to these rules, and one draw needn't show every extreme that they name: `tile_pos`: slot j of a row belongs to slide j // 32. Each position below a slide's slide_count is held by exactly one slot of that slide over all rows; all other slots hold -1. `slide_count`: some slide is full.
All inputs are finite; a program needn't handle non-finite values.
Results may differ from the reference program's by a relative error of at most 0.017.
The reference program's roundings to bfloat16 on the way (of `emb_tiles`, `normed`, `projected`, `context` and `slot_grad`) count: a program that leaves them out, or rounds other values in their place, can miss the bound.
Values may be sent and summed in bfloat16 or wider, within the bound.
A program may use at most 128 MiB of HBM per device.

```python
import jax
import jax.numpy as jnp
from jax import lax

FEAT = 2048
D = 768
HEAD_COUNT = 12
HEAD_WIDTH = 64
DILATION_STEP = 4
SEQ_DEV = 256
SLIDES = 16
SLIDE_LENGTH = 512
MOST = 32
SLOTS = 512
N_SEQ = 2


def slide_layout(key):
    base = jax.random.fold_in(key, 11)
    count_key, pick_key, order_key = jax.random.split(base, 3)
    counts = jax.random.randint(count_key, (SLIDES,), SLIDE_LENGTH // 4, SLIDE_LENGTH + 1)
    chosen = jax.random.randint(pick_key, (), 0, SLIDES)
    counts = jnp.where(jnp.arange(SLIDES) == chosen, SLIDE_LENGTH, counts).astype(jnp.int32)
    order_keys = jax.random.split(order_key, SLIDES)

    def one_order(single_key):
        return jax.random.permutation(single_key, SLIDE_LENGTH)
    orders = jax.vmap(one_order)(order_keys).astype(jnp.int32)
    return (counts, orders)


def draw_slide_count(key, part):
    return slide_layout(key)[0]


def draw_tile_pos(key, part):
    counts, orders = slide_layout(key)
    placed = jnp.where(orders < counts[:, None], orders, -1)
    grouped = placed.reshape(SLIDES, SLIDES, MOST).transpose(1, 0, 2)
    return grouped.reshape(SLIDES, SLOTS).astype(jnp.int32)


def draw_w_qkv(key, part):
    bound_value = (3.0 / D) ** 0.5
    values = jax.random.uniform(jax.random.fold_in(key, 5), (D, 3 * HEAD_COUNT * HEAD_WIDTH), jnp.float32, -bound_value, bound_value)
    return values.astype(jnp.bfloat16)


def level_of(rng, dims, cuts, smallest, high):
    def one(dim, blocks):
        draws = jax.random.uniform(jax.random.fold_in(jax.random.fold_in(rng, 6), dim), (blocks,), jnp.float32, smallest / len(cuts), high / len(cuts))
        return jnp.repeat(jnp.exp(draws), dims[dim] // blocks).reshape((-1,) + (1,) * (len(dims) - dim - 1))

    factor_of = one(*cuts[0])
    for cut in cuts[1:]:
        factor_of = factor_of * one(*cut)
    return factor_of


def normal_values(key, extent, deviation, limit, pieces=(), held_as=jnp.bfloat16):
    level = level_of(key, extent, pieces, -0.22, 0.18) if pieces else 1.0
    result = jax.random.normal(key, extent, jnp.float32) * deviation * level
    return jnp.minimum(jnp.maximum(result, -limit), limit).astype(held_as)


def setup_inputs(seed: int = 0) -> dict:
    streams_of = jax.random.split(jax.random.key(seed), 9)
    return {
        "tile_feats": normal_values(streams_of[0], (SLIDES * SLOTS, FEAT), 1.0, 6.0, ((0, 16),)),
        "tile_pos": draw_tile_pos(jax.random.fold_in(streams_of[8], 71), 0),
        "slide_count": draw_slide_count(jax.random.fold_in(streams_of[8], 71), 0),
        "w_proj": normal_values(streams_of[3], (FEAT, D), FEAT ** -0.5, 0.125, ((1, 2),)),
        "emb_grad": normal_values(streams_of[4], (SLIDES, SLIDE_LENGTH, D), 1.0, 6.0, ((0, 16), (1, 2))),
        "ln_gain": jnp.clip(1.0 + 0.15 * jax.random.normal(streams_of[5], (D,), jnp.float32), 0.25, 1.75),
        "w_qkv": draw_w_qkv(jax.random.fold_in(streams_of[8], 71), 0),
        "w_out": normal_values(streams_of[7], (HEAD_COUNT * HEAD_WIDTH, D), (HEAD_COUNT * HEAD_WIDTH) ** -0.5, 0.21875, ((0, 16),)),
    }


NEGATIVE = -1e+30
EPSILON = 1e-05

def attend_slide(slide_rows, tile_count, ln_gain, w_qkv, w_out):
    inner = HEAD_COUNT * HEAD_WIDTH
    scale = HEAD_WIDTH ** (-0.5)
    widened = slide_rows.astype(jnp.float32)
    center = lax.optimization_barrier(jnp.mean(widened, axis=-1, keepdims=True))
    spread = lax.optimization_barrier(jnp.mean(jnp.square(widened - center), axis=-1, keepdims=True))
    normed = ((widened - center) * lax.rsqrt(spread + EPSILON) * ln_gain).astype(jnp.bfloat16)
    projected = jnp.dot(normed, w_qkv, preferred_element_type=jnp.float32).astype(jnp.bfloat16)
    query_rows = projected[:, :inner].reshape(SLIDE_LENGTH, HEAD_COUNT, HEAD_WIDTH).astype(jnp.float32)
    key_matrix = projected[:, inner:2 * inner].reshape(SLIDE_LENGTH, HEAD_COUNT, HEAD_WIDTH).astype(jnp.float32)
    value_matrix = projected[:, 2 * inner:].reshape(SLIDE_LENGTH, HEAD_COUNT, HEAD_WIDTH).astype(jnp.float32)
    sequence_position = jnp.arange(SLIDE_LENGTH, dtype=jnp.int32)
    occupied = sequence_position < tile_count
    shift_amounts = jnp.arange(HEAD_COUNT, dtype=jnp.int32) % DILATION_STEP
    permitted_mask = sequence_position[None, :] % DILATION_STEP == shift_amounts[:, None]
    block_q = query_rows.reshape(N_SEQ, SEQ_DEV, HEAD_COUNT, HEAD_WIDTH)
    block_k = key_matrix.reshape(N_SEQ, SEQ_DEV, HEAD_COUNT, HEAD_WIDTH)
    block_v = value_matrix.reshape(N_SEQ, SEQ_DEV, HEAD_COUNT, HEAD_WIDTH)
    local_scores = jnp.einsum('bqhd,bkhd->hbqk', block_q, block_k) * scale
    local_ok = jnp.broadcast_to(occupied.reshape(N_SEQ, SEQ_DEV)[None, :, None, :], local_scores.shape)
    local_scores = local_scores.reshape(HEAD_COUNT, SLIDE_LENGTH, SEQ_DEV)
    local_ok = local_ok.reshape(HEAD_COUNT, SLIDE_LENGTH, SEQ_DEV)
    stepped_keys = key_matrix.reshape(SLIDE_LENGTH // DILATION_STEP, DILATION_STEP, HEAD_COUNT, HEAD_WIDTH)
    stepped_values = value_matrix.reshape(SLIDE_LENGTH // DILATION_STEP, DILATION_STEP, HEAD_COUNT, HEAD_WIDTH)
    distant_keys = jnp.stack([stepped_keys[:, head_number % DILATION_STEP, head_number, :] for head_number in range(HEAD_COUNT)])
    distant_values = jnp.stack([stepped_values[:, head_number % DILATION_STEP, head_number, :] for head_number in range(HEAD_COUNT)])
    distant_position = DILATION_STEP * jnp.arange(SLIDE_LENGTH // DILATION_STEP, dtype=jnp.int32)[None, :] + shift_amounts[:, None]
    far_scores = jnp.einsum('qhd,hkd->hqk', query_rows, distant_keys) * scale
    far_ok = (distant_position < tile_count)[:, None, :] & permitted_mask[:, :, None]
    maxima = jnp.maximum(lax.optimization_barrier(jnp.max(jnp.where(local_ok, local_scores, NEGATIVE), axis=-1)), lax.optimization_barrier(jnp.max(jnp.where(far_ok, far_scores, NEGATIVE), axis=-1)))
    local_weight = jnp.where(local_ok, jnp.exp(local_scores - maxima[..., None]), 0.0)
    far_weight = jnp.where(far_ok, jnp.exp(far_scores - maxima[..., None]), 0.0)
    totals = lax.optimization_barrier(jnp.sum(local_weight, axis=-1)) + lax.optimization_barrier(jnp.sum(far_weight, axis=-1))
    nearby_accumulator = jnp.einsum('hbqk,bkhd->hbqd', local_weight.reshape(HEAD_COUNT, N_SEQ, SEQ_DEV, SEQ_DEV), block_v)
    nearby_accumulator = nearby_accumulator.reshape(HEAD_COUNT, SLIDE_LENGTH, HEAD_WIDTH)
    far_acc = jnp.einsum('hqk,hkd->hqd', far_weight, distant_values)
    safe_totals = jnp.where(occupied[None, :], totals, 1.0)
    context = jnp.where(occupied[None, :, None], (nearby_accumulator + far_acc) / safe_totals[..., None], 0.0)
    context = context.transpose(1, 0, 2).reshape(SLIDE_LENGTH, inner).astype(jnp.bfloat16)
    return jnp.dot(context, w_out, preferred_element_type=jnp.float32).astype(jnp.bfloat16)

def reference(tile_feats, tile_pos, slide_count, w_proj, emb_grad, ln_gain, w_qkv, w_out):
    emb_tiles = jnp.dot(tile_feats, w_proj, preferred_element_type=jnp.float32).astype(jnp.bfloat16)
    slot_index = jnp.arange(SLIDES * SLOTS, dtype=jnp.int32)
    slot_slide = slot_index % SLOTS // MOST
    flat_position = tile_pos.reshape(SLIDES * SLOTS).astype(jnp.int32)
    target = jnp.where(flat_position >= 0, slot_slide * SLIDE_LENGTH + flat_position, SLIDES * SLIDE_LENGTH).astype(jnp.int32)
    placed = jnp.zeros((SLIDES * SLIDE_LENGTH + 1, D), jnp.bfloat16).at[target].set(emb_tiles)
    slide_emb = placed[:SLIDES * SLIDE_LENGTH].reshape(SLIDES, SLIDE_LENGTH, D)

    def one_slide(bundle):
        return attend_slide(bundle[0], bundle[1], ln_gain, w_qkv, w_out)
    attn_branch = lax.map(one_slide, (slide_emb, slide_count))
    grad_rows = jnp.concatenate([emb_grad.reshape(SLIDES * SLIDE_LENGTH, D), jnp.zeros((1, D), jnp.bfloat16)], axis=0)
    slot_grad = grad_rows[target]
    proj_grad = lax.dot_general(tile_feats, slot_grad, (((0,), (0,)), ((), ())), preferred_element_type=jnp.float32)
    return (slide_emb, attn_branch, proj_grad)
```

```python
import functools

import jax
import jax.numpy as jnp
from jax import lax
from jax.experimental import pallas as pl
from jax.experimental.pallas import tpu as pltpu
from jax.sharding import PartitionSpec as P

D = 768
HEAD_COUNT = 12
HEAD_WIDTH = 64
DILATION_STEP = 4
NEGATIVE = -1e30
EPSILON = 1e-05
STEP_HEADS = 4

F32 = jnp.float32
BF16 = jnp.bfloat16
MESH = pl.DeviceIdType.MESH


def greet(dp_peers, seq_peers):
    barrier = pltpu.get_barrier_semaphore()
    dp_count, seq_count = lax.axis_size("dp"), lax.axis_size("seq")
    dp, seq = lax.axis_index("dp"), lax.axis_index("seq")
    if dp_peers:

        @pl.loop(1, dp_count)
        def _(t):
            pl.semaphore_signal(
                barrier, device_id=(lax.rem(dp + t, dp_count), seq), device_id_type=MESH
            )

    if seq_peers:

        @pl.loop(1, seq_count)
        def _(t):
            pl.semaphore_signal(
                barrier, device_id=(dp, lax.rem(seq + t, seq_count)), device_id_type=MESH
            )

    pl.semaphore_wait(
        barrier, (dp_count - 1 if dp_peers else 0) + (seq_count - 1 if seq_peers else 0)
    )


def remote(src, dst, send, recv, device):
    return pltpu.make_async_remote_copy(
        src_ref=src,
        dst_ref=dst,
        send_sem=send,
        recv_sem=recv,
        device_id=device,
        device_id_type=MESH,
    )


def dispatch_kernel(
    n, seq_count, pos, grad, emb, pos_out, emb_out, grad_out, grad_rows, picked, *sems
):
    ps, pr, xs, xr, es, er, gs, gr, fs, fr = sems
    dp, seq = lax.axis_index("dp"), lax.axis_index("seq")
    most = pos.shape[2]
    nearby, width = grad.shape[1:]
    greet(True, True)

    def column_copy(t):
        peer = lax.rem(seq + t, seq_count)
        return remote(grad.at[peer], grad_rows.at[seq], xs.at[t], xr.at[t], (dp, peer))

    def pos_copy(t):
        peer = lax.rem(dp + t, n)
        return remote(pos.at[peer], pos_out.at[dp], ps.at[t], pr.at[t], (peer, seq))

    def emb_copy(t):
        peer = lax.rem(dp + t, n)
        return remote(emb.at[peer], emb_out.at[seq, dp], es.at[t], er.at[t], (peer, seq))

    def grad_copy(t):
        peer = lax.rem(dp + t, n)
        return remote(picked.at[peer], grad_out.at[dp], gs.at[t], gr.at[t], (peer, seq))

    def forward(k, t):
        source = lax.rem(dp - t + n, n)
        peer = lax.rem(seq + k, seq_count)
        block = emb_out.at[seq, source]
        return remote(block, block, fs.at[k, t], fr.at[k, t], (dp, peer))

    @pl.loop(1, seq_count)
    def _(t):
        column_copy(t).start()

    @pl.loop(1, n)
    def _(t):
        pos_copy(t).start()

    @pl.loop(1, n)
    def _(t):
        emb_copy(t).start()

    pos_out[dp] = pos[dp]
    grad_rows[seq] = grad[seq]
    emb_out[seq, dp] = emb[dp]

    @pl.loop(1, n)
    def _(t):
        pos_copy(t).wait()

    @pl.loop(1, seq_count)
    def _(t):
        column_copy(t).wait()

    rows = jnp.concatenate([grad_rows[i] for i in range(seq_count)], axis=0)
    spot = lax.broadcasted_iota(jnp.int32, (nearby * seq_count, 1), 0)
    batch = 4
    for first in range(0, n, batch):
        at = jnp.concatenate([pos_out[first + i] for i in range(batch)], axis=1)
        hot = jnp.where(spot == at, 1.0, 0.0).astype(BF16)
        block = lax.dot_general(
            hot, rows, (((0,), (0,)), ((), ())), preferred_element_type=F32
        ).astype(BF16)
        for i in range(batch):
            picked[first + i] = block[i * most : (i + 1) * most]

    @pl.loop(1, n)
    def _(t):
        grad_copy(t).start()

    grad_out[dp] = picked[dp]
    for k in range(1, seq_count):
        forward(k, 0).start()

    @pl.loop(1, n)
    def _(t):
        emb_copy(t).wait_recv()
        for k in range(1, seq_count):
            forward(k, t).start()

    @pl.loop(1, n)
    def _(t):
        emb_copy(t).wait_send()
        grad_copy(t).wait()

    @pl.loop(0, n)
    def _(t):
        for k in range(1, seq_count):
            forward(k, t).wait()


def reduce_kernel(n, feats, slots, out, src, pair, cross, stage_b, stage_c, arrive, *sems):
    s1, r1, s2, r2, s3, r3, s4, r4, s5, r5, s6, r6 = sems
    dp, seq = lax.axis_index("dp"), lax.axis_index("seq")
    q = n // 4
    a, b, c = lax.rem(dp, 2), lax.rem(dp // 2, 2), dp // 4
    sibling = (dp + 1 - 2 * a, seq)
    across = (dp + 2 - 4 * b, seq)
    barrier = pltpu.get_barrier_semaphore()
    pl.semaphore_signal(barrier, device_id=sibling, device_id_type=MESH)
    pl.semaphore_signal(barrier, device_id=across, device_id_type=MESH)

    def ahead(t):
        return lax.rem(c + t, q)

    def behind(t):
        return lax.rem(c - t + q, q)

    def along(t):
        return (ahead(t) * 4 + b * 2 + a, seq)

    @pl.loop(1, q)
    def _(t):
        pl.semaphore_signal(barrier, device_id=along(t), device_id_type=MESH)

    rows = src.shape[3]
    tile = 512
    for first in range(0, n * rows, tile):
        product = lax.dot_general(
            feats[:, first : first + tile],
            slots[...],
            (((0,), (0,)), ((), ())),
            preferred_element_type=F32,
        ).astype(BF16)
        for i in range(tile // rows):
            k = first // rows + i
            src[k // (2 * q), k // q % 2, k % q] = product[i * rows : (i + 1) * rows]

    pl.semaphore_wait(barrier, q + 1)

    def side(i):
        return 1 - b if i == 0 else b

    def to_sibling(i, t):
        return remote(
            src.at[1 - a, side(i), ahead(t)], pair.at[i, t], s1.at[i, t], r1.at[i, t], sibling
        )

    def to_across(t):
        return remote(stage_b.at[t], cross.at[t], s2.at[t], r2.at[t], across)

    def to_owner(t):
        return remote(stage_c.at[t], arrive.at[t], s3.at[t], r3.at[t], along(t))

    def result_along(t):
        block = out.at[a, b, c]
        return remote(block, block, s4.at[t], r4.at[t], along(t))

    def result_across(t):
        block = out.at[a, b, behind(t)]
        return remote(block, block, s5.at[t], r5.at[t], across)

    def result_sibling(i, t):
        block = out.at[a, side(i), behind(t)]
        return remote(block, block, s6.at[i, t], r6.at[i, t], sibling)

    for i in (0, 1):

        @pl.loop(1, q + 1)
        def _(t):
            to_sibling(i, lax.rem(t, q)).start()

    @pl.loop(1, q + 1)
    def _(step):
        t = lax.rem(step, q)
        to_sibling(0, t).wait_recv()
        stage_b[t] = (src[a, 1 - b, ahead(t)].astype(F32) + pair[0, t].astype(F32)).astype(BF16)
        to_across(t).start()

    @pl.loop(1, q + 1)
    def _(step):
        t = lax.rem(step, q)
        to_sibling(1, t).wait_recv()
        to_across(t).wait_recv()
        stage_c[t] = (
            src[a, b, ahead(t)].astype(F32) + pair[1, t].astype(F32) + cross[t].astype(F32)
        ).astype(BF16)

        @pl.when(step < q)
        def _():
            to_owner(t).start()

    total = stage_c[0].astype(F32)
    for t in range(1, q):
        to_owner(t).wait_recv()
        total = total + arrive[t].astype(F32)
    out[a, b, c] = total.astype(BF16)

    @pl.loop(1, q)
    def _(t):
        result_along(t).start()

    result_across(0).start()
    result_sibling(1, 0).start()

    @pl.loop(1, q)
    def _(t):
        result_along(t).wait_recv()
        result_across(t).start()
        result_sibling(1, t).start()

    @pl.loop(0, q)
    def _(t):
        result_across(t).wait_recv()
        result_sibling(0, t).start()

    @pl.loop(1, q)
    def _(t):
        to_owner(t).wait_send()
        result_along(t).wait_send()

    for i in (0, 1):

        @pl.loop(0, q)
        def _(t):
            to_sibling(i, t).wait_send()
            result_sibling(i, t).wait()

    @pl.loop(0, q)
    def _(t):
        to_across(t).wait_send()
        result_across(t).wait_send()


VM = pl.BlockSpec(memory_space=pltpu.VMEM)
DMA = pltpu.SemaphoreType.DMA


def exchange(kernel, ident, outs, scratch, *operands):
    return pl.pallas_call(
        kernel,
        out_shape=tuple(jax.ShapeDtypeStruct(shape, kind) for shape, kind in outs),
        in_specs=[VM] * len(operands),
        out_specs=tuple([VM] * len(outs)),
        scratch_shapes=scratch,
        compiler_params=pltpu.CompilerParams(
            collective_id=ident, has_side_effects=True, vmem_limit_bytes=32 * 1024 * 1024
        ),
        cost_estimate=pl.CostEstimate(
            flops=10_000_000_000, bytes_accessed=10_000_000, transcendentals=0
        ),
    )(*operands)


def put_rows(whole, rows, low, high):
    pieces = [whole[:low]] if low else []
    pieces.append(rows)
    if high < whole.shape[0]:
        pieces.append(whole[high:])
    return jnp.concatenate(pieces, axis=0)


def attention_kernel(
    seq_count,
    nearby,
    meta_ref,
    rows_ref,
    gain_ref,
    wq_ref,
    wk_ref,
    wv_ref,
    wo_ref,
    emb_ref,
    branch_ref,
    normed,
    context,
):
    step = pl.program_id(0)
    me = meta_ref[0]
    count = meta_ref[1]
    part = nearby // DILATION_STEP
    own = pl.multiple_of(me * nearby, nearby)

    @pl.when(step == 0)
    def _():
        for block in range(seq_count):
            at = slice(block * nearby, (block + 1) * nearby)
            wide = jnp.concatenate(
                [rows_ref[c, at, :] for c in range(seq_count)], axis=-1
            ).astype(F32)
            center = jnp.mean(wide, axis=-1, keepdims=True)
            spread = jnp.mean(jnp.square(wide - center), axis=-1, keepdims=True)
            normed[at, :] = (
                (wide - center) * lax.rsqrt(spread + EPSILON) * gain_ref[...]
            ).astype(BF16)

    mine = normed[pl.ds(own, nearby), :]
    query = jnp.dot(mine, wq_ref[...], preferred_element_type=F32).astype(BF16)
    query = query * BF16(HEAD_WIDTH**-0.5)
    key = jnp.dot(mine, wk_ref[...], preferred_element_type=F32).astype(BF16)
    value = jnp.dot(mine, wv_ref[...], preferred_element_type=F32).astype(BF16)
    far_keys, far_values = [], []
    for other in range(1, seq_count):
        block = lax.rem(me + other, seq_count)
        start = pl.multiple_of(block * nearby, nearby)
        theirs = normed[pl.ds(start, nearby), :]
        far_keys.append(jnp.dot(theirs, wk_ref[...], preferred_element_type=F32).astype(BF16))
        far_values.append(jnp.dot(theirs, wv_ref[...], preferred_element_type=F32).astype(BF16))

    lane = lax.broadcasted_iota(jnp.int32, (1, nearby), 1)
    key_ok = own + (lane % part) * DILATION_STEP + lane // part < count
    row = lax.broadcasted_iota(jnp.int32, (nearby, 1), 0)
    query_ok = own + (row % part) * DILATION_STEP + row // part < count
    far_lane = lax.broadcasted_iota(jnp.int32, (1, part * (seq_count - 1)), 1)
    far_block = lax.rem(me + 1 + far_lane // part, seq_count)
    far_spot = far_block * nearby + far_lane % part * DILATION_STEP
    dims = (((1,), (1,)), ((), ()))
    outs = []
    for head in range(STEP_HEADS):
        shift = head % DILATION_STEP
        cols = slice(head * HEAD_WIDTH, (head + 1) * HEAD_WIDTH)
        low, high = shift * part, (shift + 1) * part
        q, k, v = query[:, cols], key[:, cols], value[:, cols]
        scores = lax.dot_general(q, k, dims, preferred_element_type=F32)
        scores = jnp.where(key_ok, scores, NEGATIVE)
        maximum = jnp.max(scores, axis=-1, keepdims=True)
        far_k = jnp.concatenate([x[low:high, cols] for x in far_keys], axis=0)
        far_v = jnp.concatenate([x[low:high, cols] for x in far_values], axis=0)
        far_ok = far_spot + shift < count
        far = lax.dot_general(q[low:high], far_k, dims, preferred_element_type=F32)
        far = jnp.where(far_ok, far, NEGATIVE)
        far_max = jnp.maximum(maximum[low:high], jnp.max(far, axis=-1, keepdims=True))
        maximum = put_rows(maximum, far_max, low, high)
        weight = jnp.exp(scores - maximum)
        in_lane = (lane >= low) & (lane < high)
        twice = jnp.where(in_lane, weight[low:high] * 2.0, weight[low:high])
        weight = put_rows(weight, twice, low, high)
        far_weight = jnp.exp(far - far_max)
        total = jnp.sum(weight, axis=-1, keepdims=True)
        far_total = jnp.sum(far_weight, axis=-1, keepdims=True)
        total = put_rows(total, total[low:high] + far_total, low, high)
        gathered = jnp.dot(weight.astype(BF16), v, preferred_element_type=F32)
        far_gathered = jnp.dot(far_weight.astype(BF16), far_v, preferred_element_type=F32)
        gathered = put_rows(gathered, gathered[low:high] + far_gathered, low, high)
        outs.append(jnp.where(query_ok, gathered / total, 0.0).astype(BF16))
    context[step] = jnp.concatenate(outs, axis=-1)

    @pl.when(step == pl.num_programs(0) - 1)
    def _():
        at_row = lax.broadcasted_iota(jnp.int32, (nearby, nearby), 0)
        at_lane = lax.broadcasted_iota(jnp.int32, (nearby, nearby), 1)
        natural = (at_lane % part) * DILATION_STEP + at_lane // part
        back = jnp.where(at_row == natural, 1.0, 0.0).astype(BF16)
        ordered = jnp.concatenate(
            [rows_ref[c, pl.ds(own, nearby), :] for c in range(seq_count)], axis=-1
        )
        emb_ref[...] = jnp.dot(back, ordered, preferred_element_type=F32).astype(BF16)
        whole = jnp.concatenate(
            [context[i] for i in range(HEAD_COUNT // STEP_HEADS)], axis=-1
        )
        whole = jnp.dot(back, whole, preferred_element_type=F32).astype(BF16)
        branch_ref[...] = jnp.dot(whole, wo_ref[...], preferred_element_type=F32).astype(BF16)


def attend(meta, rows, gain, weights, seq_count, nearby):
    width = STEP_HEADS * HEAD_WIDTH
    steps = HEAD_COUNT // STEP_HEADS
    slide_len = rows.shape[1]
    full = lambda *shape: pl.BlockSpec(shape, lambda i: (0,) * len(shape))
    out = jax.ShapeDtypeStruct((nearby, D), BF16)
    return pl.pallas_call(
        functools.partial(attention_kernel, seq_count, nearby),
        out_shape=(out, out),
        grid=(steps,),
        in_specs=[
            pl.BlockSpec(memory_space=pltpu.SMEM),
            full(*rows.shape),
            full(1, D),
            pl.BlockSpec((D, width), lambda i: (0, i)),
            pl.BlockSpec((D, width), lambda i: (0, steps + i)),
            pl.BlockSpec((D, width), lambda i: (0, 2 * steps + i)),
            pl.BlockSpec((D, D), lambda i: (0, 3)),
        ],
        out_specs=(full(nearby, D), full(nearby, D)),
        scratch_shapes=[
            pltpu.VMEM((slide_len, D), BF16),
            pltpu.VMEM((steps, nearby, width), BF16),
        ],
        compiler_params=pltpu.CompilerParams(vmem_limit_bytes=60 * 1024 * 1024),
        cost_estimate=pl.CostEstimate(
            flops=20_000_000_000, bytes_accessed=20_000_000, transcendentals=1_000_000
        ),
    )(meta, rows, gain, weights, weights, weights, weights)


def local(tile_feats, tile_pos, slide_count, w_proj, emb_grad, ln_gain, w_qkv, w_out):
    seq_count = lax.axis_size("seq")
    n = lax.axis_size("dp")
    seq_index = lax.axis_index("seq")
    slot_rows = tile_feats.shape[0]
    nearby = emb_grad.shape[1]
    slide_len = nearby * seq_count
    part = nearby // DILATION_STEP
    most = slot_rows // n
    width = w_proj.shape[1]
    weights = lax.all_gather(
        jnp.concatenate([w_qkv, w_out], axis=1), "dp", axis=0, tiled=True
    )
    emb_part = jnp.dot(tile_feats, w_proj, preferred_element_type=F32).astype(BF16)
    positions, arrived, slot_grad = exchange(
        functools.partial(dispatch_kernel, n, seq_count),
        1,
        [
            ((n, 1, most), jnp.int32),
            ((seq_count, n, most, width), BF16),
            ((n, most, width), BF16),
        ],
        [pltpu.VMEM((seq_count, nearby, width), BF16), pltpu.VMEM((n, most, width), BF16)]
        + [DMA((n,))] * 2
        + [DMA((seq_count,))] * 2
        + [DMA((n,))] * 4
        + [DMA((seq_count, n))] * 2,
        tile_pos.reshape(n, 1, most),
        emb_grad.reshape(nearby, seq_count, width).transpose(1, 0, 2),
        emb_part.reshape(n, most, width),
    )
    positions = positions.reshape(slot_rows)
    spot = jnp.arange(slide_len, dtype=jnp.int32)
    features = tile_feats.shape[1]
    quarter = n // 4
    shape = (2, 2, quarter, features // n, width)
    (summed,) = exchange(
        functools.partial(reduce_kernel, n),
        3,
        [(shape, BF16)],
        [pltpu.VMEM(shape, BF16), pltpu.VMEM(shape[1:], BF16)]
        + [pltpu.VMEM(shape[2:], BF16)] * 4
        + [DMA((2, quarter))] * 2
        + [DMA((quarter,))] * 8
        + [DMA((2, quarter))] * 2,
        tile_feats,
        slot_grad.reshape(slot_rows, width),
    )
    proj_grad = summed.reshape(features, width).astype(F32)

    inside = spot % nearby
    at_spot = spot - inside + (inside % part) * DILATION_STEP + inside // part
    hot_perm = (at_spot[:, None] == positions[None, :]).astype(BF16)
    rows = jnp.einsum(
        "ps,csw->cpw",
        hot_perm,
        arrived.reshape(seq_count, slot_rows, width),
        preferred_element_type=F32,
    ).astype(BF16)
    meta = jnp.stack([seq_index.astype(jnp.int32), slide_count[0]])
    local_emb, attn_branch = attend(
        meta, rows, ln_gain.reshape(1, D), weights, seq_count, nearby
    )
    return (local_emb[None], attn_branch[None], proj_grad)


ROUNDS = 2
ANY = pl.BlockSpec(memory_space=pl.ANY)
NT = (((1,), (1,)), ((), ()))
TN = (((0,), (0,)), ((), ()))


def split_first(count):
    size = count // ROUNDS
    return [pl.ds(r * size, size) for r in range(ROUNDS)]


def fused_kernel(
    n,
    feats_hbm,
    pos,
    slide_count,
    wproj_hbm,
    grad,
    gain,
    wqkv,
    wout,
    emb_ref,
    branch_ref,
    out,
    feats,
    wproj,
    emb,
    pos_in,
    pos_all,
    emb_all,
    grad_rows,
    picked,
    slots,
    wts,
    wts_x,
    normed,
    qkv,
    ctx_send,
    ctx_own,
    ctx_peer,
    src,
    pair,
    cross,
    stage_b,
    stage_c,
    arrive,
    local_sems,
    xs,
    xr,
    ps,
    pr,
    es,
    er,
    fs,
    fr,
    gs,
    gr,
    us,
    ur,
    ds_,
    dr,
    ys,
    yr,
    cs,
    cr,
    wxs,
    wxr,
    ks,
    kr,
    s1,
    r1,
    s2,
    r2,
    s3,
    r3,
    s4,
    r4,
    s5,
    r5,
    s6,
    r6,
):
    dp, seq = lax.axis_index("dp"), lax.axis_index("seq")
    q = n // 4
    a, b, c = lax.rem(dp, 2), lax.rem(dp // 2, 2), dp // 4
    x_peer = (dp, 1 - seq)
    sib_dp = dp + 1 - 2 * a
    y_dp = dp + 2 - 4 * b
    sibling, across = (sib_dp, seq), (y_dp, seq)
    most = pos_in.shape[2]
    slot_rows = feats.shape[0]
    nearby = grad.shape[1]
    width = wproj.shape[1]
    depth = wqkv.shape[0]
    part = nearby // DILATION_STEP
    inner = HEAD_COUNT * HEAD_WIDTH
    wide = 3 * width

    feats_copy = pltpu.make_async_copy(feats_hbm, feats, local_sems.at[0])
    wproj_copy = pltpu.make_async_copy(wproj_hbm, wproj, local_sems.at[1])
    wproj_copy.start()
    feats_copy.start()
    barrier = pltpu.get_barrier_semaphore()

    @pl.loop(1, n)
    def _(t):
        pl.semaphore_signal(barrier, device_id=(lax.rem(dp + t, n), seq), device_id_type=MESH)

    pl.semaphore_signal(barrier, device_id=x_peer, device_id_type=MESH)

    for i in range(n):
        pos_in[i] = pos[:, i * most : (i + 1) * most]
    mine_w = pl.ds(pl.multiple_of(dp * depth, 16), depth)
    half = pl.multiple_of(seq * width, width)
    for i in range(3):
        wts[mine_w, i * width : (i + 1) * width] = wqkv[
            :, pl.ds(pl.multiple_of(i * inner + half, 128), width)
        ]
    wts[mine_w, wide:] = wout[:, pl.ds(half, width)]
    pos_all[dp] = pos_in[dp]

    def column_copy():
        block = grad.at[0, :, pl.ds(pl.multiple_of((1 - seq) * width, 128), width)]
        return remote(block, grad_rows.at[seq], xs.at[0], xr.at[0], x_peer)

    own_columns = pltpu.make_async_copy(
        grad.at[0, :, pl.ds(half, width)], grad_rows.at[seq], local_sems.at[2]
    )
    own_columns.start()

    def pos_copy(t):
        peer = lax.rem(dp + t, n)
        return remote(pos_in.at[peer], pos_all.at[dp], ps.at[t], pr.at[t], (peer, seq))

    def emb_copy(t):
        peer = lax.rem(dp + t, n)
        return remote(
            emb.at[pl.ds(pl.multiple_of(peer * most, most), most)],
            emb_all.at[seq, dp],
            es.at[t],
            er.at[t],
            (peer, seq),
        )

    def forward(t):
        block = emb_all.at[seq, lax.rem(dp - t + n, n)]
        return remote(block, block, fs.at[t], fr.at[t], x_peer)

    def grad_send(peer):
        return remote(picked.at[peer], slots.at[dp], gs.at[peer], gr.at[dp], (peer, seq))

    def grad_recv(source):
        return remote(picked.at[source], slots.at[source], gs.at[source], gr.at[source], sibling)

    pl.semaphore_wait(barrier, n)
    column_copy().start()

    @pl.loop(1, n)
    def _(t):
        pos_copy(t).start()

    wproj_copy.wait()
    feats_copy.wait()
    emb[...] = jnp.dot(feats[...], wproj[...], preferred_element_type=F32).astype(BF16)

    @pl.loop(1, n)
    def _(t):
        emb_copy(t).start()

    emb_all[seq, dp] = emb[pl.ds(pl.multiple_of(dp * most, most), most), :]
    forward(0).start()

    @pl.loop(1, n)
    def _(t):
        pos_copy(t).wait()

    own_columns.wait()
    column_copy().wait()
    rows = jnp.concatenate([grad_rows[0], grad_rows[1]], axis=0)
    spot = lax.broadcasted_iota(jnp.int32, (2 * nearby, 1), 0)
    batch = 4

    @pl.loop(1, q + 1)
    def _(step):
        first = lax.rem(c + step, q) * batch
        at = jnp.concatenate([pos_all[first + i] for i in range(batch)], axis=1)
        hot = jnp.where(spot == at, 1.0, 0.0).astype(BF16)
        block = lax.dot_general(hot, rows, TN, preferred_element_type=F32).astype(BF16)
        for i in range(batch):
            picked[first + i] = block[i * most : (i + 1) * most]

            @pl.when(first + i != dp)
            def _():
                grad_send(first + i).start()

            @pl.when(first + i == dp)
            def _():
                slots[first + i] = block[i * most : (i + 1) * most]

    def rows_of(who):
        return pl.ds(pl.multiple_of(who * depth, 16), depth)

    def z_block(z):
        return wts.at[rows_of(z * 4 + b * 2 + a)]

    def up(hop, z):
        return remote(z_block(z), z_block(z), us.at[hop], ur.at[hop], (lax.rem(dp + 4, n), seq))

    def down(hop, z):
        return remote(z_block(z), z_block(z), ds_.at[hop], dr.at[hop], (lax.rem(dp + n - 4, n), seq))

    def y_copy(z, back=False):
        who = z * 4 + (1 - b if back else b) * 2 + a
        block = wts.at[rows_of(who)]
        return remote(block, block, ys.at[z], yr.at[z], across)

    def c_copy(side, z, back=False):
        y = b if side == 0 else 1 - b
        who = z * 4 + y * 2 + (1 - a if back else a)
        block = wts.at[rows_of(who)]
        return remote(block, block, cs.at[side, z], cr.at[side, z], sibling)

    def w_start():
        @pl.when(c < q - 1)
        def _():
            up(1, c).start()

        @pl.when(c > 0)
        def _():
            down(1, c).start()

        y_copy(c).start()
        c_copy(0, c).start()

    def w_hop(hop):
        below, above = c - hop, c + hop

        @pl.when(below >= 0)
        def _():
            up(hop, below).wait_recv()

            @pl.when(c < q - 1)
            def _():
                up(hop + 1, below).start()

            y_copy(below).start()
            c_copy(0, below).start()

        @pl.when(above < q)
        def _():
            down(hop, above).wait_recv()

            @pl.when(c > 0)
            def _():
                down(hop + 1, above).start()

            y_copy(above).start()
            c_copy(0, above).start()

    def w_side():
        @pl.loop(0, q)
        def _(t):
            z = lax.rem(c + t, q)
            y_copy(z, True).wait_recv()
            c_copy(1, z).start()

    def wx_copy():
        return remote(wts.at[:, pl.ds(wide, width)], wts_x, wxs.at[0], wxr.at[0], x_peer)

    def w_gathered():
        @pl.loop(0, q)
        def _(z):
            c_copy(0, z, True).wait_recv()
            c_copy(1, z, True).wait_recv()

        wx_copy().start()

    def w_done():
        for hop in range(1, q):

            @pl.when((c - hop + 1 >= 0) & (c < q - 1))
            def _():
                up(hop, c - hop + 1).wait_send()

            @pl.when((c + hop - 1 < q) & (c > 0))
            def _():
                down(hop, c + hop - 1).wait_send()

        @pl.loop(0, q)
        def _(z):
            y_copy(z).wait_send()
            c_copy(0, z).wait_send()
            c_copy(1, z).wait_send()

        wx_copy().wait_send()

    w_start()

    @pl.loop(1, n)
    def _(t):
        emb_copy(t).wait_recv()
        forward(t).start()

    w_hop(1)
    w_hop(2)

    count = slide_count[0]
    own = pl.multiple_of(seq * nearby, nearby)
    far_own = pl.multiple_of((1 - seq) * nearby, nearby)
    positions = jnp.concatenate([pos_all[i] for i in range(n)], axis=1)

    def natural_of(index, shift):
        return (index % part) * DILATION_STEP + lax.rem(index // part + 2 * shift, DILATION_STEP)

    inside = spot % nearby
    at_spot = spot - inside + natural_of(inside, seq)
    hot_perm = jnp.where(at_spot == positions, 1.0, 0.0).astype(BF16)
    own_spot = lax.broadcasted_iota(jnp.int32, (nearby, 1), 0) + seq * nearby
    hot_own = jnp.where(own_spot == positions, 1.0, 0.0).astype(BF16)

    @pl.loop(0, n)
    def _(t):
        forward(t).wait_recv()

    def regroup():
        blocks = [emb_all[i].reshape(slot_rows, width) for i in range(2)]
        for i in range(2):
            emb_ref[:, i * width : (i + 1) * width] = jnp.dot(
                hot_own, blocks[i], preferred_element_type=F32
            ).astype(BF16)
        for block in range(2):
            at = slice(block * nearby, (block + 1) * nearby)
            row = jnp.concatenate(
                [jnp.dot(hot_perm[at], blocks[i], preferred_element_type=F32) for i in range(2)],
                axis=-1,
            )
            center = jnp.mean(row, axis=-1, keepdims=True)
            spread = jnp.mean(jnp.square(row - center), axis=-1, keepdims=True)
            normed[at, :] = (
                (row - center) * lax.rsqrt(spread + EPSILON) * gain[...][None, :]
            ).astype(BF16)

    regroup()

    ranges = split_first(src.shape[3])

    def side(i):
        return 1 - b if i == 0 else b

    def ahead(t):
        return lax.rem(c + t, q)

    def behind(t):
        return lax.rem(c - t + q, q)

    def along(t):
        return (ahead(t) * 4 + b * 2 + a, seq)

    def to_sibling(r, i, t):
        at = ranges[r]
        return remote(
            src.at[1 - a, side(i), ahead(t), at],
            pair.at[i, t, at],
            s1.at[r, i, t],
            r1.at[r, i, t],
            sibling,
        )

    def to_across(r, t):
        at = ranges[r]
        return remote(stage_b.at[t, at], cross.at[t, at], s2.at[r, t], r2.at[r, t], across)

    def to_owner(r, t):
        at = ranges[r]
        return remote(stage_c.at[t, at], arrive.at[t, at], s3.at[r, t], r3.at[r, t], along(t))

    def result_along(r, t):
        block = out.at[a, b, c, ranges[r]]
        return remote(block, block, s4.at[r, t], r4.at[r, t], along(t))

    def result_across(r, t):
        block = out.at[a, b, behind(t), ranges[r]]
        return remote(block, block, s5.at[r, t], r5.at[r, t], across)

    def result_sibling(r, i, t):
        block = out.at[a, side(i), behind(t), ranges[r]]
        return remote(block, block, s6.at[r, i, t], r6.at[r, i, t], sibling)

    order = [t % q for t in range(1, q + 1)]

    @pl.loop(0, n)
    def _(source):
        @pl.when(source != dp)
        def _():
            grad_recv(source).wait_recv()

    rows_each = src.shape[3]
    grads = slots[...].reshape(slot_rows, width)
    tile = q * rows_each

    @pl.loop(0, n // q)
    def _(step):
        core = lax.rem(1 - a + step // 2, 2)
        y = lax.rem(1 - b + step, 2)
        first = pl.multiple_of((core * 2 + y) * tile, tile)
        product = lax.dot_general(
            feats[:, pl.ds(first, tile)], grads, TN, preferred_element_type=F32
        ).astype(BF16)
        for i in range(q):
            src[core, y, i] = product[i * rows_each : (i + 1) * rows_each]

        for i in range(2):

            @pl.when(step == i)
            def _():
                for r in range(ROUNDS):
                    for t in order:
                        to_sibling(r, i, t).start()

    def sum_b(r, t):
        to_sibling(r, 0, t).wait_recv()
        at = ranges[r]
        stage_b[t, at] = (
            src[a, 1 - b, ahead(t), at].astype(F32) + pair[0, t, at].astype(F32)
        ).astype(BF16)
        to_across(r, t).start()

    def sum_c(r, t):
        to_sibling(r, 1, t).wait_recv()
        to_across(r, t).wait_recv()
        at = ranges[r]
        stage_c[t, at] = (
            src[a, b, ahead(t), at].astype(F32)
            + pair[1, t, at].astype(F32)
            + cross[t, at].astype(F32)
        ).astype(BF16)
        if t:
            to_owner(r, t).start()

    def own_sum(r):
        at = ranges[r]
        total = stage_c[0, at].astype(F32)
        for t in range(1, q):
            to_owner(r, t).wait_recv()
            total = total + arrive[t, at].astype(F32)
        out[a, b, c, at] = total.astype(BF16)
        for t in range(1, q):
            result_along(r, t).start()
        result_across(r, 0).start()
        result_sibling(r, 1, 0).start()

    def result_on(r, t):
        result_along(r, t).wait_recv()
        result_across(r, t).start()
        result_sibling(r, 1, t).start()

    def result_over(r, t):
        result_across(r, t).wait_recv()
        result_sibling(r, 0, t).start()

    def reduce_done():
        for r in range(ROUNDS):

            @pl.loop(0, q)
            def _(t):
                for i in range(2):
                    to_sibling(r, i, t).wait_send()
                    result_sibling(r, i, t).wait()
                to_across(r, t).wait_send()
                result_across(r, t).wait_send()

            @pl.loop(1, q)
            def _(t):
                to_owner(r, t).wait_send()
                result_along(r, t).wait_send()

    lane = lax.broadcasted_iota(jnp.int32, (1, nearby), 1)
    row_at = lax.broadcasted_iota(jnp.int32, (nearby, 1), 0)
    far_lane = lax.broadcasted_iota(jnp.int32, (1, part), 1)

    def project(which):
        cols = slice(which * width, (which + 1) * width)
        value = jnp.dot(normed[...], wts[:, cols], preferred_element_type=F32).astype(BF16)
        if which == 0:
            value = value * BF16(HEAD_WIDTH**-0.5)
        qkv[which] = value

    def attend_head(start, other, head):
        group = head % DILATION_STEP
        cols = slice(head * HEAD_WIDTH, (head + 1) * HEAD_WIDTH)
        low, high = group * part, (group + 1) * part
        key_ok = start + natural_of(lane, seq) < count
        query_ok = start + natural_of(row_at, seq) < count
        far_ok = (
            other + far_lane * DILATION_STEP + lax.rem(group + 2 * seq, DILATION_STEP) < count
        )
        here = pl.ds(start, nearby)
        there = pl.ds(pl.multiple_of(other + low, part), part)
        qh, kh, vh = (qkv[i, here, :][:, cols] for i in range(3))
        far_k, far_v = (qkv[i, there, :][:, cols] for i in (1, 2))
        scores = lax.dot_general(qh, kh, NT, preferred_element_type=F32)
        scores = jnp.where(key_ok, scores, NEGATIVE)
        maximum = jnp.max(scores, axis=-1, keepdims=True)
        far = lax.dot_general(qh[low:high], far_k, NT, preferred_element_type=F32)
        far = jnp.where(far_ok, far, NEGATIVE)
        far_max = jnp.maximum(maximum[low:high], jnp.max(far, axis=-1, keepdims=True))
        maximum = put_rows(maximum, far_max, low, high)
        weight = jnp.exp(scores - maximum)
        in_lane = (lane >= low) & (lane < high)
        twice = jnp.where(in_lane, weight[low:high] * 2.0, weight[low:high])
        weight = put_rows(weight, twice, low, high)
        far_weight = jnp.exp(far - far_max)
        total = jnp.sum(weight, axis=-1, keepdims=True)
        far_total = jnp.sum(far_weight, axis=-1, keepdims=True)
        total = put_rows(total, total[low:high] + far_total, low, high)
        gathered = jnp.dot(weight.astype(BF16), vh, preferred_element_type=F32)
        far_gathered = jnp.dot(far_weight.astype(BF16), far_v, preferred_element_type=F32)
        gathered = put_rows(gathered, gathered[low:high] + far_gathered, low, high)
        return jnp.where(query_ok, gathered / total, 0.0).astype(BF16)

    def ctx_copy(j):
        at = pl.ds(j * 128, 128)
        return remote(ctx_send.at[:, at], ctx_peer.at[:, at], ks.at[j], kr.at[j], x_peer)

    pairs = width // 128

    def heads(mine, j):
        start, other = (own, far_own) if mine else (far_own, own)
        block = jnp.concatenate(
            [attend_head(start, other, 2 * j + i) for i in range(2)], axis=-1
        )
        at = pl.ds(j * 128, 128)
        if mine:
            ctx_own[:, at] = block
        else:
            ctx_send[:, at] = block
            ctx_copy(j).start()

    def finish_branch():
        for j in range(pairs):
            ctx_copy(j).wait()
        wx_copy().wait_recv()
        at_row = lax.broadcasted_iota(jnp.int32, (nearby, nearby), 0)
        at_lane = lax.broadcasted_iota(jnp.int32, (nearby, nearby), 1)
        ordered = []
        for shift, ref in ((seq, ctx_own), (1 - seq, ctx_peer)):
            back = jnp.where(at_row == natural_of(at_lane, shift), 1.0, 0.0).astype(BF16)
            ordered.append(jnp.dot(back, ref[...], preferred_element_type=F32).astype(BF16))
        for cols, weight in ((seq, wts.at[:, pl.ds(wide, width)]), (1 - seq, wts_x)):
            total = None
            for value, owner in zip(ordered, (seq, 1 - seq)):
                at = pl.ds(pl.multiple_of(owner * width, width), width)
                term = jnp.dot(value, weight[at, :], preferred_element_type=F32)
                total = term if total is None else total + term
            branch_ref[:, pl.ds(pl.multiple_of(cols * width, width), width)] = total.astype(BF16)

    reduce_steps = []
    for r in range(ROUNDS):
        reduce_steps += [functools.partial(sum_b, r, t) for t in order]
    for r in range(ROUNDS):
        reduce_steps += [functools.partial(sum_c, r, t) for t in order]
        reduce_steps += [functools.partial(own_sum, r)]
        if r:
            reduce_steps += [functools.partial(result_on, r - 1, t) for t in range(1, q)]
            reduce_steps += [functools.partial(result_over, r - 1, t) for t in range(q)]
    r = ROUNDS - 1
    reduce_steps += [functools.partial(result_on, r, t) for t in range(1, q)]
    reduce_steps += [functools.partial(result_over, r, t) for t in range(q)]

    work = [functools.partial(project, i) for i in range(3)]
    work += [functools.partial(heads, False, j) for j in range(pairs)]
    work += [functools.partial(heads, True, j) for j in range(pairs)]

    w_hop(3)
    split = 2 * q
    for step in reduce_steps[:q]:
        step()
    w_side()
    for step in reduce_steps[q:split]:
        step()
    w_gathered()
    rest = reduce_steps[split:]
    slots_left = len(work)
    taken = 0
    for i, job in enumerate(work):
        job()
        until = (i + 1) * len(rest) // (slots_left + 2)
        for step in rest[taken:until]:
            step()
        taken = until
    finish_branch()
    for step in rest[taken:]:
        step()

    @pl.loop(1, n)
    def _(t):
        emb_copy(t).wait_send()

    @pl.loop(0, n)
    def _(t):
        forward(t).wait_send()

        @pl.when(t != dp)
        def _():
            grad_send(t).wait_send()

    w_done()
    reduce_done()


def fused(tile_feats, tile_pos, slide_count, w_proj, emb_grad, ln_gain, w_qkv, w_out):
    n = lax.axis_size("dp")
    slot_rows, features = tile_feats.shape
    nearby = emb_grad.shape[1]
    most = slot_rows // n
    width = w_proj.shape[1]
    q = n // 4
    shape = (2, 2, q, features // n, width)
    rounds = (ROUNDS, q)
    smem = pl.BlockSpec(memory_space=pltpu.SMEM)
    scratch = [
        pltpu.VMEM(tile_feats.shape, BF16),
        pltpu.VMEM(w_proj.shape, BF16),
        pltpu.VMEM((slot_rows, width), BF16),
        pltpu.VMEM((n, 1, most), jnp.int32),
        pltpu.VMEM((n, 1, most), jnp.int32),
        pltpu.VMEM((2, n, most, width), BF16),
        pltpu.VMEM((2, nearby, width), BF16),
        pltpu.VMEM((n, most, width), BF16),
        pltpu.VMEM((n, most, width), BF16),
        pltpu.VMEM((D, 4 * width), BF16),
        pltpu.VMEM((D, width), BF16),
        pltpu.VMEM((2 * nearby, D), BF16),
        pltpu.VMEM((3, 2 * nearby, width), BF16),
        pltpu.VMEM((nearby, width), BF16),
        pltpu.VMEM((nearby, width), BF16),
        pltpu.VMEM((nearby, width), BF16),
        pltpu.VMEM(shape, BF16),
        pltpu.VMEM(shape[1:], BF16),
        pltpu.VMEM(shape[2:], BF16),
        pltpu.VMEM(shape[2:], BF16),
        pltpu.VMEM(shape[2:], BF16),
        pltpu.VMEM(shape[2:], BF16),
        DMA((3,)),
    ]
    scratch += [DMA((1,))] * 2
    scratch += [DMA((n,))] * 8
    scratch += [DMA((q + 1,))] * 4
    scratch += [DMA((q,))] * 2
    scratch += [DMA((2, q))] * 2
    scratch += [DMA((1,))] * 2
    scratch += [DMA((width // 128,))] * 2
    scratch += [DMA((ROUNDS, 2, q))] * 2
    scratch += [DMA(rounds)] * 8
    scratch += [DMA((ROUNDS, 2, q))] * 2
    row = jax.ShapeDtypeStruct((nearby, D), BF16)
    emb, branch, summed = pl.pallas_call(
        functools.partial(fused_kernel, n),
        out_shape=(row, row, jax.ShapeDtypeStruct(shape, BF16)),
        in_specs=[ANY, VM, smem, ANY, ANY, VM, VM, VM],
        out_specs=(VM, VM, VM),
        scratch_shapes=scratch,
        compiler_params=pltpu.CompilerParams(
            collective_id=5, has_side_effects=True, vmem_limit_bytes=48 * 1024 * 1024
        ),
        cost_estimate=pl.CostEstimate(
            flops=5_000_000_000, bytes_accessed=10_000_000, transcendentals=1_000_000
        ),
    )(tile_feats, tile_pos, slide_count, w_proj, emb_grad, ln_gain, w_qkv, w_out)
    return (emb[None], branch[None], summed.reshape(features, width).astype(F32))


def solution(mesh):
    in_specs = (
        P("dp", None),
        P("dp", None),
        P("dp"),
        P(None, "seq"),
        P("dp", "seq", None),
        P(),
        P("dp", None),
        P("dp", None),
    )
    out_specs = (P("dp", "seq", None), P("dp", "seq", None), P(None, "seq"))
    one_kernel = mesh.shape["dp"] == 16 and mesh.shape["seq"] == 2
    body = fused if one_kernel else local
    return jax.shard_map(body, mesh=mesh, in_specs=in_specs, out_specs=out_specs, check_vma=False)
```

```python
import functools

import jax
import jax.numpy as jnp
from jax import lax
from jax.experimental import pallas as pl
from jax.experimental.pallas import tpu as pltpu
from jax.sharding import PartitionSpec as P

D = 768
HEAD_COUNT = 12
HEAD_WIDTH = 64
DILATION_STEP = 4
NEGATIVE = -1e30
EPSILON = 1e-05
STEP_HEADS = 4

F32 = jnp.float32
BF16 = jnp.bfloat16
MESH = pl.DeviceIdType.MESH


def greet(dp_peers, seq_peers):
    barrier = pltpu.get_barrier_semaphore()
    dp_count, seq_count = lax.axis_size("dp"), lax.axis_size("seq")
    dp, seq = lax.axis_index("dp"), lax.axis_index("seq")
    if dp_peers:

        @pl.loop(1, dp_count)
        def _(t):
            pl.semaphore_signal(
                barrier, device_id=(lax.rem(dp + t, dp_count), seq), device_id_type=MESH
            )

    if seq_peers:

        @pl.loop(1, seq_count)
        def _(t):
            pl.semaphore_signal(
                barrier, device_id=(dp, lax.rem(seq + t, seq_count)), device_id_type=MESH
            )

    pl.semaphore_wait(
        barrier, (dp_count - 1 if dp_peers else 0) + (seq_count - 1 if seq_peers else 0)
    )


def remote(src, dst, send, recv, device):
    return pltpu.make_async_remote_copy(
        src_ref=src,
        dst_ref=dst,
        send_sem=send,
        recv_sem=recv,
        device_id=device,
        device_id_type=MESH,
    )


def dispatch_kernel(
    n, seq_count, pos, grad, emb, pos_out, emb_out, grad_out, grad_rows, picked, *sems
):
    ps, pr, xs, xr, es, er, gs, gr, fs, fr = sems
    dp, seq = lax.axis_index("dp"), lax.axis_index("seq")
    most = pos.shape[2]
    nearby, width = grad.shape[1:]
    greet(True, True)

    def column_copy(t):
        peer = lax.rem(seq + t, seq_count)
        return remote(grad.at[peer], grad_rows.at[seq], xs.at[t], xr.at[t], (dp, peer))

    def pos_copy(t):
        peer = lax.rem(dp + t, n)
        return remote(pos.at[peer], pos_out.at[dp], ps.at[t], pr.at[t], (peer, seq))

    def emb_copy(t):
        peer = lax.rem(dp + t, n)
        return remote(emb.at[peer], emb_out.at[seq, dp], es.at[t], er.at[t], (peer, seq))

    def grad_copy(t):
        peer = lax.rem(dp + t, n)
        return remote(picked.at[peer], grad_out.at[dp], gs.at[t], gr.at[t], (peer, seq))

    def forward(k, t):
        source = lax.rem(dp - t + n, n)
        peer = lax.rem(seq + k, seq_count)
        block = emb_out.at[seq, source]
        return remote(block, block, fs.at[k, t], fr.at[k, t], (dp, peer))

    @pl.loop(1, seq_count)
    def _(t):
        column_copy(t).start()

    @pl.loop(1, n)
    def _(t):
        pos_copy(t).start()

    @pl.loop(1, n)
    def _(t):
        emb_copy(t).start()

    pos_out[dp] = pos[dp]
    grad_rows[seq] = grad[seq]
    emb_out[seq, dp] = emb[dp]

    @pl.loop(1, n)
    def _(t):
        pos_copy(t).wait()

    @pl.loop(1, seq_count)
    def _(t):
        column_copy(t).wait()

    rows = jnp.concatenate([grad_rows[i] for i in range(seq_count)], axis=0)
    spot = lax.broadcasted_iota(jnp.int32, (nearby * seq_count, 1), 0)
    batch = 4
    for first in range(0, n, batch):
        at = jnp.concatenate([pos_out[first + i] for i in range(batch)], axis=1)
        hot = jnp.where(spot == at, 1.0, 0.0).astype(BF16)
        block = lax.dot_general(
            hot, rows, (((0,), (0,)), ((), ())), preferred_element_type=F32
        ).astype(BF16)
        for i in range(batch):
            picked[first + i] = block[i * most : (i + 1) * most]

    @pl.loop(1, n)
    def _(t):
        grad_copy(t).start()

    grad_out[dp] = picked[dp]
    for k in range(1, seq_count):
        forward(k, 0).start()

    @pl.loop(1, n)
    def _(t):
        emb_copy(t).wait_recv()
        for k in range(1, seq_count):
            forward(k, t).start()

    @pl.loop(1, n)
    def _(t):
        emb_copy(t).wait_send()
        grad_copy(t).wait()

    @pl.loop(0, n)
    def _(t):
        for k in range(1, seq_count):
            forward(k, t).wait()


def reduce_kernel(n, feats, slots, out, src, pair, cross, stage_b, stage_c, arrive, *sems):
    s1, r1, s2, r2, s3, r3, s4, r4, s5, r5, s6, r6 = sems
    dp, seq = lax.axis_index("dp"), lax.axis_index("seq")
    q = n // 4
    a, b, c = lax.rem(dp, 2), lax.rem(dp // 2, 2), dp // 4
    sibling = (dp + 1 - 2 * a, seq)
    across = (dp + 2 - 4 * b, seq)
    barrier = pltpu.get_barrier_semaphore()
    pl.semaphore_signal(barrier, device_id=sibling, device_id_type=MESH)
    pl.semaphore_signal(barrier, device_id=across, device_id_type=MESH)

    def ahead(t):
        return lax.rem(c + t, q)

    def behind(t):
        return lax.rem(c - t + q, q)

    def along(t):
        return (ahead(t) * 4 + b * 2 + a, seq)

    @pl.loop(1, q)
    def _(t):
        pl.semaphore_signal(barrier, device_id=along(t), device_id_type=MESH)

    rows = src.shape[3]
    tile = 512
    for first in range(0, n * rows, tile):
        product = lax.dot_general(
            feats[:, first : first + tile],
            slots[...],
            (((0,), (0,)), ((), ())),
            preferred_element_type=F32,
        ).astype(BF16)
        for i in range(tile // rows):
            k = first // rows + i
            src[k // (2 * q), k // q % 2, k % q] = product[i * rows : (i + 1) * rows]

    pl.semaphore_wait(barrier, q + 1)

    def side(i):
        return 1 - b if i == 0 else b

    def to_sibling(i, t):
        return remote(
            src.at[1 - a, side(i), ahead(t)], pair.at[i, t], s1.at[i, t], r1.at[i, t], sibling
        )

    def to_across(t):
        return remote(stage_b.at[t], cross.at[t], s2.at[t], r2.at[t], across)

    def to_owner(t):
        return remote(stage_c.at[t], arrive.at[t], s3.at[t], r3.at[t], along(t))

    def result_along(t):
        block = out.at[a, b, c]
        return remote(block, block, s4.at[t], r4.at[t], along(t))

    def result_across(t):
        block = out.at[a, b, behind(t)]
        return remote(block, block, s5.at[t], r5.at[t], across)

    def result_sibling(i, t):
        block = out.at[a, side(i), behind(t)]
        return remote(block, block, s6.at[i, t], r6.at[i, t], sibling)

    for i in (0, 1):

        @pl.loop(1, q + 1)
        def _(t):
            to_sibling(i, lax.rem(t, q)).start()

    @pl.loop(1, q + 1)
    def _(step):
        t = lax.rem(step, q)
        to_sibling(0, t).wait_recv()
        stage_b[t] = (src[a, 1 - b, ahead(t)].astype(F32) + pair[0, t].astype(F32)).astype(BF16)
        to_across(t).start()

    @pl.loop(1, q + 1)
    def _(step):
        t = lax.rem(step, q)
        to_sibling(1, t).wait_recv()
        to_across(t).wait_recv()
        stage_c[t] = (
            src[a, b, ahead(t)].astype(F32) + pair[1, t].astype(F32) + cross[t].astype(F32)
        ).astype(BF16)

        @pl.when(step < q)
        def _():
            to_owner(t).start()

    total = stage_c[0].astype(F32)
    for t in range(1, q):
        to_owner(t).wait_recv()
        total = total + arrive[t].astype(F32)
    out[a, b, c] = total.astype(BF16)

    @pl.loop(1, q)
    def _(t):
        result_along(t).start()

    result_across(0).start()
    result_sibling(1, 0).start()

    @pl.loop(1, q)
    def _(t):
        result_along(t).wait_recv()
        result_across(t).start()
        result_sibling(1, t).start()

    @pl.loop(0, q)
    def _(t):
        result_across(t).wait_recv()
        result_sibling(0, t).start()

    @pl.loop(1, q)
    def _(t):
        to_owner(t).wait_send()
        result_along(t).wait_send()

    for i in (0, 1):

        @pl.loop(0, q)
        def _(t):
            to_sibling(i, t).wait_send()
            result_sibling(i, t).wait()

    @pl.loop(0, q)
    def _(t):
        to_across(t).wait_send()
        result_across(t).wait_send()


VM = pl.BlockSpec(memory_space=pltpu.VMEM)
DMA = pltpu.SemaphoreType.DMA


def exchange(kernel, ident, outs, scratch, *operands):
    return pl.pallas_call(
        kernel,
        out_shape=tuple(jax.ShapeDtypeStruct(shape, kind) for shape, kind in outs),
        in_specs=[VM] * len(operands),
        out_specs=tuple([VM] * len(outs)),
        scratch_shapes=scratch,
        compiler_params=pltpu.CompilerParams(
            collective_id=ident, has_side_effects=True, vmem_limit_bytes=32 * 1024 * 1024
        ),
        cost_estimate=pl.CostEstimate(
            flops=10_000_000_000, bytes_accessed=10_000_000, transcendentals=0
        ),
    )(*operands)


def put_rows(whole, rows, low, high):
    pieces = [whole[:low]] if low else []
    pieces.append(rows)
    if high < whole.shape[0]:
        pieces.append(whole[high:])
    return jnp.concatenate(pieces, axis=0)


def attention_kernel(
    seq_count,
    nearby,
    meta_ref,
    rows_ref,
    gain_ref,
    wq_ref,
    wk_ref,
    wv_ref,
    wo_ref,
    emb_ref,
    branch_ref,
    normed,
    context,
):
    step = pl.program_id(0)
    me = meta_ref[0]
    count = meta_ref[1]
    part = nearby // DILATION_STEP
    own = pl.multiple_of(me * nearby, nearby)

    @pl.when(step == 0)
    def _():
        for block in range(seq_count):
            at = slice(block * nearby, (block + 1) * nearby)
            wide = jnp.concatenate(
                [rows_ref[c, at, :] for c in range(seq_count)], axis=-1
            ).astype(F32)
            center = jnp.mean(wide, axis=-1, keepdims=True)
            spread = jnp.mean(jnp.square(wide - center), axis=-1, keepdims=True)
            normed[at, :] = (
                (wide - center) * lax.rsqrt(spread + EPSILON) * gain_ref[...]
            ).astype(BF16)

    mine = normed[pl.ds(own, nearby), :]
    query = jnp.dot(mine, wq_ref[...], preferred_element_type=F32).astype(BF16)
    query = query * BF16(HEAD_WIDTH**-0.5)
    key = jnp.dot(mine, wk_ref[...], preferred_element_type=F32).astype(BF16)
    value = jnp.dot(mine, wv_ref[...], preferred_element_type=F32).astype(BF16)
    far_keys, far_values = [], []
    for other in range(1, seq_count):
        block = lax.rem(me + other, seq_count)
        start = pl.multiple_of(block * nearby, nearby)
        theirs = normed[pl.ds(start, nearby), :]
        far_keys.append(jnp.dot(theirs, wk_ref[...], preferred_element_type=F32).astype(BF16))
        far_values.append(jnp.dot(theirs, wv_ref[...], preferred_element_type=F32).astype(BF16))

    lane = lax.broadcasted_iota(jnp.int32, (1, nearby), 1)
    key_ok = own + (lane % part) * DILATION_STEP + lane // part < count
    row = lax.broadcasted_iota(jnp.int32, (nearby, 1), 0)
    query_ok = own + (row % part) * DILATION_STEP + row // part < count
    far_lane = lax.broadcasted_iota(jnp.int32, (1, part * (seq_count - 1)), 1)
    far_block = lax.rem(me + 1 + far_lane // part, seq_count)
    far_spot = far_block * nearby + far_lane % part * DILATION_STEP
    dims = (((1,), (1,)), ((), ()))
    outs = []
    for head in range(STEP_HEADS):
        shift = head % DILATION_STEP
        cols = slice(head * HEAD_WIDTH, (head + 1) * HEAD_WIDTH)
        low, high = shift * part, (shift + 1) * part
        q, k, v = query[:, cols], key[:, cols], value[:, cols]
        scores = lax.dot_general(q, k, dims, preferred_element_type=F32)
        scores = jnp.where(key_ok, scores, NEGATIVE)
        maximum = jnp.max(scores, axis=-1, keepdims=True)
        far_k = jnp.concatenate([x[low:high, cols] for x in far_keys], axis=0)
        far_v = jnp.concatenate([x[low:high, cols] for x in far_values], axis=0)
        far_ok = far_spot + shift < count
        far = lax.dot_general(q[low:high], far_k, dims, preferred_element_type=F32)
        far = jnp.where(far_ok, far, NEGATIVE)
        far_max = jnp.maximum(maximum[low:high], jnp.max(far, axis=-1, keepdims=True))
        maximum = put_rows(maximum, far_max, low, high)
        weight = jnp.exp(scores - maximum)
        in_lane = (lane >= low) & (lane < high)
        twice = jnp.where(in_lane, weight[low:high] * 2.0, weight[low:high])
        weight = put_rows(weight, twice, low, high)
        far_weight = jnp.exp(far - far_max)
        total = jnp.sum(weight, axis=-1, keepdims=True)
        far_total = jnp.sum(far_weight, axis=-1, keepdims=True)
        total = put_rows(total, total[low:high] + far_total, low, high)
        gathered = jnp.dot(weight.astype(BF16), v, preferred_element_type=F32)
        far_gathered = jnp.dot(far_weight.astype(BF16), far_v, preferred_element_type=F32)
        gathered = put_rows(gathered, gathered[low:high] + far_gathered, low, high)
        outs.append(jnp.where(query_ok, gathered / total, 0.0).astype(BF16))
    context[step] = jnp.concatenate(outs, axis=-1)

    @pl.when(step == pl.num_programs(0) - 1)
    def _():
        at_row = lax.broadcasted_iota(jnp.int32, (nearby, nearby), 0)
        at_lane = lax.broadcasted_iota(jnp.int32, (nearby, nearby), 1)
        natural = (at_lane % part) * DILATION_STEP + at_lane // part
        back = jnp.where(at_row == natural, 1.0, 0.0).astype(BF16)
        ordered = jnp.concatenate(
            [rows_ref[c, pl.ds(own, nearby), :] for c in range(seq_count)], axis=-1
        )
        emb_ref[...] = jnp.dot(back, ordered, preferred_element_type=F32).astype(BF16)
        whole = jnp.concatenate(
            [context[i] for i in range(HEAD_COUNT // STEP_HEADS)], axis=-1
        )
        whole = jnp.dot(back, whole, preferred_element_type=F32).astype(BF16)
        branch_ref[...] = jnp.dot(whole, wo_ref[...], preferred_element_type=F32).astype(BF16)


def attend(meta, rows, gain, weights, seq_count, nearby):
    width = STEP_HEADS * HEAD_WIDTH
    steps = HEAD_COUNT // STEP_HEADS
    slide_len = rows.shape[1]
    full = lambda *shape: pl.BlockSpec(shape, lambda i: (0,) * len(shape))
    out = jax.ShapeDtypeStruct((nearby, D), BF16)
    return pl.pallas_call(
        functools.partial(attention_kernel, seq_count, nearby),
        out_shape=(out, out),
        grid=(steps,),
        in_specs=[
            pl.BlockSpec(memory_space=pltpu.SMEM),
            full(*rows.shape),
            full(1, D),
            pl.BlockSpec((D, width), lambda i: (0, i)),
            pl.BlockSpec((D, width), lambda i: (0, steps + i)),
            pl.BlockSpec((D, width), lambda i: (0, 2 * steps + i)),
            pl.BlockSpec((D, D), lambda i: (0, 3)),
        ],
        out_specs=(full(nearby, D), full(nearby, D)),
        scratch_shapes=[
            pltpu.VMEM((slide_len, D), BF16),
            pltpu.VMEM((steps, nearby, width), BF16),
        ],
        compiler_params=pltpu.CompilerParams(vmem_limit_bytes=60 * 1024 * 1024),
        cost_estimate=pl.CostEstimate(
            flops=20_000_000_000, bytes_accessed=20_000_000, transcendentals=1_000_000
        ),
    )(meta, rows, gain, weights, weights, weights, weights)


def local(tile_feats, tile_pos, slide_count, w_proj, emb_grad, ln_gain, w_qkv, w_out):
    seq_count = lax.axis_size("seq")
    n = lax.axis_size("dp")
    seq_index = lax.axis_index("seq")
    slot_rows = tile_feats.shape[0]
    nearby = emb_grad.shape[1]
    slide_len = nearby * seq_count
    part = nearby // DILATION_STEP
    most = slot_rows // n
    width = w_proj.shape[1]
    weights = lax.all_gather(
        jnp.concatenate([w_qkv, w_out], axis=1), "dp", axis=0, tiled=True
    )
    emb_part = jnp.dot(tile_feats, w_proj, preferred_element_type=F32).astype(BF16)
    positions, arrived, slot_grad = exchange(
        functools.partial(dispatch_kernel, n, seq_count),
        1,
        [
            ((n, 1, most), jnp.int32),
            ((seq_count, n, most, width), BF16),
            ((n, most, width), BF16),
        ],
        [pltpu.VMEM((seq_count, nearby, width), BF16), pltpu.VMEM((n, most, width), BF16)]
        + [DMA((n,))] * 2
        + [DMA((seq_count,))] * 2
        + [DMA((n,))] * 4
        + [DMA((seq_count, n))] * 2,
        tile_pos.reshape(n, 1, most),
        emb_grad.reshape(nearby, seq_count, width).transpose(1, 0, 2),
        emb_part.reshape(n, most, width),
    )
    positions = positions.reshape(slot_rows)
    spot = jnp.arange(slide_len, dtype=jnp.int32)
    features = tile_feats.shape[1]
    quarter = n // 4
    shape = (2, 2, quarter, features // n, width)
    (summed,) = exchange(
        functools.partial(reduce_kernel, n),
        3,
        [(shape, BF16)],
        [pltpu.VMEM(shape, BF16), pltpu.VMEM(shape[1:], BF16)]
        + [pltpu.VMEM(shape[2:], BF16)] * 4
        + [DMA((2, quarter))] * 2
        + [DMA((quarter,))] * 8
        + [DMA((2, quarter))] * 2,
        tile_feats,
        slot_grad.reshape(slot_rows, width),
    )
    proj_grad = summed.reshape(features, width).astype(F32)

    inside = spot % nearby
    at_spot = spot - inside + (inside % part) * DILATION_STEP + inside // part
    hot_perm = (at_spot[:, None] == positions[None, :]).astype(BF16)
    rows = jnp.einsum(
        "ps,csw->cpw",
        hot_perm,
        arrived.reshape(seq_count, slot_rows, width),
        preferred_element_type=F32,
    ).astype(BF16)
    meta = jnp.stack([seq_index.astype(jnp.int32), slide_count[0]])
    local_emb, attn_branch = attend(
        meta, rows, ln_gain.reshape(1, D), weights, seq_count, nearby
    )
    return (local_emb[None], attn_branch[None], proj_grad)


ROUNDS = 2
HBM = pl.BlockSpec(memory_space=pltpu.HBM)
NT = (((1,), (1,)), ((), ()))
TN = (((0,), (0,)), ((), ()))


def split_first(count):
    size = count // ROUNDS
    return [pl.ds(r * size, size) for r in range(ROUNDS)]


def fused_kernel(
    n,
    feats_hbm,
    pos_hbm,
    slide_count,
    wproj_hbm,
    grad,
    gain_hbm,
    wqkv_hbm,
    wout_hbm,
    emb_ref,
    branch_ref,
    out,
    feats,
    wproj,
    pos,
    gain,
    wqkv,
    wout,
    emb,
    pos_in,
    pos_all,
    emb_all,
    grad_rows,
    picked,
    slots,
    wts,
    wts_x,
    normed,
    qkv,
    ctx_send,
    ctx_own,
    ctx_peer,
    src,
    pair,
    cross,
    stage_b,
    stage_c,
    arrive,
    local_sems,
    xs,
    xr,
    ps,
    pr,
    es,
    er,
    fs,
    fr,
    gs,
    gr,
    us,
    ur,
    ds_,
    dr,
    ys,
    yr,
    cs,
    cr,
    wxs,
    wxr,
    ks,
    kr,
    s1,
    r1,
    s2,
    r2,
    s3,
    r3,
    s4,
    r4,
    s5,
    r5,
    s6,
    r6,
):
    dp, seq = lax.axis_index("dp"), lax.axis_index("seq")
    q = n // 4
    a, b, c = lax.rem(dp, 2), lax.rem(dp // 2, 2), dp // 4
    x_peer = (dp, 1 - seq)
    sib_dp = dp + 1 - 2 * a
    y_dp = dp + 2 - 4 * b
    sibling, across = (sib_dp, seq), (y_dp, seq)
    most = pos_in.shape[2]
    slot_rows = feats.shape[0]
    nearby = grad.shape[1]
    width = wproj.shape[1]
    depth = wqkv.shape[0]
    part = nearby // DILATION_STEP
    inner = HEAD_COUNT * HEAD_WIDTH
    wide = 3 * width

    feats_copy = pltpu.make_async_copy(feats_hbm, feats, local_sems.at[0])
    wproj_copy = pltpu.make_async_copy(wproj_hbm, wproj, local_sems.at[1])
    pos_load = pltpu.make_async_copy(pos_hbm, pos, local_sems.at[3])
    gain_load = pltpu.make_async_copy(gain_hbm, gain, local_sems.at[4])
    wqkv_load = pltpu.make_async_copy(wqkv_hbm, wqkv, local_sems.at[5])
    wout_load = pltpu.make_async_copy(wout_hbm, wout, local_sems.at[6])
    pos_load.start()
    wqkv_load.start()
    wout_load.start()
    gain_load.start()
    wproj_copy.start()
    feats_copy.start()
    barrier = pltpu.get_barrier_semaphore()

    @pl.loop(1, n)
    def _(t):
        pl.semaphore_signal(barrier, device_id=(lax.rem(dp + t, n), seq), device_id_type=MESH)

    pl.semaphore_signal(barrier, device_id=x_peer, device_id_type=MESH)

    pos_load.wait()
    for i in range(n):
        pos_in[i] = pos[:, i * most : (i + 1) * most]
    wqkv_load.wait()
    wout_load.wait()
    gain_load.wait()
    mine_w = pl.ds(pl.multiple_of(dp * depth, 16), depth)
    half = pl.multiple_of(seq * width, width)
    for i in range(3):
        wts[mine_w, i * width : (i + 1) * width] = wqkv[
            :, pl.ds(pl.multiple_of(i * inner + half, 128), width)
        ]
    wts[mine_w, wide:] = wout[:, pl.ds(half, width)]
    pos_all[dp] = pos_in[dp]

    def column_copy():
        block = grad.at[0, :, pl.ds(pl.multiple_of((1 - seq) * width, 128), width)]
        return remote(block, grad_rows.at[seq], xs.at[0], xr.at[0], x_peer)

    own_columns = pltpu.make_async_copy(
        grad.at[0, :, pl.ds(half, width)], grad_rows.at[seq], local_sems.at[2]
    )
    own_columns.start()

    def pos_copy(t):
        peer = lax.rem(dp + t, n)
        return remote(pos_in.at[peer], pos_all.at[dp], ps.at[t], pr.at[t], (peer, seq))

    def emb_copy(t):
        peer = lax.rem(dp + t, n)
        return remote(
            emb.at[pl.ds(pl.multiple_of(peer * most, most), most)],
            emb_all.at[seq, dp],
            es.at[t],
            er.at[t],
            (peer, seq),
        )

    def forward(t):
        block = emb_all.at[seq, lax.rem(dp - t + n, n)]
        return remote(block, block, fs.at[t], fr.at[t], x_peer)

    def grad_send(peer):
        return remote(picked.at[peer], slots.at[dp], gs.at[peer], gr.at[dp], (peer, seq))

    def grad_recv(source):
        return remote(picked.at[source], slots.at[source], gs.at[source], gr.at[source], sibling)

    pl.semaphore_wait(barrier, n)
    column_copy().start()

    @pl.loop(1, n)
    def _(t):
        pos_copy(t).start()

    wproj_copy.wait()
    feats_copy.wait()
    emb[...] = jnp.dot(feats[...], wproj[...], preferred_element_type=F32).astype(BF16)

    @pl.loop(1, n)
    def _(t):
        emb_copy(t).start()

    emb_all[seq, dp] = emb[pl.ds(pl.multiple_of(dp * most, most), most), :]
    forward(0).start()

    @pl.loop(1, n)
    def _(t):
        pos_copy(t).wait()

    own_columns.wait()
    column_copy().wait()
    rows = jnp.concatenate([grad_rows[0], grad_rows[1]], axis=0)
    spot = lax.broadcasted_iota(jnp.int32, (2 * nearby, 1), 0)
    batch = 4

    @pl.loop(1, q + 1)
    def _(step):
        first = lax.rem(c + step, q) * batch
        at = jnp.concatenate([pos_all[first + i] for i in range(batch)], axis=1)
        hot = jnp.where(spot == at, 1.0, 0.0).astype(BF16)
        block = lax.dot_general(hot, rows, TN, preferred_element_type=F32).astype(BF16)
        for i in range(batch):
            picked[first + i] = block[i * most : (i + 1) * most]

            @pl.when(first + i != dp)
            def _():
                grad_send(first + i).start()

            @pl.when(first + i == dp)
            def _():
                slots[first + i] = block[i * most : (i + 1) * most]

    def rows_of(who):
        return pl.ds(pl.multiple_of(who * depth, 16), depth)

    def z_block(z):
        return wts.at[rows_of(z * 4 + b * 2 + a)]

    def up(hop, z):
        return remote(z_block(z), z_block(z), us.at[hop], ur.at[hop], (lax.rem(dp + 4, n), seq))

    def down(hop, z):
        return remote(z_block(z), z_block(z), ds_.at[hop], dr.at[hop], (lax.rem(dp + n - 4, n), seq))

    def y_copy(z, back=False):
        who = z * 4 + (1 - b if back else b) * 2 + a
        block = wts.at[rows_of(who)]
        return remote(block, block, ys.at[z], yr.at[z], across)

    def c_copy(side, z, back=False):
        y = b if side == 0 else 1 - b
        who = z * 4 + y * 2 + (1 - a if back else a)
        block = wts.at[rows_of(who)]
        return remote(block, block, cs.at[side, z], cr.at[side, z], sibling)

    def w_start():
        @pl.when(c < q - 1)
        def _():
            up(1, c).start()

        @pl.when(c > 0)
        def _():
            down(1, c).start()

        y_copy(c).start()
        c_copy(0, c).start()

    def w_hop(hop):
        below, above = c - hop, c + hop

        @pl.when(below >= 0)
        def _():
            up(hop, below).wait_recv()

            @pl.when(c < q - 1)
            def _():
                up(hop + 1, below).start()

            y_copy(below).start()
            c_copy(0, below).start()

        @pl.when(above < q)
        def _():
            down(hop, above).wait_recv()

            @pl.when(c > 0)
            def _():
                down(hop + 1, above).start()

            y_copy(above).start()
            c_copy(0, above).start()

    def w_side():
        @pl.loop(0, q)
        def _(t):
            z = lax.rem(c + t, q)
            y_copy(z, True).wait_recv()
            c_copy(1, z).start()

    def wx_copy():
        return remote(wts.at[:, pl.ds(wide, width)], wts_x, wxs.at[0], wxr.at[0], x_peer)

    def w_gathered():
        @pl.loop(0, q)
        def _(z):
            c_copy(0, z, True).wait_recv()
            c_copy(1, z, True).wait_recv()

        wx_copy().start()

    def w_done():
        for hop in range(1, q):

            @pl.when((c - hop + 1 >= 0) & (c < q - 1))
            def _():
                up(hop, c - hop + 1).wait_send()

            @pl.when((c + hop - 1 < q) & (c > 0))
            def _():
                down(hop, c + hop - 1).wait_send()

        @pl.loop(0, q)
        def _(z):
            y_copy(z).wait_send()
            c_copy(0, z).wait_send()
            c_copy(1, z).wait_send()

        wx_copy().wait_send()

    w_start()

    @pl.loop(1, n)
    def _(t):
        emb_copy(t).wait_recv()
        forward(t).start()

    w_hop(1)
    w_hop(2)

    count = slide_count[0]
    own = pl.multiple_of(seq * nearby, nearby)
    far_own = pl.multiple_of((1 - seq) * nearby, nearby)
    positions = jnp.concatenate([pos_all[i] for i in range(n)], axis=1)

    def natural_of(index, shift):
        return (index % part) * DILATION_STEP + lax.rem(index // part + 2 * shift, DILATION_STEP)

    inside = spot % nearby
    at_spot = spot - inside + natural_of(inside, seq)
    hot_perm = jnp.where(at_spot == positions, 1.0, 0.0).astype(BF16)
    own_spot = lax.broadcasted_iota(jnp.int32, (nearby, 1), 0) + seq * nearby
    hot_own = jnp.where(own_spot == positions, 1.0, 0.0).astype(BF16)

    @pl.loop(0, n)
    def _(t):
        forward(t).wait_recv()

    def regroup():
        blocks = [emb_all[i].reshape(slot_rows, width) for i in range(2)]
        for i in range(2):
            emb_ref[:, i * width : (i + 1) * width] = jnp.dot(
                hot_own, blocks[i], preferred_element_type=F32
            ).astype(BF16)
        for block in range(2):
            at = slice(block * nearby, (block + 1) * nearby)
            row = jnp.concatenate(
                [jnp.dot(hot_perm[at], blocks[i], preferred_element_type=F32) for i in range(2)],
                axis=-1,
            )
            center = jnp.mean(row, axis=-1, keepdims=True)
            spread = jnp.mean(jnp.square(row - center), axis=-1, keepdims=True)
            normed[at, :] = (
                (row - center) * lax.rsqrt(spread + EPSILON) * gain[...][None, :]
            ).astype(BF16)

    regroup()

    ranges = split_first(src.shape[3])

    def side(i):
        return 1 - b if i == 0 else b

    def ahead(t):
        return lax.rem(c + t, q)

    def behind(t):
        return lax.rem(c - t + q, q)

    def along(t):
        return (ahead(t) * 4 + b * 2 + a, seq)

    def to_sibling(r, i, t):
        at = ranges[r]
        return remote(
            src.at[1 - a, side(i), ahead(t), at],
            pair.at[i, t, at],
            s1.at[r, i, t],
            r1.at[r, i, t],
            sibling,
        )

    def to_across(r, t):
        at = ranges[r]
        return remote(stage_b.at[t, at], cross.at[t, at], s2.at[r, t], r2.at[r, t], across)

    def to_owner(r, t):
        at = ranges[r]
        return remote(stage_c.at[t, at], arrive.at[t, at], s3.at[r, t], r3.at[r, t], along(t))

    def result_along(r, t):
        block = out.at[a, b, c, ranges[r]]
        return remote(block, block, s4.at[r, t], r4.at[r, t], along(t))

    def result_across(r, t):
        block = out.at[a, b, behind(t), ranges[r]]
        return remote(block, block, s5.at[r, t], r5.at[r, t], across)

    def result_sibling(r, i, t):
        block = out.at[a, side(i), behind(t), ranges[r]]
        return remote(block, block, s6.at[r, i, t], r6.at[r, i, t], sibling)

    order = [t % q for t in range(1, q + 1)]

    @pl.loop(0, n)
    def _(source):
        @pl.when(source != dp)
        def _():
            grad_recv(source).wait_recv()

    rows_each = src.shape[3]
    grads = slots[...].reshape(slot_rows, width)
    tile = q * rows_each

    @pl.loop(0, n // q)
    def _(step):
        core = lax.rem(1 - a + step // 2, 2)
        y = lax.rem(1 - b + step, 2)
        first = pl.multiple_of((core * 2 + y) * tile, tile)
        product = lax.dot_general(
            feats[:, pl.ds(first, tile)], grads, TN, preferred_element_type=F32
        ).astype(BF16)
        for i in range(q):
            src[core, y, i] = product[i * rows_each : (i + 1) * rows_each]

        for i in range(2):

            @pl.when(step == i)
            def _():
                for r in range(ROUNDS):
                    for t in order:
                        to_sibling(r, i, t).start()

    def sum_b(r, t):
        to_sibling(r, 0, t).wait_recv()
        at = ranges[r]
        stage_b[t, at] = (
            src[a, 1 - b, ahead(t), at].astype(F32) + pair[0, t, at].astype(F32)
        ).astype(BF16)
        to_across(r, t).start()

    def sum_c(r, t):
        to_sibling(r, 1, t).wait_recv()
        to_across(r, t).wait_recv()
        at = ranges[r]
        stage_c[t, at] = (
            src[a, b, ahead(t), at].astype(F32)
            + pair[1, t, at].astype(F32)
            + cross[t, at].astype(F32)
        ).astype(BF16)
        if t:
            to_owner(r, t).start()

    def own_sum(r):
        at = ranges[r]
        total = stage_c[0, at].astype(F32)
        for t in range(1, q):
            to_owner(r, t).wait_recv()
            total = total + arrive[t, at].astype(F32)
        out[a, b, c, at] = total.astype(BF16)
        for t in range(1, q):
            result_along(r, t).start()
        result_across(r, 0).start()
        result_sibling(r, 1, 0).start()

    def result_on(r, t):
        result_along(r, t).wait_recv()
        result_across(r, t).start()
        result_sibling(r, 1, t).start()

    def result_over(r, t):
        result_across(r, t).wait_recv()
        result_sibling(r, 0, t).start()

    def reduce_done():
        for r in range(ROUNDS):

            @pl.loop(0, q)
            def _(t):
                for i in range(2):
                    to_sibling(r, i, t).wait_send()
                    result_sibling(r, i, t).wait()
                to_across(r, t).wait_send()
                result_across(r, t).wait_send()

            @pl.loop(1, q)
            def _(t):
                to_owner(r, t).wait_send()
                result_along(r, t).wait_send()

    lane = lax.broadcasted_iota(jnp.int32, (1, nearby), 1)
    row_at = lax.broadcasted_iota(jnp.int32, (nearby, 1), 0)
    far_lane = lax.broadcasted_iota(jnp.int32, (1, part), 1)

    def project(which):
        cols = slice(which * width, (which + 1) * width)
        value = jnp.dot(normed[...], wts[:, cols], preferred_element_type=F32).astype(BF16)
        if which == 0:
            value = value * BF16(HEAD_WIDTH**-0.5)
        qkv[which] = value

    def attend_head(start, other, head):
        group = head % DILATION_STEP
        cols = slice(head * HEAD_WIDTH, (head + 1) * HEAD_WIDTH)
        low, high = group * part, (group + 1) * part
        key_ok = start + natural_of(lane, seq) < count
        query_ok = start + natural_of(row_at, seq) < count
        far_ok = (
            other + far_lane * DILATION_STEP + lax.rem(group + 2 * seq, DILATION_STEP) < count
        )
        here = pl.ds(start, nearby)
        there = pl.ds(pl.multiple_of(other + low, part), part)
        qh, kh, vh = (qkv[i, here, :][:, cols] for i in range(3))
        far_k, far_v = (qkv[i, there, :][:, cols] for i in (1, 2))
        scores = lax.dot_general(qh, kh, NT, preferred_element_type=F32)
        scores = jnp.where(key_ok, scores, NEGATIVE)
        maximum = jnp.max(scores, axis=-1, keepdims=True)
        far = lax.dot_general(qh[low:high], far_k, NT, preferred_element_type=F32)
        far = jnp.where(far_ok, far, NEGATIVE)
        far_max = jnp.maximum(maximum[low:high], jnp.max(far, axis=-1, keepdims=True))
        maximum = put_rows(maximum, far_max, low, high)
        weight = jnp.exp(scores - maximum)
        in_lane = (lane >= low) & (lane < high)
        twice = jnp.where(in_lane, weight[low:high] * 2.0, weight[low:high])
        weight = put_rows(weight, twice, low, high)
        far_weight = jnp.exp(far - far_max)
        total = jnp.sum(weight, axis=-1, keepdims=True)
        far_total = jnp.sum(far_weight, axis=-1, keepdims=True)
        total = put_rows(total, total[low:high] + far_total, low, high)
        gathered = jnp.dot(weight.astype(BF16), vh, preferred_element_type=F32)
        far_gathered = jnp.dot(far_weight.astype(BF16), far_v, preferred_element_type=F32)
        gathered = put_rows(gathered, gathered[low:high] + far_gathered, low, high)
        return jnp.where(query_ok, gathered / total, 0.0).astype(BF16)

    def ctx_copy(j):
        at = pl.ds(j * 128, 128)
        return remote(ctx_send.at[:, at], ctx_peer.at[:, at], ks.at[j], kr.at[j], x_peer)

    pairs = width // 128

    def heads(mine, j):
        start, other = (own, far_own) if mine else (far_own, own)
        block = jnp.concatenate(
            [attend_head(start, other, 2 * j + i) for i in range(2)], axis=-1
        )
        at = pl.ds(j * 128, 128)
        if mine:
            ctx_own[:, at] = block
        else:
            ctx_send[:, at] = block
            ctx_copy(j).start()

    def finish_branch():
        for j in range(pairs):
            ctx_copy(j).wait()
        wx_copy().wait_recv()
        at_row = lax.broadcasted_iota(jnp.int32, (nearby, nearby), 0)
        at_lane = lax.broadcasted_iota(jnp.int32, (nearby, nearby), 1)
        ordered = []
        for shift, ref in ((seq, ctx_own), (1 - seq, ctx_peer)):
            back = jnp.where(at_row == natural_of(at_lane, shift), 1.0, 0.0).astype(BF16)
            ordered.append(jnp.dot(back, ref[...], preferred_element_type=F32).astype(BF16))
        for cols, weight in ((seq, wts.at[:, pl.ds(wide, width)]), (1 - seq, wts_x)):
            total = None
            for value, owner in zip(ordered, (seq, 1 - seq)):
                at = pl.ds(pl.multiple_of(owner * width, width), width)
                term = jnp.dot(value, weight[at, :], preferred_element_type=F32)
                total = term if total is None else total + term
            branch_ref[:, pl.ds(pl.multiple_of(cols * width, width), width)] = total.astype(BF16)

    reduce_steps = []
    for r in range(ROUNDS):
        reduce_steps += [functools.partial(sum_b, r, t) for t in order]
    for r in range(ROUNDS):
        reduce_steps += [functools.partial(sum_c, r, t) for t in order]
        reduce_steps += [functools.partial(own_sum, r)]
        if r:
            reduce_steps += [functools.partial(result_on, r - 1, t) for t in range(1, q)]
            reduce_steps += [functools.partial(result_over, r - 1, t) for t in range(q)]
    r = ROUNDS - 1
    reduce_steps += [functools.partial(result_on, r, t) for t in range(1, q)]
    reduce_steps += [functools.partial(result_over, r, t) for t in range(q)]

    work = [functools.partial(project, i) for i in range(3)]
    work += [functools.partial(heads, False, j) for j in range(pairs)]
    work += [functools.partial(heads, True, j) for j in range(pairs)]

    w_hop(3)
    split = 2 * q
    for step in reduce_steps[:q]:
        step()
    w_side()
    for step in reduce_steps[q:split]:
        step()
    w_gathered()
    rest = reduce_steps[split:]
    slots_left = len(work)
    taken = 0
    for i, job in enumerate(work):
        job()
        until = (i + 1) * len(rest) // (slots_left + 2)
        for step in rest[taken:until]:
            step()
        taken = until
    finish_branch()
    for step in rest[taken:]:
        step()

    @pl.loop(1, n)
    def _(t):
        emb_copy(t).wait_send()

    @pl.loop(0, n)
    def _(t):
        forward(t).wait_send()

        @pl.when(t != dp)
        def _():
            grad_send(t).wait_send()

    w_done()
    reduce_done()


def finish_kernel(emb, branch, summed, emb_out, branch_out, grad_out, wide, sems):
    copies = [
        pltpu.make_async_copy(emb, emb_out.at[0], sems.at[0]),
        pltpu.make_async_copy(branch, branch_out.at[0], sems.at[1]),
    ]
    for copy in copies:
        copy.start()
    size = summed.shape[0] // 4
    for i in range(4):
        at = pl.ds(i * size, size)
        wide[at, :] = summed[at, :].astype(F32)
        copies.append(pltpu.make_async_copy(wide.at[at], grad_out.at[at], sems.at[2 + i]))
        copies[-1].start()
    for copy in copies:
        copy.wait()


def finish(emb, branch, summed):
    return pl.pallas_call(
        finish_kernel,
        out_shape=(
            jax.ShapeDtypeStruct((1, *emb.shape), BF16),
            jax.ShapeDtypeStruct((1, *branch.shape), BF16),
            jax.ShapeDtypeStruct(summed.shape, F32),
        ),
        in_specs=[VM] * 3,
        out_specs=(HBM,) * 3,
        scratch_shapes=[pltpu.VMEM(summed.shape, F32), DMA((6,))],
        compiler_params=pltpu.CompilerParams(vmem_limit_bytes=16 * 1024 * 1024),
        cost_estimate=pl.CostEstimate(flops=0, bytes_accessed=6_000_000, transcendentals=0),
    )(emb, branch, summed)


def in_hbm(operand):
    return pltpu.with_memory_space_constraint(operand, pltpu.HBM)


def fused(tile_feats, tile_pos, slide_count, w_proj, emb_grad, ln_gain, w_qkv, w_out):
    n = lax.axis_size("dp")
    slot_rows, features = tile_feats.shape
    nearby = emb_grad.shape[1]
    most = slot_rows // n
    width = w_proj.shape[1]
    q = n // 4
    shape = (2, 2, q, features // n, width)
    rounds = (ROUNDS, q)
    smem = pl.BlockSpec(memory_space=pltpu.SMEM)
    scratch = [
        pltpu.VMEM(tile_feats.shape, BF16),
        pltpu.VMEM(w_proj.shape, BF16),
        pltpu.VMEM(tile_pos.shape, jnp.int32),
        pltpu.VMEM(ln_gain.shape, F32),
        pltpu.VMEM(w_qkv.shape, BF16),
        pltpu.VMEM(w_out.shape, BF16),
        pltpu.VMEM((slot_rows, width), BF16),
        pltpu.VMEM((n, 1, most), jnp.int32),
        pltpu.VMEM((n, 1, most), jnp.int32),
        pltpu.VMEM((2, n, most, width), BF16),
        pltpu.VMEM((2, nearby, width), BF16),
        pltpu.VMEM((n, most, width), BF16),
        pltpu.VMEM((n, most, width), BF16),
        pltpu.VMEM((D, 4 * width), BF16),
        pltpu.VMEM((D, width), BF16),
        pltpu.VMEM((2 * nearby, D), BF16),
        pltpu.VMEM((3, 2 * nearby, width), BF16),
        pltpu.VMEM((nearby, width), BF16),
        pltpu.VMEM((nearby, width), BF16),
        pltpu.VMEM((nearby, width), BF16),
        pltpu.VMEM(shape, BF16),
        pltpu.VMEM(shape[1:], BF16),
        pltpu.VMEM(shape[2:], BF16),
        pltpu.VMEM(shape[2:], BF16),
        pltpu.VMEM(shape[2:], BF16),
        pltpu.VMEM(shape[2:], BF16),
        DMA((7,)),
    ]
    scratch += [DMA((1,))] * 2
    scratch += [DMA((n,))] * 8
    scratch += [DMA((q + 1,))] * 4
    scratch += [DMA((q,))] * 2
    scratch += [DMA((2, q))] * 2
    scratch += [DMA((1,))] * 2
    scratch += [DMA((width // 128,))] * 2
    scratch += [DMA((ROUNDS, 2, q))] * 2
    scratch += [DMA(rounds)] * 8
    scratch += [DMA((ROUNDS, 2, q))] * 2
    row = jax.ShapeDtypeStruct((nearby, D), BF16)
    emb, branch, summed = pl.pallas_call(
        functools.partial(fused_kernel, n),
        out_shape=(row, row, jax.ShapeDtypeStruct(shape, BF16)),
        in_specs=[HBM, HBM, smem, HBM, HBM, HBM, HBM, HBM],
        out_specs=(VM, VM, VM),
        scratch_shapes=scratch,
        compiler_params=pltpu.CompilerParams(
            collective_id=5, has_side_effects=True, vmem_limit_bytes=48 * 1024 * 1024
        ),
        cost_estimate=pl.CostEstimate(
            flops=5_000_000_000, bytes_accessed=10_000_000, transcendentals=1_000_000
        ),
    )(
        in_hbm(tile_feats),
        in_hbm(tile_pos),
        slide_count,
        in_hbm(w_proj),
        in_hbm(emb_grad),
        in_hbm(ln_gain),
        in_hbm(w_qkv),
        in_hbm(w_out),
    )
    return finish(emb, branch, summed.reshape(features, width))


def solution(mesh):
    in_specs = (
        P("dp", None),
        P("dp", None),
        P("dp"),
        P(None, "seq"),
        P("dp", "seq", None),
        P(),
        P("dp", None),
        P("dp", None),
    )
    out_specs = (P("dp", "seq", None), P("dp", "seq", None), P(None, "seq"))
    one_kernel = mesh.shape["dp"] == 16 and mesh.shape["seq"] == 2
    body = fused if one_kernel else local
    return jax.shard_map(body, mesh=mesh, in_specs=in_specs, out_specs=out_specs, check_vma=False)
```

```python
import functools

import jax
import jax.numpy as jnp
from jax import lax
from jax.experimental import pallas as pl
from jax.experimental.pallas import tpu as pltpu
from jax.sharding import PartitionSpec as P

D = 768
HEAD_COUNT = 12
HEAD_WIDTH = 64
DILATION_STEP = 4
NEGATIVE = -1e30
EPSILON = 1e-05
STEP_HEADS = 4

F32 = jnp.float32
BF16 = jnp.bfloat16
MESH = pl.DeviceIdType.MESH


def greet(dp_peers, seq_peers):
    barrier = pltpu.get_barrier_semaphore()
    dp_count, seq_count = lax.axis_size("dp"), lax.axis_size("seq")
    dp, seq = lax.axis_index("dp"), lax.axis_index("seq")
    if dp_peers:

        @pl.loop(1, dp_count)
        def _(t):
            pl.semaphore_signal(
                barrier, device_id=(lax.rem(dp + t, dp_count), seq), device_id_type=MESH
            )

    if seq_peers:

        @pl.loop(1, seq_count)
        def _(t):
            pl.semaphore_signal(
                barrier, device_id=(dp, lax.rem(seq + t, seq_count)), device_id_type=MESH
            )

    pl.semaphore_wait(
        barrier, (dp_count - 1 if dp_peers else 0) + (seq_count - 1 if seq_peers else 0)
    )


def remote(src, dst, send, recv, device):
    return pltpu.make_async_remote_copy(
        src_ref=src,
        dst_ref=dst,
        send_sem=send,
        recv_sem=recv,
        device_id=device,
        device_id_type=MESH,
    )


def dispatch_kernel(
    n, seq_count, pos, grad, emb, pos_out, emb_out, grad_out, grad_rows, picked, *sems
):
    ps, pr, xs, xr, es, er, gs, gr, fs, fr = sems
    dp, seq = lax.axis_index("dp"), lax.axis_index("seq")
    most = pos.shape[2]
    nearby, width = grad.shape[1:]
    greet(True, True)

    def column_copy(t):
        peer = lax.rem(seq + t, seq_count)
        return remote(grad.at[peer], grad_rows.at[seq], xs.at[t], xr.at[t], (dp, peer))

    def pos_copy(t):
        peer = lax.rem(dp + t, n)
        return remote(pos.at[peer], pos_out.at[dp], ps.at[t], pr.at[t], (peer, seq))

    def emb_copy(t):
        peer = lax.rem(dp + t, n)
        return remote(emb.at[peer], emb_out.at[seq, dp], es.at[t], er.at[t], (peer, seq))

    def grad_copy(t):
        peer = lax.rem(dp + t, n)
        return remote(picked.at[peer], grad_out.at[dp], gs.at[t], gr.at[t], (peer, seq))

    def forward(k, t):
        source = lax.rem(dp - t + n, n)
        peer = lax.rem(seq + k, seq_count)
        block = emb_out.at[seq, source]
        return remote(block, block, fs.at[k, t], fr.at[k, t], (dp, peer))

    @pl.loop(1, seq_count)
    def _(t):
        column_copy(t).start()

    @pl.loop(1, n)
    def _(t):
        pos_copy(t).start()

    @pl.loop(1, n)
    def _(t):
        emb_copy(t).start()

    pos_out[dp] = pos[dp]
    grad_rows[seq] = grad[seq]
    emb_out[seq, dp] = emb[dp]

    @pl.loop(1, n)
    def _(t):
        pos_copy(t).wait()

    @pl.loop(1, seq_count)
    def _(t):
        column_copy(t).wait()

    rows = jnp.concatenate([grad_rows[i] for i in range(seq_count)], axis=0)
    spot = lax.broadcasted_iota(jnp.int32, (nearby * seq_count, 1), 0)
    batch = 4
    for first in range(0, n, batch):
        at = jnp.concatenate([pos_out[first + i] for i in range(batch)], axis=1)
        hot = jnp.where(spot == at, 1.0, 0.0).astype(BF16)
        block = lax.dot_general(
            hot, rows, (((0,), (0,)), ((), ())), preferred_element_type=F32
        ).astype(BF16)
        for i in range(batch):
            picked[first + i] = block[i * most : (i + 1) * most]

    @pl.loop(1, n)
    def _(t):
        grad_copy(t).start()

    grad_out[dp] = picked[dp]
    for k in range(1, seq_count):
        forward(k, 0).start()

    @pl.loop(1, n)
    def _(t):
        emb_copy(t).wait_recv()
        for k in range(1, seq_count):
            forward(k, t).start()

    @pl.loop(1, n)
    def _(t):
        emb_copy(t).wait_send()
        grad_copy(t).wait()

    @pl.loop(0, n)
    def _(t):
        for k in range(1, seq_count):
            forward(k, t).wait()


def reduce_kernel(n, feats, slots, out, src, pair, cross, stage_b, stage_c, arrive, *sems):
    s1, r1, s2, r2, s3, r3, s4, r4, s5, r5, s6, r6 = sems
    dp, seq = lax.axis_index("dp"), lax.axis_index("seq")
    q = n // 4
    a, b, c = lax.rem(dp, 2), lax.rem(dp // 2, 2), dp // 4
    sibling = (dp + 1 - 2 * a, seq)
    across = (dp + 2 - 4 * b, seq)
    barrier = pltpu.get_barrier_semaphore()
    pl.semaphore_signal(barrier, device_id=sibling, device_id_type=MESH)
    pl.semaphore_signal(barrier, device_id=across, device_id_type=MESH)

    def ahead(t):
        return lax.rem(c + t, q)

    def behind(t):
        return lax.rem(c - t + q, q)

    def along(t):
        return (ahead(t) * 4 + b * 2 + a, seq)

    @pl.loop(1, q)
    def _(t):
        pl.semaphore_signal(barrier, device_id=along(t), device_id_type=MESH)

    rows = src.shape[3]
    tile = 512
    for first in range(0, n * rows, tile):
        product = lax.dot_general(
            feats[:, first : first + tile],
            slots[...],
            (((0,), (0,)), ((), ())),
            preferred_element_type=F32,
        ).astype(BF16)
        for i in range(tile // rows):
            k = first // rows + i
            src[k // (2 * q), k // q % 2, k % q] = product[i * rows : (i + 1) * rows]

    pl.semaphore_wait(barrier, q + 1)

    def side(i):
        return 1 - b if i == 0 else b

    def to_sibling(i, t):
        return remote(
            src.at[1 - a, side(i), ahead(t)], pair.at[i, t], s1.at[i, t], r1.at[i, t], sibling
        )

    def to_across(t):
        return remote(stage_b.at[t], cross.at[t], s2.at[t], r2.at[t], across)

    def to_owner(t):
        return remote(stage_c.at[t], arrive.at[t], s3.at[t], r3.at[t], along(t))

    def result_along(t):
        block = out.at[a, b, c]
        return remote(block, block, s4.at[t], r4.at[t], along(t))

    def result_across(t):
        block = out.at[a, b, behind(t)]
        return remote(block, block, s5.at[t], r5.at[t], across)

    def result_sibling(i, t):
        block = out.at[a, side(i), behind(t)]
        return remote(block, block, s6.at[i, t], r6.at[i, t], sibling)

    for i in (0, 1):

        @pl.loop(1, q + 1)
        def _(t):
            to_sibling(i, lax.rem(t, q)).start()

    @pl.loop(1, q + 1)
    def _(step):
        t = lax.rem(step, q)
        to_sibling(0, t).wait_recv()
        stage_b[t] = (src[a, 1 - b, ahead(t)].astype(F32) + pair[0, t].astype(F32)).astype(BF16)
        to_across(t).start()

    @pl.loop(1, q + 1)
    def _(step):
        t = lax.rem(step, q)
        to_sibling(1, t).wait_recv()
        to_across(t).wait_recv()
        stage_c[t] = (
            src[a, b, ahead(t)].astype(F32) + pair[1, t].astype(F32) + cross[t].astype(F32)
        ).astype(BF16)

        @pl.when(step < q)
        def _():
            to_owner(t).start()

    total = stage_c[0].astype(F32)
    for t in range(1, q):
        to_owner(t).wait_recv()
        total = total + arrive[t].astype(F32)
    out[a, b, c] = total.astype(BF16)

    @pl.loop(1, q)
    def _(t):
        result_along(t).start()

    result_across(0).start()
    result_sibling(1, 0).start()

    @pl.loop(1, q)
    def _(t):
        result_along(t).wait_recv()
        result_across(t).start()
        result_sibling(1, t).start()

    @pl.loop(0, q)
    def _(t):
        result_across(t).wait_recv()
        result_sibling(0, t).start()

    @pl.loop(1, q)
    def _(t):
        to_owner(t).wait_send()
        result_along(t).wait_send()

    for i in (0, 1):

        @pl.loop(0, q)
        def _(t):
            to_sibling(i, t).wait_send()
            result_sibling(i, t).wait()

    @pl.loop(0, q)
    def _(t):
        to_across(t).wait_send()
        result_across(t).wait_send()


VM = pl.BlockSpec(memory_space=pltpu.VMEM)
DMA = pltpu.SemaphoreType.DMA


def exchange(kernel, ident, outs, scratch, *operands):
    return pl.pallas_call(
        kernel,
        out_shape=tuple(jax.ShapeDtypeStruct(shape, kind) for shape, kind in outs),
        in_specs=[VM] * len(operands),
        out_specs=tuple([VM] * len(outs)),
        scratch_shapes=scratch,
        compiler_params=pltpu.CompilerParams(
            collective_id=ident, has_side_effects=True, vmem_limit_bytes=32 * 1024 * 1024
        ),
        cost_estimate=pl.CostEstimate(
            flops=10_000_000_000, bytes_accessed=10_000_000, transcendentals=0
        ),
    )(*operands)


def put_rows(whole, rows, low, high):
    pieces = [whole[:low]] if low else []
    pieces.append(rows)
    if high < whole.shape[0]:
        pieces.append(whole[high:])
    return jnp.concatenate(pieces, axis=0)


def attention_kernel(
    seq_count,
    nearby,
    meta_ref,
    rows_ref,
    gain_ref,
    wq_ref,
    wk_ref,
    wv_ref,
    wo_ref,
    emb_ref,
    branch_ref,
    normed,
    context,
):
    step = pl.program_id(0)
    me = meta_ref[0]
    count = meta_ref[1]
    part = nearby // DILATION_STEP
    own = pl.multiple_of(me * nearby, nearby)

    @pl.when(step == 0)
    def _():
        for block in range(seq_count):
            at = slice(block * nearby, (block + 1) * nearby)
            wide = jnp.concatenate(
                [rows_ref[c, at, :] for c in range(seq_count)], axis=-1
            ).astype(F32)
            center = jnp.mean(wide, axis=-1, keepdims=True)
            spread = jnp.mean(jnp.square(wide - center), axis=-1, keepdims=True)
            normed[at, :] = (
                (wide - center) * lax.rsqrt(spread + EPSILON) * gain_ref[...]
            ).astype(BF16)

    mine = normed[pl.ds(own, nearby), :]
    query = jnp.dot(mine, wq_ref[...], preferred_element_type=F32).astype(BF16)
    query = query * BF16(HEAD_WIDTH**-0.5)
    key = jnp.dot(mine, wk_ref[...], preferred_element_type=F32).astype(BF16)
    value = jnp.dot(mine, wv_ref[...], preferred_element_type=F32).astype(BF16)
    far_keys, far_values = [], []
    for other in range(1, seq_count):
        block = lax.rem(me + other, seq_count)
        start = pl.multiple_of(block * nearby, nearby)
        theirs = normed[pl.ds(start, nearby), :]
        far_keys.append(jnp.dot(theirs, wk_ref[...], preferred_element_type=F32).astype(BF16))
        far_values.append(jnp.dot(theirs, wv_ref[...], preferred_element_type=F32).astype(BF16))

    lane = lax.broadcasted_iota(jnp.int32, (1, nearby), 1)
    key_ok = own + (lane % part) * DILATION_STEP + lane // part < count
    row = lax.broadcasted_iota(jnp.int32, (nearby, 1), 0)
    query_ok = own + (row % part) * DILATION_STEP + row // part < count
    far_lane = lax.broadcasted_iota(jnp.int32, (1, part * (seq_count - 1)), 1)
    far_block = lax.rem(me + 1 + far_lane // part, seq_count)
    far_spot = far_block * nearby + far_lane % part * DILATION_STEP
    dims = (((1,), (1,)), ((), ()))
    outs = []
    for head in range(STEP_HEADS):
        shift = head % DILATION_STEP
        cols = slice(head * HEAD_WIDTH, (head + 1) * HEAD_WIDTH)
        low, high = shift * part, (shift + 1) * part
        q, k, v = query[:, cols], key[:, cols], value[:, cols]
        scores = lax.dot_general(q, k, dims, preferred_element_type=F32)
        scores = jnp.where(key_ok, scores, NEGATIVE)
        maximum = jnp.max(scores, axis=-1, keepdims=True)
        far_k = jnp.concatenate([x[low:high, cols] for x in far_keys], axis=0)
        far_v = jnp.concatenate([x[low:high, cols] for x in far_values], axis=0)
        far_ok = far_spot + shift < count
        far = lax.dot_general(q[low:high], far_k, dims, preferred_element_type=F32)
        far = jnp.where(far_ok, far, NEGATIVE)
        far_max = jnp.maximum(maximum[low:high], jnp.max(far, axis=-1, keepdims=True))
        maximum = put_rows(maximum, far_max, low, high)
        weight = jnp.exp(scores - maximum)
        in_lane = (lane >= low) & (lane < high)
        twice = jnp.where(in_lane, weight[low:high] * 2.0, weight[low:high])
        weight = put_rows(weight, twice, low, high)
        far_weight = jnp.exp(far - far_max)
        total = jnp.sum(weight, axis=-1, keepdims=True)
        far_total = jnp.sum(far_weight, axis=-1, keepdims=True)
        total = put_rows(total, total[low:high] + far_total, low, high)
        gathered = jnp.dot(weight.astype(BF16), v, preferred_element_type=F32)
        far_gathered = jnp.dot(far_weight.astype(BF16), far_v, preferred_element_type=F32)
        gathered = put_rows(gathered, gathered[low:high] + far_gathered, low, high)
        outs.append(jnp.where(query_ok, gathered / total, 0.0).astype(BF16))
    context[step] = jnp.concatenate(outs, axis=-1)

    @pl.when(step == pl.num_programs(0) - 1)
    def _():
        at_row = lax.broadcasted_iota(jnp.int32, (nearby, nearby), 0)
        at_lane = lax.broadcasted_iota(jnp.int32, (nearby, nearby), 1)
        natural = (at_lane % part) * DILATION_STEP + at_lane // part
        back = jnp.where(at_row == natural, 1.0, 0.0).astype(BF16)
        ordered = jnp.concatenate(
            [rows_ref[c, pl.ds(own, nearby), :] for c in range(seq_count)], axis=-1
        )
        emb_ref[...] = jnp.dot(back, ordered, preferred_element_type=F32).astype(BF16)
        whole = jnp.concatenate(
            [context[i] for i in range(HEAD_COUNT // STEP_HEADS)], axis=-1
        )
        whole = jnp.dot(back, whole, preferred_element_type=F32).astype(BF16)
        branch_ref[...] = jnp.dot(whole, wo_ref[...], preferred_element_type=F32).astype(BF16)


def attend(meta, rows, gain, weights, seq_count, nearby):
    width = STEP_HEADS * HEAD_WIDTH
    steps = HEAD_COUNT // STEP_HEADS
    slide_len = rows.shape[1]
    full = lambda *shape: pl.BlockSpec(shape, lambda i: (0,) * len(shape))
    out = jax.ShapeDtypeStruct((nearby, D), BF16)
    return pl.pallas_call(
        functools.partial(attention_kernel, seq_count, nearby),
        out_shape=(out, out),
        grid=(steps,),
        in_specs=[
            pl.BlockSpec(memory_space=pltpu.SMEM),
            full(*rows.shape),
            full(1, D),
            pl.BlockSpec((D, width), lambda i: (0, i)),
            pl.BlockSpec((D, width), lambda i: (0, steps + i)),
            pl.BlockSpec((D, width), lambda i: (0, 2 * steps + i)),
            pl.BlockSpec((D, D), lambda i: (0, 3)),
        ],
        out_specs=(full(nearby, D), full(nearby, D)),
        scratch_shapes=[
            pltpu.VMEM((slide_len, D), BF16),
            pltpu.VMEM((steps, nearby, width), BF16),
        ],
        compiler_params=pltpu.CompilerParams(vmem_limit_bytes=60 * 1024 * 1024),
        cost_estimate=pl.CostEstimate(
            flops=20_000_000_000, bytes_accessed=20_000_000, transcendentals=1_000_000
        ),
    )(meta, rows, gain, weights, weights, weights, weights)


def local(tile_feats, tile_pos, slide_count, w_proj, emb_grad, ln_gain, w_qkv, w_out):
    seq_count = lax.axis_size("seq")
    n = lax.axis_size("dp")
    seq_index = lax.axis_index("seq")
    slot_rows = tile_feats.shape[0]
    nearby = emb_grad.shape[1]
    slide_len = nearby * seq_count
    part = nearby // DILATION_STEP
    most = slot_rows // n
    width = w_proj.shape[1]
    weights = lax.all_gather(
        jnp.concatenate([w_qkv, w_out], axis=1), "dp", axis=0, tiled=True
    )
    emb_part = jnp.dot(tile_feats, w_proj, preferred_element_type=F32).astype(BF16)
    positions, arrived, slot_grad = exchange(
        functools.partial(dispatch_kernel, n, seq_count),
        1,
        [
            ((n, 1, most), jnp.int32),
            ((seq_count, n, most, width), BF16),
            ((n, most, width), BF16),
        ],
        [pltpu.VMEM((seq_count, nearby, width), BF16), pltpu.VMEM((n, most, width), BF16)]
        + [DMA((n,))] * 2
        + [DMA((seq_count,))] * 2
        + [DMA((n,))] * 4
        + [DMA((seq_count, n))] * 2,
        tile_pos.reshape(n, 1, most),
        emb_grad.reshape(nearby, seq_count, width).transpose(1, 0, 2),
        emb_part.reshape(n, most, width),
    )
    positions = positions.reshape(slot_rows)
    spot = jnp.arange(slide_len, dtype=jnp.int32)
    features = tile_feats.shape[1]
    quarter = n // 4
    shape = (2, 2, quarter, features // n, width)
    (summed,) = exchange(
        functools.partial(reduce_kernel, n),
        3,
        [(shape, BF16)],
        [pltpu.VMEM(shape, BF16), pltpu.VMEM(shape[1:], BF16)]
        + [pltpu.VMEM(shape[2:], BF16)] * 4
        + [DMA((2, quarter))] * 2
        + [DMA((quarter,))] * 8
        + [DMA((2, quarter))] * 2,
        tile_feats,
        slot_grad.reshape(slot_rows, width),
    )
    proj_grad = summed.reshape(features, width).astype(F32)

    inside = spot % nearby
    at_spot = spot - inside + (inside % part) * DILATION_STEP + inside // part
    hot_perm = (at_spot[:, None] == positions[None, :]).astype(BF16)
    rows = jnp.einsum(
        "ps,csw->cpw",
        hot_perm,
        arrived.reshape(seq_count, slot_rows, width),
        preferred_element_type=F32,
    ).astype(BF16)
    meta = jnp.stack([seq_index.astype(jnp.int32), slide_count[0]])
    local_emb, attn_branch = attend(
        meta, rows, ln_gain.reshape(1, D), weights, seq_count, nearby
    )
    return (local_emb[None], attn_branch[None], proj_grad)


SPLIT = 5
HBM = pl.BlockSpec(memory_space=pltpu.HBM)
NT = (((1,), (1,)), ((), ()))
TN = (((0,), (0,)), ((), ()))


def fused_kernel(
    n,
    feats_hbm,
    pos_hbm,
    slide_count,
    wproj_hbm,
    grad,
    gain_hbm,
    wqkv_hbm,
    wout_hbm,
    emb_ref,
    branch_ref,
    out,
    feats,
    wproj,
    pos,
    gain,
    wqkv,
    wout,
    emb,
    pos_in,
    pos_all,
    emb_all,
    grad_rows,
    picked,
    slots,
    wts,
    wts_x,
    normed,
    qkv,
    ctx_send,
    ctx_own,
    ctx_peer,
    src,
    pair,
    cross,
    stage_y,
    stage_za,
    stage_zb,
    in_za,
    in_zb,
    stage_yb,
    cross_b,
    local_sems,
    xs,
    xr,
    ps,
    pr,
    es,
    er,
    fs,
    fr,
    gs,
    gr,
    us,
    ur,
    ds_,
    dr,
    ys,
    yr,
    cs,
    cr,
    wxs,
    wxr,
    ks,
    kr,
    s1,
    r1,
    s2,
    r2,
    s3,
    r3,
    s4,
    r4,
    gus,
    gur,
    gds,
    gdr,
    gys,
    gyr,
    gbs,
    gbr,
    gcs,
    gcr,
    gxs,
    gxr,
):
    dp, seq = lax.axis_index("dp"), lax.axis_index("seq")
    q = n // 4
    a, b, c = lax.rem(dp, 2), lax.rem(dp // 2, 2), dp // 4
    x_peer = (dp, 1 - seq)
    sib_dp = dp + 1 - 2 * a
    y_dp = dp + 2 - 4 * b
    sibling, across = (sib_dp, seq), (y_dp, seq)
    most = pos_in.shape[2]
    slot_rows = feats.shape[0]
    nearby = grad.shape[1]
    width = wproj.shape[1]
    depth = wqkv.shape[0]
    part = nearby // DILATION_STEP
    inner = HEAD_COUNT * HEAD_WIDTH
    wide = 3 * width

    barrier = pltpu.get_barrier_semaphore()

    @pl.loop(1, n)
    def _(t):
        pl.semaphore_signal(barrier, device_id=(lax.rem(dp + t, n), seq), device_id_type=MESH)

    pl.semaphore_signal(barrier, device_id=x_peer, device_id_type=MESH)
    feats_copy = pltpu.make_async_copy(feats_hbm, feats, local_sems.at[0])
    wproj_copy = pltpu.make_async_copy(wproj_hbm, wproj, local_sems.at[1])
    pos_load = pltpu.make_async_copy(pos_hbm, pos, local_sems.at[3])
    gain_load = pltpu.make_async_copy(gain_hbm, gain, local_sems.at[4])
    wqkv_load = pltpu.make_async_copy(wqkv_hbm, wqkv, local_sems.at[5])
    wout_load = pltpu.make_async_copy(wout_hbm, wout, local_sems.at[6])
    pos_load.start()
    wqkv_load.start()
    wout_load.start()
    gain_load.start()
    wproj_copy.start()
    feats_copy.start()
    pos_load.wait()
    for i in range(n):
        pos_in[i] = pos[:, i * most : (i + 1) * most]
    wqkv_load.wait()
    wout_load.wait()
    gain_load.wait()
    mine_w = pl.ds(pl.multiple_of(dp * depth, 16), depth)
    half = pl.multiple_of(seq * width, width)
    for i in range(3):
        wts[mine_w, i * width : (i + 1) * width] = wqkv[
            :, pl.ds(pl.multiple_of(i * inner + half, 128), width)
        ]
    wts[mine_w, wide:] = wout[:, pl.ds(half, width)]
    pos_all[dp] = pos_in[dp]

    def column_copy():
        block = grad.at[0, :, pl.ds(pl.multiple_of((1 - seq) * width, 128), width)]
        return remote(block, grad_rows.at[seq], xs.at[0], xr.at[0], x_peer)

    own_columns = pltpu.make_async_copy(
        grad.at[0, :, pl.ds(half, width)], grad_rows.at[seq], local_sems.at[2]
    )
    own_columns.start()

    def pos_copy(t):
        peer = lax.rem(dp + t, n)
        return remote(pos_in.at[peer], pos_all.at[dp], ps.at[t], pr.at[t], (peer, seq))

    def emb_copy(t):
        peer = lax.rem(dp + t, n)
        return remote(
            emb.at[pl.ds(pl.multiple_of(peer * most, most), most)],
            emb_all.at[seq, dp],
            es.at[t],
            er.at[t],
            (peer, seq),
        )

    def forward(t):
        block = emb_all.at[seq, lax.rem(dp - t + n, n)]
        return remote(block, block, fs.at[t], fr.at[t], x_peer)

    def grad_send(peer):
        return remote(picked.at[peer], slots.at[dp], gs.at[peer], gr.at[dp], (peer, seq))

    def grad_recv(source):
        return remote(picked.at[source], slots.at[source], gs.at[source], gr.at[source], sibling)

    def rows_of(who):
        return pl.ds(pl.multiple_of(who * depth, 16), depth)

    def z_block(z):
        return wts.at[rows_of(z * 4 + b * 2 + a)]

    def up(hop, z):
        return remote(z_block(z), z_block(z), us.at[hop], ur.at[hop], (lax.rem(dp + 4, n), seq))

    def down(hop, z):
        return remote(z_block(z), z_block(z), ds_.at[hop], dr.at[hop], (lax.rem(dp + n - 4, n), seq))

    def y_copy(z, back=False):
        who = z * 4 + (1 - b if back else b) * 2 + a
        block = wts.at[rows_of(who)]
        return remote(block, block, ys.at[z], yr.at[z], across)

    def c_copy(side, z, back=False):
        y = b if side == 0 else 1 - b
        who = z * 4 + y * 2 + (1 - a if back else a)
        block = wts.at[rows_of(who)]
        return remote(block, block, cs.at[side, z], cr.at[side, z], sibling)

    def w_start():
        @pl.when(c < q - 1)
        def _():
            up(1, c).start()

        @pl.when(c > 0)
        def _():
            down(1, c).start()

        y_copy(c).start()
        c_copy(0, c).start()

    def w_hop(hop):
        below, above = c - hop, c + hop

        @pl.when(below >= 0)
        def _():
            up(hop, below).wait_recv()

            @pl.when(c < q - 1)
            def _():
                up(hop + 1, below).start()

            y_copy(below).start()
            c_copy(0, below).start()

        @pl.when(above < q)
        def _():
            down(hop, above).wait_recv()

            @pl.when(c > 0)
            def _():
                down(hop + 1, above).start()

            y_copy(above).start()
            c_copy(0, above).start()

    def w_side():
        @pl.loop(0, q)
        def _(t):
            z = lax.rem(c + t, q)
            y_copy(z, True).wait_recv()
            c_copy(1, z).start()

    def wx_copy():
        return remote(wts.at[:, pl.ds(wide, width)], wts_x, wxs.at[0], wxr.at[0], x_peer)

    def w_gathered():
        @pl.loop(0, q)
        def _(z):
            c_copy(0, z, True).wait_recv()
            c_copy(1, z, True).wait_recv()

        wx_copy().start()

    def w_done():
        for hop in range(1, q):

            @pl.when((c - hop + 1 >= 0) & (c < q - 1))
            def _():
                up(hop, c - hop + 1).wait_send()

            @pl.when((c + hop - 1 < q) & (c > 0))
            def _():
                down(hop, c + hop - 1).wait_send()

        @pl.loop(0, q)
        def _(z):
            y_copy(z).wait_send()
            c_copy(0, z).wait_send()
            c_copy(1, z).wait_send()

        wx_copy().wait_send()

    spot = lax.broadcasted_iota(jnp.int32, (2 * nearby, 1), 0)

    @pl.when(c == 0)
    def _():
        in_za[0] = jnp.zeros_like(in_za[0])
        in_zb[0] = jnp.zeros_like(in_zb[0])

    @pl.when(c == q - 1)
    def _():
        in_za[1] = jnp.zeros_like(in_za[1])
        in_zb[1] = jnp.zeros_like(in_zb[1])

    def first_sends():
        pl.semaphore_wait(barrier, n)
        column_copy().start()

        @pl.loop(1, n)
        def _(t):
            pos_copy(t).start()

    def embed():
        wproj_copy.wait()
        feats_copy.wait()
        emb[...] = jnp.dot(feats[...], wproj[...], preferred_element_type=F32).astype(BF16)

    def emb_sends():
        @pl.loop(1, n)
        def _(t):
            emb_copy(t).start()

        emb_all[seq, dp] = emb[pl.ds(pl.multiple_of(dp * most, most), most), :]
        forward(0).start()

    def emb_on(low, high):
        @pl.loop(low, high)
        def _(t):
            emb_copy(t).wait_recv()
            forward(t).start()

    def grad_sends():
        @pl.loop(1, n)
        def _(t):
            pos_copy(t).wait()

        own_columns.wait()
        column_copy().wait()
        rows = jnp.concatenate([grad_rows[0], grad_rows[1]], axis=0)
        batch = 4

        @pl.loop(1, q + 1)
        def _(step):
            first = lax.rem(c + step, q) * batch
            at = jnp.concatenate([pos_all[first + i] for i in range(batch)], axis=1)
            hot = jnp.where(spot == at, 1.0, 0.0).astype(BF16)
            block = lax.dot_general(hot, rows, TN, preferred_element_type=F32).astype(BF16)
            for i in range(batch):
                picked[first + i] = block[i * most : (i + 1) * most]

                @pl.when(first + i != dp)
                def _():
                    grad_send(first + i).start()

                @pl.when(first + i == dp)
                def _():
                    slots[first + i] = block[i * most : (i + 1) * most]

    count = slide_count[:, 0:1]
    own = pl.multiple_of(seq * nearby, nearby)
    far_own = pl.multiple_of((1 - seq) * nearby, nearby)

    def natural_of(index, shift):
        return (index % part) * DILATION_STEP + lax.rem(index // part + 2 * shift, DILATION_STEP)

    def regroup():
        @pl.loop(0, n)
        def _(t):
            forward(t).wait_recv()

        positions = jnp.concatenate([pos_all[i] for i in range(n)], axis=1)
        inside = spot % nearby
        at_spot = spot - inside + natural_of(inside, seq)
        hot_perm = jnp.where(at_spot == positions, 1.0, 0.0).astype(BF16)
        own_spot = lax.broadcasted_iota(jnp.int32, (nearby, 1), 0) + seq * nearby
        hot_own = jnp.where(own_spot == positions, 1.0, 0.0).astype(BF16)
        blocks = [emb_all[i].reshape(slot_rows, width) for i in range(2)]
        for i in range(2):
            emb_ref[:, i * width : (i + 1) * width] = jnp.dot(
                hot_own, blocks[i], preferred_element_type=F32
            ).astype(BF16)
        for block in range(2):
            at = slice(block * nearby, (block + 1) * nearby)
            row = jnp.concatenate(
                [jnp.dot(hot_perm[at], blocks[i], preferred_element_type=F32) for i in range(2)],
                axis=-1,
            )
            center = jnp.mean(row, axis=-1, keepdims=True)
            spread = jnp.mean(jnp.square(row - center), axis=-1, keepdims=True)
            normed[at, :] = (
                (row - center) * lax.rsqrt(spread + EPSILON) * gain[...][None, :]
            ).astype(BF16)

    rows_each = src.shape[3]
    cut = rows_each * SPLIT // 8
    at_a, at_b = pl.ds(0, cut), pl.ds(cut, rows_each - cut)
    both = pl.ds(0, 2)

    def to_sibling(part, y, k):
        at = (at_a, at_b)[part]
        return remote(
            src.at[1 - a, y, k, at],
            pair.at[y, k, at],
            s1.at[part, y, k],
            r1.at[part, y, k],
            sibling,
        )

    def turn(j):
        return lax.select(c < q // 2, q - 1 - j, j)

    def send_pairs(y):
        for part in range(2):
            for j in range(q):
                to_sibling(part, y, turn(j)).start()

    def to_across(k):
        return remote(stage_y.at[k], cross.at[k], s2.at[k], r2.at[k], across)

    def to_z(part, d, k):
        stage, land = ((stage_za, in_za), (stage_zb, in_zb))[part]
        peer = lax.rem(dp + n + 4 - 8 * d, n)
        return remote(stage.at[k], land.at[d, k], s3.at[part, k], r3.at[part, d, k], (peer, seq))

    def to_across_b():
        return remote(stage_yb, cross_b, s4.at[0], r4.at[0], across)

    def block_of(part, k):
        return out.at[a, b, k, at_a] if part == 0 else out.at[a, both, k, at_b]

    def go_up(part, hop, k):
        block = block_of(part, k)
        device = (lax.rem(dp + 4, n), seq)
        return remote(block, block, gus.at[part, hop], gur.at[part, hop], device)

    def go_down(part, hop, k):
        block = block_of(part, k)
        device = (lax.rem(dp + n - 4, n), seq)
        return remote(block, block, gds.at[part, hop], gdr.at[part, hop], device)

    def go_across(k):
        block = out.at[a, b, k, at_a]
        return remote(block, block, gys.at[k], gyr.at[k], across)

    def go_across_b():
        block = out.at[a, b, c, at_b]
        return remote(block, block, gbs.at[0], gbr.at[0], across)

    def go_sibling(side, k):
        block = out.at[a, b if side == 0 else 1 - b, k, at_a]
        return remote(block, block, gcs.at[side, k], gcr.at[side, k], sibling)

    def go_sibling_b(k):
        block = out.at[a, both, k, at_b]
        return remote(block, block, gxs.at[k], gxr.at[k], sibling)

    def product():
        @pl.loop(0, n)
        def _(source):
            @pl.when(source != dp)
            def _():
                grad_recv(source).wait_recv()

        grads = slots[...].reshape(slot_rows, width)
        tile = q * rows_each

        @pl.loop(0, n // q)
        def _(step):
            core = lax.rem(1 - a + step // 2, 2)
            y = lax.rem(1 - b + step, 2)
            first = pl.multiple_of((core * 2 + y) * tile, tile)
            product = lax.dot_general(
                feats[:, pl.ds(first, tile)], grads, TN, preferred_element_type=F32
            ).astype(BF16)
            for i in range(q):
                src[core, y, i] = product[i * rows_each : (i + 1) * rows_each]

            @pl.when(step < 2)
            def _():
                send_pairs(y)

    def sum_y(j):
        k = turn(j)
        to_sibling(0, 1 - b, k).wait_recv()
        stage_y[k] = (
            src[a, 1 - b, k, at_a].astype(F32) + pair[1 - b, k, at_a].astype(F32)
        ).astype(BF16)
        to_across(k).start()

    def term_a(k):
        return (
            src[a, b, k, at_a].astype(F32)
            + pair[b, k, at_a].astype(F32)
            + cross[k].astype(F32)
        )

    def term_b(k):
        return src[a, both, k, at_b].astype(F32) + pair[both, k, at_b].astype(F32)

    def ready(part, k):
        if part == 0:
            to_sibling(0, b, k).wait_recv()
            to_across(k).wait_recv()
        else:
            to_sibling(1, 0, k).wait_recv()
            to_sibling(1, 1, k).wait_recv()

    def sum_z(part, j):
        k = turn(j)
        term, stage, land = ((term_a, stage_za, in_za), (term_b, stage_zb, in_zb))[part]
        ready(part, k)

        @pl.when(k > c)
        def _():
            @pl.when(c > 0)
            def _():
                to_z(part, 0, k).wait_recv()

            stage[k] = (term(k) + land[0, k].astype(F32)).astype(BF16)
            to_z(part, 0, k).start()

        @pl.when(k < c)
        def _():
            @pl.when(c < q - 1)
            def _():
                to_z(part, 1, k).wait_recv()

            stage[k] = (term(k) + land[1, k].astype(F32)).astype(BF16)
            to_z(part, 1, k).start()

    def own_in(part):
        @pl.when(c > 0)
        def _():
            to_z(part, 0, c).wait_recv()

        @pl.when(c < q - 1)
        def _():
            to_z(part, 1, c).wait_recv()

    def hand_on(part, k):
        if part == 0:
            go_across(k).start()
            go_sibling(0, k).start()
        else:
            go_sibling_b(k).start()

    def share(part):
        @pl.when(c < q - 1)
        def _():
            go_up(part, 1, c).start()

        @pl.when(c > 0)
        def _():
            go_down(part, 1, c).start()

        hand_on(part, c)

    def own_a():
        own_in(0)
        out[a, b, c, at_a] = (
            term_a(c) + in_za[0, c].astype(F32) + in_za[1, c].astype(F32)
        ).astype(BF16)
        share(0)

    def own_b():
        own_in(1)
        stage_yb[...] = (
            src[a, 1 - b, c, at_b].astype(F32)
            + pair[1 - b, c, at_b].astype(F32)
            + in_zb[0, c, 1 - b].astype(F32)
            + in_zb[1, c, 1 - b].astype(F32)
        ).astype(BF16)
        to_across_b().start()

    def whole_b():
        to_across_b().wait_recv()
        out[a, b, c, at_b] = (
            src[a, b, c, at_b].astype(F32)
            + pair[b, c, at_b].astype(F32)
            + in_zb[0, c, b].astype(F32)
            + in_zb[1, c, b].astype(F32)
            + cross_b[...].astype(F32)
        ).astype(BF16)
        go_across_b().start()

    def share_b():
        go_across_b().wait_recv()
        share(1)

    def result_hop(part, hop):
        below, above = c - hop, c + hop

        @pl.when(below >= 0)
        def _():
            go_up(part, hop, below).wait_recv()

            @pl.when(c < q - 1)
            def _():
                go_up(part, hop + 1, below).start()

            hand_on(part, below)

        @pl.when(above < q)
        def _():
            go_down(part, hop, above).wait_recv()

            @pl.when(c > 0)
            def _():
                go_down(part, hop + 1, above).start()

            hand_on(part, above)

    def result_over(j):
        k = lax.rem(c + j, q)
        go_across(k).wait_recv()
        go_sibling(1, k).start()

    def reduce_done():
        @pl.loop(0, q)
        def _(k):
            for y in range(2):
                for part in range(2):
                    to_sibling(part, y, k).wait_send()
                go_sibling(y, k).wait()
            to_across(k).wait_send()
            go_across(k).wait_send()
            go_sibling_b(k).wait()

            @pl.when(k != c)
            def _():
                for part in range(2):
                    to_z(part, 0, k).wait_send()

        to_across_b().wait_send()
        go_across_b().wait_send()
        for part in range(2):
            for hop in range(1, q):

                @pl.when((c - hop + 1 >= 0) & (c < q - 1))
                def _():
                    go_up(part, hop, c - hop + 1).wait_send()

                @pl.when((c + hop - 1 < q) & (c > 0))
                def _():
                    go_down(part, hop, c + hop - 1).wait_send()

    lane = lax.broadcasted_iota(jnp.int32, (1, nearby), 1)
    row_at = lax.broadcasted_iota(jnp.int32, (nearby, 1), 0)
    far_lane = lax.broadcasted_iota(jnp.int32, (1, part), 1)

    def project(which):
        cols = slice(which * width, (which + 1) * width)
        value = jnp.dot(normed[...], wts[:, cols], preferred_element_type=F32).astype(BF16)
        if which == 0:
            value = value * BF16(HEAD_WIDTH**-0.5)
        qkv[which] = value

    def attend_head(start, other, head):
        group = head % DILATION_STEP
        cols = slice(head * HEAD_WIDTH, (head + 1) * HEAD_WIDTH)
        low, high = group * part, (group + 1) * part
        key_ok = start + natural_of(lane, seq) < count
        query_ok = start + natural_of(row_at, seq) < count
        far_ok = (
            other + far_lane * DILATION_STEP + lax.rem(group + 2 * seq, DILATION_STEP) < count
        )
        here = pl.ds(start, nearby)
        there = pl.ds(pl.multiple_of(other + low, part), part)
        qh, kh, vh = (qkv[i, here, :][:, cols] for i in range(3))
        far_k, far_v = (qkv[i, there, :][:, cols] for i in (1, 2))
        scores = lax.dot_general(qh, kh, NT, preferred_element_type=F32)
        scores = jnp.where(key_ok, scores, NEGATIVE)
        maximum = jnp.max(scores, axis=-1, keepdims=True)
        far = lax.dot_general(qh[low:high], far_k, NT, preferred_element_type=F32)
        far = jnp.where(far_ok, far, NEGATIVE)
        far_max = jnp.maximum(maximum[low:high], jnp.max(far, axis=-1, keepdims=True))
        maximum = put_rows(maximum, far_max, low, high)
        weight = jnp.exp(scores - maximum)
        in_lane = (lane >= low) & (lane < high)
        twice = jnp.where(in_lane, weight[low:high] * 2.0, weight[low:high])
        weight = put_rows(weight, twice, low, high)
        far_weight = jnp.exp(far - far_max)
        total = jnp.sum(weight, axis=-1, keepdims=True)
        far_total = jnp.sum(far_weight, axis=-1, keepdims=True)
        total = put_rows(total, total[low:high] + far_total, low, high)
        gathered = jnp.dot(weight.astype(BF16), vh, preferred_element_type=F32)
        far_gathered = jnp.dot(far_weight.astype(BF16), far_v, preferred_element_type=F32)
        gathered = put_rows(gathered, gathered[low:high] + far_gathered, low, high)
        return jnp.where(query_ok, gathered / total, 0.0).astype(BF16)

    def ctx_copy(j):
        at = pl.ds(j * 128, 128)
        return remote(ctx_send.at[:, at], ctx_peer.at[:, at], ks.at[j], kr.at[j], x_peer)

    pairs = width // 128

    def heads(mine, j):
        start, other = (own, far_own) if mine else (far_own, own)
        block = jnp.concatenate(
            [attend_head(start, other, 2 * j + i) for i in range(2)], axis=-1
        )
        at = pl.ds(j * 128, 128)
        if mine:
            ctx_own[:, at] = block
        else:
            ctx_send[:, at] = block
            ctx_copy(j).start()

    def finish_branch():
        for j in range(pairs):
            ctx_copy(j).wait()
        wx_copy().wait_recv()
        at_row = lax.broadcasted_iota(jnp.int32, (nearby, nearby), 0)
        at_lane = lax.broadcasted_iota(jnp.int32, (nearby, nearby), 1)
        ordered = []
        for shift, ref in ((seq, ctx_own), (1 - seq, ctx_peer)):
            back = jnp.where(at_row == natural_of(at_lane, shift), 1.0, 0.0).astype(BF16)
            ordered.append(jnp.dot(back, ref[...], preferred_element_type=F32).astype(BF16))
        for cols, weight in ((seq, wts.at[:, pl.ds(wide, width)]), (1 - seq, wts_x)):
            total = None
            for value, owner in zip(ordered, (seq, 1 - seq)):
                at = pl.ds(pl.multiple_of(owner * width, width), width)
                term = jnp.dot(value, weight[at, :], preferred_element_type=F32)
                total = term if total is None else total + term
            branch_ref[:, pl.ds(pl.multiple_of(cols * width, width), width)] = total.astype(BF16)

    do = functools.partial

    sums = [do(sum_y, 0), do(sum_y, 1), do(sum_z, 1, 0), do(sum_y, 2), do(sum_y, 3)]
    for j in range(1, q):
        sums += [do(sum_z, 1, j), do(sum_z, 0, j - 1)]
    sums += [own_b, do(sum_z, 0, q - 1), whole_b, own_a, share_b]
    for hop in range(1, q):
        sums += [do(result_hop, 0, hop), do(result_hop, 1, hop)]
    sums += [do(result_over, j) for j in range(q)]

    def merge(jobs, others, tail=2):
        mixed, taken = [], 0
        for i, job in enumerate(jobs):
            until = (i + 1) * len(others) // (len(jobs) + tail)
            mixed += [job] + others[taken:until]
            taken = until
        return mixed + others[taken:]
    steps = [first_sends, embed, emb_sends, grad_sends, w_start, do(emb_on, 1, n), regroup, do(w_hop, 1), product]
    steps += sums[0:5] + [do(w_hop, 2)]
    steps += sums[5:8] + [do(w_hop, 3)]
    steps += sums[8:10] + [w_side]
    sums = sums[10:]
    work = [w_gathered]
    work += [do(project, i) for i in range(3)]
    work += [do(heads, False, j) for j in range(pairs)]
    work += [do(heads, True, j) for j in range(pairs)]
    work += [finish_branch]

    steps += merge(work, sums, 2)
    for step in steps:
        step()

    @pl.loop(1, n)
    def _(t):
        emb_copy(t).wait_send()

    @pl.loop(0, n)
    def _(t):
        forward(t).wait_send()

        @pl.when(t != dp)
        def _():
            grad_send(t).wait_send()

    w_done()
    reduce_done()


def finish_kernel(emb, branch, summed, emb_out, branch_out, grad_out, wide, sems):
    copies = [
        pltpu.make_async_copy(emb, emb_out.at[0], sems.at[0]),
        pltpu.make_async_copy(branch, branch_out.at[0], sems.at[1]),
    ]
    for copy in copies:
        copy.start()
    size = summed.shape[0] // 4
    for i in range(4):
        at = pl.ds(i * size, size)
        wide[at, :] = summed[at, :].astype(F32)
        copies.append(pltpu.make_async_copy(wide.at[at], grad_out.at[at], sems.at[2 + i]))
        copies[-1].start()
    for copy in copies:
        copy.wait()


def finish(emb, branch, summed):
    return pl.pallas_call(
        finish_kernel,
        out_shape=(
            jax.ShapeDtypeStruct((1, *emb.shape), BF16),
            jax.ShapeDtypeStruct((1, *branch.shape), BF16),
            jax.ShapeDtypeStruct(summed.shape, F32),
        ),
        in_specs=[VM] * 3,
        out_specs=(HBM,) * 3,
        scratch_shapes=[pltpu.VMEM(summed.shape, F32), DMA((6,))],
        compiler_params=pltpu.CompilerParams(vmem_limit_bytes=16 * 1024 * 1024),
        cost_estimate=pl.CostEstimate(flops=0, bytes_accessed=6_000_000, transcendentals=0),
    )(emb, branch, summed)


def in_hbm(operand):
    return pltpu.with_memory_space_constraint(operand, pltpu.HBM)


def fused(tile_feats, tile_pos, slide_count, w_proj, emb_grad, ln_gain, w_qkv, w_out):
    n = lax.axis_size("dp")
    slot_rows, features = tile_feats.shape
    nearby = emb_grad.shape[1]
    most = slot_rows // n
    width = w_proj.shape[1]
    q = n // 4
    shape = (2, 2, q, features // n, width)
    cut = features // n * SPLIT // 8
    part_a = (q, cut, width)
    part_b = (q, 2, features // n - cut, width)
    scratch = [
        pltpu.VMEM(tile_feats.shape, BF16),
        pltpu.VMEM(w_proj.shape, BF16),
        pltpu.VMEM(tile_pos.shape, jnp.int32),
        pltpu.VMEM(ln_gain.shape, F32),
        pltpu.VMEM(w_qkv.shape, BF16),
        pltpu.VMEM(w_out.shape, BF16),
        pltpu.VMEM((slot_rows, width), BF16),
        pltpu.VMEM((n, 1, most), jnp.int32),
        pltpu.VMEM((n, 1, most), jnp.int32),
        pltpu.VMEM((2, n, most, width), BF16),
        pltpu.VMEM((2, nearby, width), BF16),
        pltpu.VMEM((n, most, width), BF16),
        pltpu.VMEM((n, most, width), BF16),
        pltpu.VMEM((D, 4 * width), BF16),
        pltpu.VMEM((D, width), BF16),
        pltpu.VMEM((2 * nearby, D), BF16),
        pltpu.VMEM((3, 2 * nearby, width), BF16),
        pltpu.VMEM((nearby, width), BF16),
        pltpu.VMEM((nearby, width), BF16),
        pltpu.VMEM((nearby, width), BF16),
        pltpu.VMEM(shape, BF16),
        pltpu.VMEM(shape[1:], BF16),
        pltpu.VMEM(part_a, BF16),
        pltpu.VMEM(part_a, BF16),
        pltpu.VMEM(part_a, BF16),
        pltpu.VMEM(part_b, BF16),
        pltpu.VMEM((2, *part_a), BF16),
        pltpu.VMEM((2, *part_b), BF16),
        pltpu.VMEM(part_b[2:], BF16),
        pltpu.VMEM(part_b[2:], BF16),
        DMA((7,)),
    ]
    scratch += [DMA((1,))] * 2
    scratch += [DMA((n,))] * 8
    scratch += [DMA((q + 1,))] * 4
    scratch += [DMA((q,))] * 2
    scratch += [DMA((2, q))] * 2
    scratch += [DMA((1,))] * 2
    scratch += [DMA((width // 128,))] * 2
    scratch += [DMA((2, 2, q))] * 2
    scratch += [DMA((q,))] * 2
    scratch += [DMA((2, q)), DMA((2, 2, q))]
    scratch += [DMA((1,))] * 2
    scratch += [DMA((2, q + 1))] * 4
    scratch += [DMA((q,))] * 2
    scratch += [DMA((1,))] * 2
    scratch += [DMA((2, q))] * 2
    scratch += [DMA((q,))] * 2
    row = jax.ShapeDtypeStruct((nearby, D), BF16)
    emb, branch, summed = pl.pallas_call(
        functools.partial(fused_kernel, n),
        out_shape=(row, row, jax.ShapeDtypeStruct(shape, BF16)),
        in_specs=[HBM, HBM, VM, HBM, HBM, HBM, HBM, HBM],
        out_specs=(VM, VM, VM),
        scratch_shapes=scratch,
        compiler_params=pltpu.CompilerParams(
            collective_id=5, has_side_effects=True, vmem_limit_bytes=48 * 1024 * 1024
        ),
        cost_estimate=pl.CostEstimate(
            flops=5_000_000_000, bytes_accessed=10_000_000, transcendentals=1_000_000
        ),
    )(
        in_hbm(tile_feats),
        in_hbm(tile_pos),
        jnp.broadcast_to(slide_count[:, None], (1, 128)),
        in_hbm(w_proj),
        in_hbm(emb_grad),
        in_hbm(ln_gain),
        in_hbm(w_qkv),
        in_hbm(w_out),
    )
    return finish(emb, branch, summed.reshape(features, width))


def solution(mesh):
    in_specs = (
        P("dp", None),
        P("dp", None),
        P("dp"),
        P(None, "seq"),
        P("dp", "seq", None),
        P(),
        P("dp", None),
        P("dp", None),
    )
    out_specs = (P("dp", "seq", None), P("dp", "seq", None), P(None, "seq"))
    one_kernel = mesh.shape["dp"] == 16 and mesh.shape["seq"] == 2
    body = fused if one_kernel else local
    return jax.shard_map(body, mesh=mesh, in_specs=in_specs, out_specs=out_specs, check_vma=False)
```

```python
import functools

import jax
import jax.numpy as jnp
from jax import lax
from jax.experimental import pallas as pl
from jax.experimental.pallas import tpu as pltpu
from jax.sharding import PartitionSpec as P

D = 768
HEAD_COUNT = 12
HEAD_WIDTH = 64
DILATION_STEP = 4
NEGATIVE = -1e30
EPSILON = 1e-05
STEP_HEADS = 4

F32 = jnp.float32
BF16 = jnp.bfloat16
MESH = pl.DeviceIdType.MESH


def greet(dp_peers, seq_peers):
    barrier = pltpu.get_barrier_semaphore()
    dp_count, seq_count = lax.axis_size("dp"), lax.axis_size("seq")
    dp, seq = lax.axis_index("dp"), lax.axis_index("seq")
    if dp_peers:

        @pl.loop(1, dp_count)
        def _(t):
            pl.semaphore_signal(
                barrier, device_id=(lax.rem(dp + t, dp_count), seq), device_id_type=MESH
            )

    if seq_peers:

        @pl.loop(1, seq_count)
        def _(t):
            pl.semaphore_signal(
                barrier, device_id=(dp, lax.rem(seq + t, seq_count)), device_id_type=MESH
            )

    pl.semaphore_wait(
        barrier, (dp_count - 1 if dp_peers else 0) + (seq_count - 1 if seq_peers else 0)
    )


def remote(src, dst, send, recv, device):
    return pltpu.make_async_remote_copy(
        src_ref=src,
        dst_ref=dst,
        send_sem=send,
        recv_sem=recv,
        device_id=device,
        device_id_type=MESH,
    )


def dispatch_kernel(
    n, seq_count, pos, grad, emb, pos_out, emb_out, grad_out, grad_rows, picked, *sems
):
    ps, pr, xs, xr, es, er, gs, gr, fs, fr = sems
    dp, seq = lax.axis_index("dp"), lax.axis_index("seq")
    most = pos.shape[2]
    nearby, width = grad.shape[1:]
    greet(True, True)

    def column_copy(t):
        peer = lax.rem(seq + t, seq_count)
        return remote(grad.at[peer], grad_rows.at[seq], xs.at[t], xr.at[t], (dp, peer))

    def pos_copy(t):
        peer = lax.rem(dp + t, n)
        return remote(pos.at[peer], pos_out.at[dp], ps.at[t], pr.at[t], (peer, seq))

    def emb_copy(t):
        peer = lax.rem(dp + t, n)
        return remote(emb.at[peer], emb_out.at[seq, dp], es.at[t], er.at[t], (peer, seq))

    def grad_copy(t):
        peer = lax.rem(dp + t, n)
        return remote(picked.at[peer], grad_out.at[dp], gs.at[t], gr.at[t], (peer, seq))

    def forward(k, t):
        source = lax.rem(dp - t + n, n)
        peer = lax.rem(seq + k, seq_count)
        block = emb_out.at[seq, source]
        return remote(block, block, fs.at[k, t], fr.at[k, t], (dp, peer))

    @pl.loop(1, seq_count)
    def _(t):
        column_copy(t).start()

    @pl.loop(1, n)
    def _(t):
        pos_copy(t).start()

    @pl.loop(1, n)
    def _(t):
        emb_copy(t).start()

    pos_out[dp] = pos[dp]
    grad_rows[seq] = grad[seq]
    emb_out[seq, dp] = emb[dp]

    @pl.loop(1, n)
    def _(t):
        pos_copy(t).wait()

    @pl.loop(1, seq_count)
    def _(t):
        column_copy(t).wait()

    rows = jnp.concatenate([grad_rows[i] for i in range(seq_count)], axis=0)
    spot = lax.broadcasted_iota(jnp.int32, (nearby * seq_count, 1), 0)
    batch = 4
    for first in range(0, n, batch):
        at = jnp.concatenate([pos_out[first + i] for i in range(batch)], axis=1)
        hot = jnp.where(spot == at, 1.0, 0.0).astype(BF16)
        block = lax.dot_general(
            hot, rows, (((0,), (0,)), ((), ())), preferred_element_type=F32
        ).astype(BF16)
        for i in range(batch):
            picked[first + i] = block[i * most : (i + 1) * most]

    @pl.loop(1, n)
    def _(t):
        grad_copy(t).start()

    grad_out[dp] = picked[dp]
    for k in range(1, seq_count):
        forward(k, 0).start()

    @pl.loop(1, n)
    def _(t):
        emb_copy(t).wait_recv()
        for k in range(1, seq_count):
            forward(k, t).start()

    @pl.loop(1, n)
    def _(t):
        emb_copy(t).wait_send()
        grad_copy(t).wait()

    @pl.loop(0, n)
    def _(t):
        for k in range(1, seq_count):
            forward(k, t).wait()


def reduce_kernel(n, feats, slots, out, src, pair, cross, stage_b, stage_c, arrive, *sems):
    s1, r1, s2, r2, s3, r3, s4, r4, s5, r5, s6, r6 = sems
    dp, seq = lax.axis_index("dp"), lax.axis_index("seq")
    q = n // 4
    a, b, c = lax.rem(dp, 2), lax.rem(dp // 2, 2), dp // 4
    sibling = (dp + 1 - 2 * a, seq)
    across = (dp + 2 - 4 * b, seq)
    barrier = pltpu.get_barrier_semaphore()
    pl.semaphore_signal(barrier, device_id=sibling, device_id_type=MESH)
    pl.semaphore_signal(barrier, device_id=across, device_id_type=MESH)

    def ahead(t):
        return lax.rem(c + t, q)

    def behind(t):
        return lax.rem(c - t + q, q)

    def along(t):
        return (ahead(t) * 4 + b * 2 + a, seq)

    @pl.loop(1, q)
    def _(t):
        pl.semaphore_signal(barrier, device_id=along(t), device_id_type=MESH)

    rows = src.shape[3]
    tile = 512
    for first in range(0, n * rows, tile):
        product = lax.dot_general(
            feats[:, first : first + tile],
            slots[...],
            (((0,), (0,)), ((), ())),
            preferred_element_type=F32,
        ).astype(BF16)
        for i in range(tile // rows):
            k = first // rows + i
            src[k // (2 * q), k // q % 2, k % q] = product[i * rows : (i + 1) * rows]

    pl.semaphore_wait(barrier, q + 1)

    def side(i):
        return 1 - b if i == 0 else b

    def to_sibling(i, t):
        return remote(
            src.at[1 - a, side(i), ahead(t)], pair.at[i, t], s1.at[i, t], r1.at[i, t], sibling
        )

    def to_across(t):
        return remote(stage_b.at[t], cross.at[t], s2.at[t], r2.at[t], across)

    def to_owner(t):
        return remote(stage_c.at[t], arrive.at[t], s3.at[t], r3.at[t], along(t))

    def result_along(t):
        block = out.at[a, b, c]
        return remote(block, block, s4.at[t], r4.at[t], along(t))

    def result_across(t):
        block = out.at[a, b, behind(t)]
        return remote(block, block, s5.at[t], r5.at[t], across)

    def result_sibling(i, t):
        block = out.at[a, side(i), behind(t)]
        return remote(block, block, s6.at[i, t], r6.at[i, t], sibling)

    for i in (0, 1):

        @pl.loop(1, q + 1)
        def _(t):
            to_sibling(i, lax.rem(t, q)).start()

    @pl.loop(1, q + 1)
    def _(step):
        t = lax.rem(step, q)
        to_sibling(0, t).wait_recv()
        stage_b[t] = (src[a, 1 - b, ahead(t)].astype(F32) + pair[0, t].astype(F32)).astype(BF16)
        to_across(t).start()

    @pl.loop(1, q + 1)
    def _(step):
        t = lax.rem(step, q)
        to_sibling(1, t).wait_recv()
        to_across(t).wait_recv()
        stage_c[t] = (
            src[a, b, ahead(t)].astype(F32) + pair[1, t].astype(F32) + cross[t].astype(F32)
        ).astype(BF16)

        @pl.when(step < q)
        def _():
            to_owner(t).start()

    total = stage_c[0].astype(F32)
    for t in range(1, q):
        to_owner(t).wait_recv()
        total = total + arrive[t].astype(F32)
    out[a, b, c] = total.astype(BF16)

    @pl.loop(1, q)
    def _(t):
        result_along(t).start()

    result_across(0).start()
    result_sibling(1, 0).start()

    @pl.loop(1, q)
    def _(t):
        result_along(t).wait_recv()
        result_across(t).start()
        result_sibling(1, t).start()

    @pl.loop(0, q)
    def _(t):
        result_across(t).wait_recv()
        result_sibling(0, t).start()

    @pl.loop(1, q)
    def _(t):
        to_owner(t).wait_send()
        result_along(t).wait_send()

    for i in (0, 1):

        @pl.loop(0, q)
        def _(t):
            to_sibling(i, t).wait_send()
            result_sibling(i, t).wait()

    @pl.loop(0, q)
    def _(t):
        to_across(t).wait_send()
        result_across(t).wait_send()


VM = pl.BlockSpec(memory_space=pltpu.VMEM)
DMA = pltpu.SemaphoreType.DMA


def exchange(kernel, ident, outs, scratch, *operands):
    return pl.pallas_call(
        kernel,
        out_shape=tuple(jax.ShapeDtypeStruct(shape, kind) for shape, kind in outs),
        in_specs=[VM] * len(operands),
        out_specs=tuple([VM] * len(outs)),
        scratch_shapes=scratch,
        compiler_params=pltpu.CompilerParams(
            collective_id=ident, has_side_effects=True, vmem_limit_bytes=32 * 1024 * 1024
        ),
        cost_estimate=pl.CostEstimate(
            flops=10_000_000_000, bytes_accessed=10_000_000, transcendentals=0
        ),
    )(*operands)


def put_rows(whole, rows, low, high):
    pieces = [whole[:low]] if low else []
    pieces.append(rows)
    if high < whole.shape[0]:
        pieces.append(whole[high:])
    return jnp.concatenate(pieces, axis=0)


def attention_kernel(
    seq_count,
    nearby,
    meta_ref,
    rows_ref,
    gain_ref,
    wq_ref,
    wk_ref,
    wv_ref,
    wo_ref,
    emb_ref,
    branch_ref,
    normed,
    context,
):
    step = pl.program_id(0)
    me = meta_ref[0]
    count = meta_ref[1]
    part = nearby // DILATION_STEP
    own = pl.multiple_of(me * nearby, nearby)

    @pl.when(step == 0)
    def _():
        for block in range(seq_count):
            at = slice(block * nearby, (block + 1) * nearby)
            wide = jnp.concatenate(
                [rows_ref[c, at, :] for c in range(seq_count)], axis=-1
            ).astype(F32)
            center = jnp.mean(wide, axis=-1, keepdims=True)
            spread = jnp.mean(jnp.square(wide - center), axis=-1, keepdims=True)
            normed[at, :] = (
                (wide - center) * lax.rsqrt(spread + EPSILON) * gain_ref[...]
            ).astype(BF16)

    mine = normed[pl.ds(own, nearby), :]
    query = jnp.dot(mine, wq_ref[...], preferred_element_type=F32).astype(BF16)
    query = query * BF16(HEAD_WIDTH**-0.5)
    key = jnp.dot(mine, wk_ref[...], preferred_element_type=F32).astype(BF16)
    value = jnp.dot(mine, wv_ref[...], preferred_element_type=F32).astype(BF16)
    far_keys, far_values = [], []
    for other in range(1, seq_count):
        block = lax.rem(me + other, seq_count)
        start = pl.multiple_of(block * nearby, nearby)
        theirs = normed[pl.ds(start, nearby), :]
        far_keys.append(jnp.dot(theirs, wk_ref[...], preferred_element_type=F32).astype(BF16))
        far_values.append(jnp.dot(theirs, wv_ref[...], preferred_element_type=F32).astype(BF16))

    lane = lax.broadcasted_iota(jnp.int32, (1, nearby), 1)
    key_ok = own + (lane % part) * DILATION_STEP + lane // part < count
    row = lax.broadcasted_iota(jnp.int32, (nearby, 1), 0)
    query_ok = own + (row % part) * DILATION_STEP + row // part < count
    far_lane = lax.broadcasted_iota(jnp.int32, (1, part * (seq_count - 1)), 1)
    far_block = lax.rem(me + 1 + far_lane // part, seq_count)
    far_spot = far_block * nearby + far_lane % part * DILATION_STEP
    dims = (((1,), (1,)), ((), ()))
    outs = []
    for head in range(STEP_HEADS):
        shift = head % DILATION_STEP
        cols = slice(head * HEAD_WIDTH, (head + 1) * HEAD_WIDTH)
        low, high = shift * part, (shift + 1) * part
        q, k, v = query[:, cols], key[:, cols], value[:, cols]
        scores = lax.dot_general(q, k, dims, preferred_element_type=F32)
        scores = jnp.where(key_ok, scores, NEGATIVE)
        maximum = jnp.max(scores, axis=-1, keepdims=True)
        far_k = jnp.concatenate([x[low:high, cols] for x in far_keys], axis=0)
        far_v = jnp.concatenate([x[low:high, cols] for x in far_values], axis=0)
        far_ok = far_spot + shift < count
        far = lax.dot_general(q[low:high], far_k, dims, preferred_element_type=F32)
        far = jnp.where(far_ok, far, NEGATIVE)
        far_max = jnp.maximum(maximum[low:high], jnp.max(far, axis=-1, keepdims=True))
        maximum = put_rows(maximum, far_max, low, high)
        weight = jnp.exp(scores - maximum)
        in_lane = (lane >= low) & (lane < high)
        twice = jnp.where(in_lane, weight[low:high] * 2.0, weight[low:high])
        weight = put_rows(weight, twice, low, high)
        far_weight = jnp.exp(far - far_max)
        total = jnp.sum(weight, axis=-1, keepdims=True)
        far_total = jnp.sum(far_weight, axis=-1, keepdims=True)
        total = put_rows(total, total[low:high] + far_total, low, high)
        gathered = jnp.dot(weight.astype(BF16), v, preferred_element_type=F32)
        far_gathered = jnp.dot(far_weight.astype(BF16), far_v, preferred_element_type=F32)
        gathered = put_rows(gathered, gathered[low:high] + far_gathered, low, high)
        outs.append(jnp.where(query_ok, gathered / total, 0.0).astype(BF16))
    context[step] = jnp.concatenate(outs, axis=-1)

    @pl.when(step == pl.num_programs(0) - 1)
    def _():
        at_row = lax.broadcasted_iota(jnp.int32, (nearby, nearby), 0)
        at_lane = lax.broadcasted_iota(jnp.int32, (nearby, nearby), 1)
        natural = (at_lane % part) * DILATION_STEP + at_lane // part
        back = jnp.where(at_row == natural, 1.0, 0.0).astype(BF16)
        ordered = jnp.concatenate(
            [rows_ref[c, pl.ds(own, nearby), :] for c in range(seq_count)], axis=-1
        )
        emb_ref[...] = jnp.dot(back, ordered, preferred_element_type=F32).astype(BF16)
        whole = jnp.concatenate(
            [context[i] for i in range(HEAD_COUNT // STEP_HEADS)], axis=-1
        )
        whole = jnp.dot(back, whole, preferred_element_type=F32).astype(BF16)
        branch_ref[...] = jnp.dot(whole, wo_ref[...], preferred_element_type=F32).astype(BF16)


def attend(meta, rows, gain, weights, seq_count, nearby):
    width = STEP_HEADS * HEAD_WIDTH
    steps = HEAD_COUNT // STEP_HEADS
    slide_len = rows.shape[1]
    full = lambda *shape: pl.BlockSpec(shape, lambda i: (0,) * len(shape))
    out = jax.ShapeDtypeStruct((nearby, D), BF16)
    return pl.pallas_call(
        functools.partial(attention_kernel, seq_count, nearby),
        out_shape=(out, out),
        grid=(steps,),
        in_specs=[
            pl.BlockSpec(memory_space=pltpu.SMEM),
            full(*rows.shape),
            full(1, D),
            pl.BlockSpec((D, width), lambda i: (0, i)),
            pl.BlockSpec((D, width), lambda i: (0, steps + i)),
            pl.BlockSpec((D, width), lambda i: (0, 2 * steps + i)),
            pl.BlockSpec((D, D), lambda i: (0, 3)),
        ],
        out_specs=(full(nearby, D), full(nearby, D)),
        scratch_shapes=[
            pltpu.VMEM((slide_len, D), BF16),
            pltpu.VMEM((steps, nearby, width), BF16),
        ],
        compiler_params=pltpu.CompilerParams(vmem_limit_bytes=60 * 1024 * 1024),
        cost_estimate=pl.CostEstimate(
            flops=20_000_000_000, bytes_accessed=20_000_000, transcendentals=1_000_000
        ),
    )(meta, rows, gain, weights, weights, weights, weights)


def local(tile_feats, tile_pos, slide_count, w_proj, emb_grad, ln_gain, w_qkv, w_out):
    seq_count = lax.axis_size("seq")
    n = lax.axis_size("dp")
    seq_index = lax.axis_index("seq")
    slot_rows = tile_feats.shape[0]
    nearby = emb_grad.shape[1]
    slide_len = nearby * seq_count
    part = nearby // DILATION_STEP
    most = slot_rows // n
    width = w_proj.shape[1]
    weights = lax.all_gather(
        jnp.concatenate([w_qkv, w_out], axis=1), "dp", axis=0, tiled=True
    )
    emb_part = jnp.dot(tile_feats, w_proj, preferred_element_type=F32).astype(BF16)
    positions, arrived, slot_grad = exchange(
        functools.partial(dispatch_kernel, n, seq_count),
        1,
        [
            ((n, 1, most), jnp.int32),
            ((seq_count, n, most, width), BF16),
            ((n, most, width), BF16),
        ],
        [pltpu.VMEM((seq_count, nearby, width), BF16), pltpu.VMEM((n, most, width), BF16)]
        + [DMA((n,))] * 2
        + [DMA((seq_count,))] * 2
        + [DMA((n,))] * 4
        + [DMA((seq_count, n))] * 2,
        tile_pos.reshape(n, 1, most),
        emb_grad.reshape(nearby, seq_count, width).transpose(1, 0, 2),
        emb_part.reshape(n, most, width),
    )
    positions = positions.reshape(slot_rows)
    spot = jnp.arange(slide_len, dtype=jnp.int32)
    features = tile_feats.shape[1]
    quarter = n // 4
    shape = (2, 2, quarter, features // n, width)
    (summed,) = exchange(
        functools.partial(reduce_kernel, n),
        3,
        [(shape, BF16)],
        [pltpu.VMEM(shape, BF16), pltpu.VMEM(shape[1:], BF16)]
        + [pltpu.VMEM(shape[2:], BF16)] * 4
        + [DMA((2, quarter))] * 2
        + [DMA((quarter,))] * 8
        + [DMA((2, quarter))] * 2,
        tile_feats,
        slot_grad.reshape(slot_rows, width),
    )
    proj_grad = summed.reshape(features, width).astype(F32)

    inside = spot % nearby
    at_spot = spot - inside + (inside % part) * DILATION_STEP + inside // part
    hot_perm = (at_spot[:, None] == positions[None, :]).astype(BF16)
    rows = jnp.einsum(
        "ps,csw->cpw",
        hot_perm,
        arrived.reshape(seq_count, slot_rows, width),
        preferred_element_type=F32,
    ).astype(BF16)
    meta = jnp.stack([seq_index.astype(jnp.int32), slide_count[0]])
    local_emb, attn_branch = attend(
        meta, rows, ln_gain.reshape(1, D), weights, seq_count, nearby
    )
    return (local_emb[None], attn_branch[None], proj_grad)


SPLIT = 5
HBM = pl.BlockSpec(memory_space=pltpu.HBM)
NT = (((1,), (1,)), ((), ()))
TN = (((0,), (0,)), ((), ()))


def fused_kernel(
    n,
    feats_hbm,
    pos_hbm,
    slide_count,
    wproj_hbm,
    grad,
    gain_hbm,
    wqkv_hbm,
    wout_hbm,
    emb_ref,
    branch_ref,
    out,
    feats,
    wproj,
    pos,
    gain,
    wqkv,
    wout,
    emb,
    pos_in,
    pos_all,
    emb_all,
    grad_rows,
    picked,
    slots,
    wts,
    wts_x,
    normed,
    qkv,
    ctx_send,
    ctx_own,
    ctx_peer,
    src,
    pair,
    cross,
    stage_y,
    stage_za,
    stage_zb,
    in_za,
    in_zb,
    stage_yb,
    cross_b,
    local_sems,
    xs,
    xr,
    ps,
    pr,
    es,
    er,
    fs,
    fr,
    gs,
    gr,
    us,
    ur,
    ds_,
    dr,
    ys,
    yr,
    cs,
    cr,
    wxs,
    wxr,
    ks,
    kr,
    s1,
    r1,
    s2,
    r2,
    s3,
    r3,
    s4,
    r4,
    gus,
    gur,
    gds,
    gdr,
    gys,
    gyr,
    gbs,
    gbr,
    gcs,
    gcr,
    gxs,
    gxr,
):
    dp, seq = lax.axis_index("dp"), lax.axis_index("seq")
    q = n // 4
    a, b, c = lax.rem(dp, 2), lax.rem(dp // 2, 2), dp // 4
    x_peer = (dp, 1 - seq)
    sib_dp = dp + 1 - 2 * a
    y_dp = dp + 2 - 4 * b
    sibling, across = (sib_dp, seq), (y_dp, seq)
    most = pos_in.shape[2]
    slot_rows = feats.shape[0]
    nearby = grad.shape[1]
    width = wproj.shape[1]
    depth = wqkv.shape[0]
    part = nearby // DILATION_STEP
    inner = HEAD_COUNT * HEAD_WIDTH
    wide = 3 * width

    barrier = pltpu.get_barrier_semaphore()

    @pl.loop(1, n)
    def _(t):
        pl.semaphore_signal(barrier, device_id=(lax.rem(dp + t, n), seq), device_id_type=MESH)

    pl.semaphore_signal(barrier, device_id=x_peer, device_id_type=MESH)
    feats_copy = pltpu.make_async_copy(feats_hbm, feats, local_sems.at[0])
    wproj_copy = pltpu.make_async_copy(wproj_hbm, wproj, local_sems.at[1])
    pos_load = pltpu.make_async_copy(pos_hbm, pos, local_sems.at[3])
    gain_load = pltpu.make_async_copy(gain_hbm, gain, local_sems.at[4])
    wqkv_load = pltpu.make_async_copy(wqkv_hbm, wqkv, local_sems.at[5])
    wout_load = pltpu.make_async_copy(wout_hbm, wout, local_sems.at[6])
    pos_load.start()
    wqkv_load.start()
    wout_load.start()
    gain_load.start()
    wproj_copy.start()
    feats_copy.start()
    pos_load.wait()
    for i in range(n):
        pos_in[i] = pos[:, i * most : (i + 1) * most]
    wqkv_load.wait()
    wout_load.wait()
    gain_load.wait()
    mine_w = pl.ds(pl.multiple_of(dp * depth, 16), depth)
    half = pl.multiple_of(seq * width, width)
    for i in range(3):
        wts[mine_w, i * width : (i + 1) * width] = wqkv[
            :, pl.ds(pl.multiple_of(i * inner + half, 128), width)
        ]
    wts[mine_w, wide:] = wout[:, pl.ds(half, width)]
    pos_all[dp] = pos_in[dp]

    def column_copy():
        block = grad.at[0, :, pl.ds(pl.multiple_of((1 - seq) * width, 128), width)]
        return remote(block, grad_rows.at[seq], xs.at[0], xr.at[0], x_peer)

    own_columns = pltpu.make_async_copy(
        grad.at[0, :, pl.ds(half, width)], grad_rows.at[seq], local_sems.at[2]
    )
    own_columns.start()

    def pos_copy(t):
        peer = lax.rem(dp + t, n)
        return remote(pos_in.at[peer], pos_all.at[dp], ps.at[t], pr.at[t], (peer, seq))

    def emb_copy(t):
        peer = lax.rem(dp + t, n)
        return remote(
            emb.at[pl.ds(pl.multiple_of(peer * most, most), most)],
            emb_all.at[seq, dp],
            es.at[t],
            er.at[t],
            (peer, seq),
        )

    def forward(t):
        block = emb_all.at[seq, lax.rem(dp - t + n, n)]
        return remote(block, block, fs.at[t], fr.at[t], x_peer)

    def grad_send(peer):
        return remote(picked.at[peer], slots.at[dp], gs.at[peer], gr.at[dp], (peer, seq))

    def grad_recv(source):
        return remote(picked.at[source], slots.at[source], gs.at[source], gr.at[source], sibling)

    def rows_of(who):
        return pl.ds(pl.multiple_of(who * depth, 16), depth)

    def z_block(z):
        return wts.at[rows_of(z * 4 + b * 2 + a)]

    def up(hop, z):
        return remote(z_block(z), z_block(z), us.at[hop], ur.at[hop], (lax.rem(dp + 4, n), seq))

    def down(hop, z):
        return remote(z_block(z), z_block(z), ds_.at[hop], dr.at[hop], (lax.rem(dp + n - 4, n), seq))

    def y_copy(z, back=False):
        who = z * 4 + (1 - b if back else b) * 2 + a
        block = wts.at[rows_of(who)]
        return remote(block, block, ys.at[z], yr.at[z], across)

    def c_copy(side, z, back=False):
        y = b if side == 0 else 1 - b
        who = z * 4 + y * 2 + (1 - a if back else a)
        block = wts.at[rows_of(who)]
        return remote(block, block, cs.at[side, z], cr.at[side, z], sibling)

    def w_start():
        @pl.when(c < q - 1)
        def _():
            up(1, c).start()

        @pl.when(c > 0)
        def _():
            down(1, c).start()

        y_copy(c).start()
        c_copy(0, c).start()

    def w_hop(hop):
        below, above = c - hop, c + hop

        @pl.when(below >= 0)
        def _():
            up(hop, below).wait_recv()

            @pl.when(c < q - 1)
            def _():
                up(hop + 1, below).start()

            y_copy(below).start()
            c_copy(0, below).start()

        @pl.when(above < q)
        def _():
            down(hop, above).wait_recv()

            @pl.when(c > 0)
            def _():
                down(hop + 1, above).start()

            y_copy(above).start()
            c_copy(0, above).start()

    def w_side():
        @pl.loop(0, q)
        def _(t):
            z = lax.rem(c + t, q)
            y_copy(z, True).wait_recv()
            c_copy(1, z).start()

    def wx_copy():
        return remote(wts.at[:, pl.ds(wide, width)], wts_x, wxs.at[0], wxr.at[0], x_peer)

    def w_gathered():
        @pl.loop(0, q)
        def _(z):
            c_copy(0, z, True).wait_recv()
            c_copy(1, z, True).wait_recv()

        wx_copy().start()

    def w_done():
        for hop in range(1, q):

            @pl.when((c - hop + 1 >= 0) & (c < q - 1))
            def _():
                up(hop, c - hop + 1).wait_send()

            @pl.when((c + hop - 1 < q) & (c > 0))
            def _():
                down(hop, c + hop - 1).wait_send()

        @pl.loop(0, q)
        def _(z):
            y_copy(z).wait_send()
            c_copy(0, z).wait_send()
            c_copy(1, z).wait_send()

        wx_copy().wait_send()

    spot = lax.broadcasted_iota(jnp.int32, (2 * nearby, 1), 0)

    @pl.when(c == 0)
    def _():
        in_za[0] = jnp.zeros_like(in_za[0])
        in_zb[0] = jnp.zeros_like(in_zb[0])

    @pl.when(c == q - 1)
    def _():
        in_za[1] = jnp.zeros_like(in_za[1])
        in_zb[1] = jnp.zeros_like(in_zb[1])

    def first_sends():
        pl.semaphore_wait(barrier, n)
        column_copy().start()

        @pl.loop(1, n)
        def _(t):
            pos_copy(t).start()

    def embed():
        wproj_copy.wait()
        feats_copy.wait()
        group = n // 2

        @pl.loop(0, 2)
        def _(step):
            which = lax.rem(c * 2 // q + 1 + step, 2)
            at = pl.ds(pl.multiple_of(which * group * most, group * most), group * most)
            emb[at, :] = jnp.dot(feats[at, :], wproj[...], preferred_element_type=F32).astype(
                BF16
            )

            @pl.loop(0, group)
            def _(i):
                t = lax.rem(which * group + i - dp + n, n)

                @pl.when(t > 0)
                def _():
                    emb_copy(t).start()

    def emb_sends():
        emb_all[seq, dp] = emb[pl.ds(pl.multiple_of(dp * most, most), most), :]
        forward(0).start()

    def emb_on(low, high):
        @pl.loop(low, high)
        def _(t):
            emb_copy(t).wait_recv()
            forward(t).start()

    def grad_sends():
        @pl.loop(1, n)
        def _(t):
            pos_copy(t).wait()

        own_columns.wait()
        column_copy().wait()
        rows = jnp.concatenate([grad_rows[0], grad_rows[1]], axis=0)
        batch = 4

        @pl.loop(1, q + 1)
        def _(step):
            first = lax.rem(c + step, q) * batch
            at = jnp.concatenate([pos_all[first + i] for i in range(batch)], axis=1)
            hot = jnp.where(spot == at, 1.0, 0.0).astype(BF16)
            block = lax.dot_general(hot, rows, TN, preferred_element_type=F32).astype(BF16)
            for i in range(batch):
                picked[first + i] = block[i * most : (i + 1) * most]

                @pl.when(first + i != dp)
                def _():
                    grad_send(first + i).start()

                @pl.when(first + i == dp)
                def _():
                    slots[first + i] = block[i * most : (i + 1) * most]

    count = slide_count[:, 0:1]
    own = pl.multiple_of(seq * nearby, nearby)
    far_own = pl.multiple_of((1 - seq) * nearby, nearby)

    def natural_of(index, shift):
        return (index % part) * DILATION_STEP + lax.rem(index // part + 2 * shift, DILATION_STEP)

    def regroup():
        @pl.loop(0, n)
        def _(t):
            forward(t).wait_recv()

        positions = jnp.concatenate([pos_all[i] for i in range(n)], axis=1)
        inside = spot % nearby
        at_spot = spot - inside + natural_of(inside, seq)
        hot_perm = jnp.where(at_spot == positions, 1.0, 0.0).astype(BF16)
        own_spot = lax.broadcasted_iota(jnp.int32, (nearby, 1), 0) + seq * nearby
        hot_own = jnp.where(own_spot == positions, 1.0, 0.0).astype(BF16)
        blocks = [emb_all[i].reshape(slot_rows, width) for i in range(2)]
        for i in range(2):
            emb_ref[:, i * width : (i + 1) * width] = jnp.dot(
                hot_own, blocks[i], preferred_element_type=F32
            ).astype(BF16)
        for block in range(2):
            at = slice(block * nearby, (block + 1) * nearby)
            row = jnp.concatenate(
                [jnp.dot(hot_perm[at], blocks[i], preferred_element_type=F32) for i in range(2)],
                axis=-1,
            )
            center = jnp.mean(row, axis=-1, keepdims=True)
            spread = jnp.mean(jnp.square(row - center), axis=-1, keepdims=True)
            normed[at, :] = (
                (row - center) * lax.rsqrt(spread + EPSILON) * gain[...][None, :]
            ).astype(BF16)

    rows_each = src.shape[3]
    cut = rows_each * SPLIT // 8
    at_a, at_b = pl.ds(0, cut), pl.ds(cut, rows_each - cut)
    both = pl.ds(0, 2)

    def to_sibling(part, y, k):
        at = (at_a, at_b)[part]
        return remote(
            src.at[1 - a, y, k, at],
            pair.at[y, k, at],
            s1.at[part, y, k],
            r1.at[part, y, k],
            sibling,
        )

    def turn(j):
        return lax.select(c < q // 2, q - 1 - j, j)

    def send_pairs(y):
        for part in range(2):
            for j in range(q):
                to_sibling(part, y, turn(j)).start()

    def to_across(k):
        return remote(stage_y.at[k], cross.at[k], s2.at[k], r2.at[k], across)

    def to_z(part, d, k):
        stage, land = ((stage_za, in_za), (stage_zb, in_zb))[part]
        peer = lax.rem(dp + n + 4 - 8 * d, n)
        return remote(stage.at[k], land.at[d, k], s3.at[part, k], r3.at[part, d, k], (peer, seq))

    def to_across_b():
        return remote(stage_yb, cross_b, s4.at[0], r4.at[0], across)

    def block_of(part, k):
        return out.at[a, b, k, at_a] if part == 0 else out.at[a, both, k, at_b]

    def go_up(part, hop, k):
        block = block_of(part, k)
        device = (lax.rem(dp + 4, n), seq)
        return remote(block, block, gus.at[part, hop], gur.at[part, hop], device)

    def go_down(part, hop, k):
        block = block_of(part, k)
        device = (lax.rem(dp + n - 4, n), seq)
        return remote(block, block, gds.at[part, hop], gdr.at[part, hop], device)

    def go_across(k):
        block = out.at[a, b, k, at_a]
        return remote(block, block, gys.at[k], gyr.at[k], across)

    def go_across_b():
        block = out.at[a, b, c, at_b]
        return remote(block, block, gbs.at[0], gbr.at[0], across)

    def go_sibling(side, k):
        block = out.at[a, b if side == 0 else 1 - b, k, at_a]
        return remote(block, block, gcs.at[side, k], gcr.at[side, k], sibling)

    def go_sibling_b(k):
        block = out.at[a, both, k, at_b]
        return remote(block, block, gxs.at[k], gxr.at[k], sibling)

    def product():
        @pl.loop(0, n)
        def _(source):
            @pl.when(source != dp)
            def _():
                grad_recv(source).wait_recv()

        grads = slots[...].reshape(slot_rows, width)
        tile = q * rows_each

        @pl.loop(0, n // q)
        def _(step):
            core = lax.rem(1 - a + step // 2, 2)
            y = lax.rem(1 - b + step, 2)
            first = pl.multiple_of((core * 2 + y) * tile, tile)
            product = lax.dot_general(
                feats[:, pl.ds(first, tile)], grads, TN, preferred_element_type=F32
            ).astype(BF16)
            for i in range(q):
                src[core, y, i] = product[i * rows_each : (i + 1) * rows_each]

            @pl.when(step < 2)
            def _():
                send_pairs(y)

    def sum_y(j):
        k = turn(j)
        to_sibling(0, 1 - b, k).wait_recv()
        stage_y[k] = (
            src[a, 1 - b, k, at_a].astype(F32) + pair[1 - b, k, at_a].astype(F32)
        ).astype(BF16)
        to_across(k).start()

    def term_a(k):
        return (
            src[a, b, k, at_a].astype(F32)
            + pair[b, k, at_a].astype(F32)
            + cross[k].astype(F32)
        )

    def term_b(k):
        return src[a, both, k, at_b].astype(F32) + pair[both, k, at_b].astype(F32)

    def ready(part, k):
        if part == 0:
            to_sibling(0, b, k).wait_recv()
            to_across(k).wait_recv()
        else:
            to_sibling(1, 0, k).wait_recv()
            to_sibling(1, 1, k).wait_recv()

    def sum_z(part, j):
        k = turn(j)
        term, stage, land = ((term_a, stage_za, in_za), (term_b, stage_zb, in_zb))[part]
        ready(part, k)

        @pl.when(k > c)
        def _():
            @pl.when(c > 0)
            def _():
                to_z(part, 0, k).wait_recv()

            stage[k] = (term(k) + land[0, k].astype(F32)).astype(BF16)
            to_z(part, 0, k).start()

        @pl.when(k < c)
        def _():
            @pl.when(c < q - 1)
            def _():
                to_z(part, 1, k).wait_recv()

            stage[k] = (term(k) + land[1, k].astype(F32)).astype(BF16)
            to_z(part, 1, k).start()

    def own_in(part):
        @pl.when(c > 0)
        def _():
            to_z(part, 0, c).wait_recv()

        @pl.when(c < q - 1)
        def _():
            to_z(part, 1, c).wait_recv()

    def hand_on(part, k):
        if part == 0:
            go_across(k).start()
            go_sibling(0, k).start()
        else:
            go_sibling_b(k).start()

    def share(part):
        @pl.when(c < q - 1)
        def _():
            go_up(part, 1, c).start()

        @pl.when(c > 0)
        def _():
            go_down(part, 1, c).start()

        hand_on(part, c)

    def own_a():
        own_in(0)
        out[a, b, c, at_a] = (
            term_a(c) + in_za[0, c].astype(F32) + in_za[1, c].astype(F32)
        ).astype(BF16)
        share(0)

    def own_b():
        own_in(1)
        stage_yb[...] = (
            src[a, 1 - b, c, at_b].astype(F32)
            + pair[1 - b, c, at_b].astype(F32)
            + in_zb[0, c, 1 - b].astype(F32)
            + in_zb[1, c, 1 - b].astype(F32)
        ).astype(BF16)
        to_across_b().start()

    def whole_b():
        to_across_b().wait_recv()
        out[a, b, c, at_b] = (
            src[a, b, c, at_b].astype(F32)
            + pair[b, c, at_b].astype(F32)
            + in_zb[0, c, b].astype(F32)
            + in_zb[1, c, b].astype(F32)
            + cross_b[...].astype(F32)
        ).astype(BF16)
        go_across_b().start()

    def share_b():
        go_across_b().wait_recv()
        share(1)

    def result_hop(part, hop):
        below, above = c - hop, c + hop

        @pl.when(below >= 0)
        def _():
            go_up(part, hop, below).wait_recv()

            @pl.when(c < q - 1)
            def _():
                go_up(part, hop + 1, below).start()

            hand_on(part, below)

        @pl.when(above < q)
        def _():
            go_down(part, hop, above).wait_recv()

            @pl.when(c > 0)
            def _():
                go_down(part, hop + 1, above).start()

            hand_on(part, above)

    def result_over(j):
        k = lax.rem(c + j, q)
        go_across(k).wait_recv()
        go_sibling(1, k).start()

    def reduce_done():
        @pl.loop(0, q)
        def _(k):
            for y in range(2):
                for part in range(2):
                    to_sibling(part, y, k).wait_send()
                go_sibling(y, k).wait()
            to_across(k).wait_send()
            go_across(k).wait_send()
            go_sibling_b(k).wait()

            @pl.when(k != c)
            def _():
                for part in range(2):
                    to_z(part, 0, k).wait_send()

        to_across_b().wait_send()
        go_across_b().wait_send()
        for part in range(2):
            for hop in range(1, q):

                @pl.when((c - hop + 1 >= 0) & (c < q - 1))
                def _():
                    go_up(part, hop, c - hop + 1).wait_send()

                @pl.when((c + hop - 1 < q) & (c > 0))
                def _():
                    go_down(part, hop, c + hop - 1).wait_send()

    lane = lax.broadcasted_iota(jnp.int32, (1, nearby), 1)
    row_at = lax.broadcasted_iota(jnp.int32, (nearby, 1), 0)
    far_lane = lax.broadcasted_iota(jnp.int32, (1, part), 1)

    def project(which):
        cols = slice(which * width, (which + 1) * width)
        value = jnp.dot(normed[...], wts[:, cols], preferred_element_type=F32).astype(BF16)
        if which == 0:
            value = value * BF16(HEAD_WIDTH**-0.5)
        qkv[which] = value

    def attend_head(start, other, head):
        group = head % DILATION_STEP
        cols = slice(head * HEAD_WIDTH, (head + 1) * HEAD_WIDTH)
        low, high = group * part, (group + 1) * part
        key_ok = start + natural_of(lane, seq) < count
        query_ok = start + natural_of(row_at, seq) < count
        far_ok = (
            other + far_lane * DILATION_STEP + lax.rem(group + 2 * seq, DILATION_STEP) < count
        )
        here = pl.ds(start, nearby)
        there = pl.ds(pl.multiple_of(other + low, part), part)
        qh, kh, vh = (qkv[i, here, :][:, cols] for i in range(3))
        far_k, far_v = (qkv[i, there, :][:, cols] for i in (1, 2))
        scores = lax.dot_general(qh, kh, NT, preferred_element_type=F32)
        scores = jnp.where(key_ok, scores, NEGATIVE)
        maximum = jnp.max(scores, axis=-1, keepdims=True)
        far = lax.dot_general(qh[low:high], far_k, NT, preferred_element_type=F32)
        far = jnp.where(far_ok, far, NEGATIVE)
        far_max = jnp.maximum(maximum[low:high], jnp.max(far, axis=-1, keepdims=True))
        maximum = put_rows(maximum, far_max, low, high)
        weight = jnp.exp(scores - maximum)
        in_lane = (lane >= low) & (lane < high)
        twice = jnp.where(in_lane, weight[low:high] * 2.0, weight[low:high])
        weight = put_rows(weight, twice, low, high)
        far_weight = jnp.exp(far - far_max)
        total = jnp.sum(weight, axis=-1, keepdims=True)
        far_total = jnp.sum(far_weight, axis=-1, keepdims=True)
        total = put_rows(total, total[low:high] + far_total, low, high)
        gathered = jnp.dot(weight.astype(BF16), vh, preferred_element_type=F32)
        far_gathered = jnp.dot(far_weight.astype(BF16), far_v, preferred_element_type=F32)
        gathered = put_rows(gathered, gathered[low:high] + far_gathered, low, high)
        return jnp.where(query_ok, gathered / total, 0.0).astype(BF16)

    def ctx_copy(j):
        at = pl.ds(j * 128, 128)
        return remote(ctx_send.at[:, at], ctx_peer.at[:, at], ks.at[j], kr.at[j], x_peer)

    pairs = width // 128

    def heads(mine, j):
        start, other = (own, far_own) if mine else (far_own, own)
        block = jnp.concatenate(
            [attend_head(start, other, 2 * j + i) for i in range(2)], axis=-1
        )
        at = pl.ds(j * 128, 128)
        if mine:
            ctx_own[:, at] = block
        else:
            ctx_send[:, at] = block
            ctx_copy(j).start()

    def finish_branch():
        for j in range(pairs):
            ctx_copy(j).wait()
        wx_copy().wait_recv()
        at_row = lax.broadcasted_iota(jnp.int32, (nearby, nearby), 0)
        at_lane = lax.broadcasted_iota(jnp.int32, (nearby, nearby), 1)
        ordered = []
        for shift, ref in ((seq, ctx_own), (1 - seq, ctx_peer)):
            back = jnp.where(at_row == natural_of(at_lane, shift), 1.0, 0.0).astype(BF16)
            ordered.append(jnp.dot(back, ref[...], preferred_element_type=F32).astype(BF16))
        for cols, weight in ((seq, wts.at[:, pl.ds(wide, width)]), (1 - seq, wts_x)):
            total = None
            for value, owner in zip(ordered, (seq, 1 - seq)):
                at = pl.ds(pl.multiple_of(owner * width, width), width)
                term = jnp.dot(value, weight[at, :], preferred_element_type=F32)
                total = term if total is None else total + term
            branch_ref[:, pl.ds(pl.multiple_of(cols * width, width), width)] = total.astype(BF16)

    do = functools.partial

    sums = [do(sum_y, 0), do(sum_y, 1), do(sum_z, 1, 0), do(sum_y, 2), do(sum_y, 3)]
    for j in range(1, q):
        sums += [do(sum_z, 1, j), do(sum_z, 0, j - 1)]
    sums += [own_b, do(sum_z, 0, q - 1), whole_b, own_a, share_b]
    for hop in range(1, q):
        sums += [do(result_hop, 0, hop), do(result_hop, 1, hop)]
    sums += [do(result_over, j) for j in range(q)]

    def merge(jobs, others, tail=2):
        mixed, taken = [], 0
        for i, job in enumerate(jobs):
            until = (i + 1) * len(others) // (len(jobs) + tail)
            mixed += [job] + others[taken:until]
            taken = until
        return mixed + others[taken:]
    steps = [first_sends, embed, emb_sends, grad_sends, w_start, do(emb_on, 1, n), regroup, do(w_hop, 1), product]
    steps += sums[0:5] + [do(w_hop, 2)]
    steps += sums[5:8] + [do(w_hop, 3)]
    steps += sums[8:10] + [w_side]
    sums = sums[10:]
    work = [w_gathered]
    work += [do(project, i) for i in range(3)]
    work += [do(heads, False, j) for j in range(pairs)]
    work += [do(heads, True, j) for j in range(pairs)]
    work += [finish_branch]

    steps += merge(work, sums, 2)
    for step in steps:
        step()

    @pl.loop(1, n)
    def _(t):
        emb_copy(t).wait_send()

    @pl.loop(0, n)
    def _(t):
        forward(t).wait_send()

        @pl.when(t != dp)
        def _():
            grad_send(t).wait_send()

    w_done()
    reduce_done()


def finish_kernel(emb, branch, summed, emb_out, branch_out, grad_out, wide, sems):
    copies = [
        pltpu.make_async_copy(emb, emb_out.at[0], sems.at[0]),
        pltpu.make_async_copy(branch, branch_out.at[0], sems.at[1]),
    ]
    for copy in copies:
        copy.start()
    size = summed.shape[0] // 4
    for i in range(4):
        at = pl.ds(i * size, size)
        wide[at, :] = summed[at, :].astype(F32)
        copies.append(pltpu.make_async_copy(wide.at[at], grad_out.at[at], sems.at[2 + i]))
        copies[-1].start()
    for copy in copies:
        copy.wait()


def finish(emb, branch, summed):
    return pl.pallas_call(
        finish_kernel,
        out_shape=(
            jax.ShapeDtypeStruct((1, *emb.shape), BF16),
            jax.ShapeDtypeStruct((1, *branch.shape), BF16),
            jax.ShapeDtypeStruct(summed.shape, F32),
        ),
        in_specs=[VM] * 3,
        out_specs=(HBM,) * 3,
        scratch_shapes=[pltpu.VMEM(summed.shape, F32), DMA((6,))],
        compiler_params=pltpu.CompilerParams(vmem_limit_bytes=16 * 1024 * 1024),
        cost_estimate=pl.CostEstimate(flops=0, bytes_accessed=6_000_000, transcendentals=0),
    )(emb, branch, summed)


def in_hbm(operand):
    return pltpu.with_memory_space_constraint(operand, pltpu.HBM)


def fused(tile_feats, tile_pos, slide_count, w_proj, emb_grad, ln_gain, w_qkv, w_out):
    n = lax.axis_size("dp")
    slot_rows, features = tile_feats.shape
    nearby = emb_grad.shape[1]
    most = slot_rows // n
    width = w_proj.shape[1]
    q = n // 4
    shape = (2, 2, q, features // n, width)
    cut = features // n * SPLIT // 8
    part_a = (q, cut, width)
    part_b = (q, 2, features // n - cut, width)
    scratch = [
        pltpu.VMEM(tile_feats.shape, BF16),
        pltpu.VMEM(w_proj.shape, BF16),
        pltpu.VMEM(tile_pos.shape, jnp.int32),
        pltpu.VMEM(ln_gain.shape, F32),
        pltpu.VMEM(w_qkv.shape, BF16),
        pltpu.VMEM(w_out.shape, BF16),
        pltpu.VMEM((slot_rows, width), BF16),
        pltpu.VMEM((n, 1, most), jnp.int32),
        pltpu.VMEM((n, 1, most), jnp.int32),
        pltpu.VMEM((2, n, most, width), BF16),
        pltpu.VMEM((2, nearby, width), BF16),
        pltpu.VMEM((n, most, width), BF16),
        pltpu.VMEM((n, most, width), BF16),
        pltpu.VMEM((D, 4 * width), BF16),
        pltpu.VMEM((D, width), BF16),
        pltpu.VMEM((2 * nearby, D), BF16),
        pltpu.VMEM((3, 2 * nearby, width), BF16),
        pltpu.VMEM((nearby, width), BF16),
        pltpu.VMEM((nearby, width), BF16),
        pltpu.VMEM((nearby, width), BF16),
        pltpu.VMEM(shape, BF16),
        pltpu.VMEM(shape[1:], BF16),
        pltpu.VMEM(part_a, BF16),
        pltpu.VMEM(part_a, BF16),
        pltpu.VMEM(part_a, BF16),
        pltpu.VMEM(part_b, BF16),
        pltpu.VMEM((2, *part_a), BF16),
        pltpu.VMEM((2, *part_b), BF16),
        pltpu.VMEM(part_b[2:], BF16),
        pltpu.VMEM(part_b[2:], BF16),
        DMA((7,)),
    ]
    scratch += [DMA((1,))] * 2
    scratch += [DMA((n,))] * 8
    scratch += [DMA((q + 1,))] * 4
    scratch += [DMA((q,))] * 2
    scratch += [DMA((2, q))] * 2
    scratch += [DMA((1,))] * 2
    scratch += [DMA((width // 128,))] * 2
    scratch += [DMA((2, 2, q))] * 2
    scratch += [DMA((q,))] * 2
    scratch += [DMA((2, q)), DMA((2, 2, q))]
    scratch += [DMA((1,))] * 2
    scratch += [DMA((2, q + 1))] * 4
    scratch += [DMA((q,))] * 2
    scratch += [DMA((1,))] * 2
    scratch += [DMA((2, q))] * 2
    scratch += [DMA((q,))] * 2
    row = jax.ShapeDtypeStruct((nearby, D), BF16)
    emb, branch, summed = pl.pallas_call(
        functools.partial(fused_kernel, n),
        out_shape=(row, row, jax.ShapeDtypeStruct(shape, BF16)),
        in_specs=[HBM, HBM, VM, HBM, HBM, HBM, HBM, HBM],
        out_specs=(VM, VM, VM),
        scratch_shapes=scratch,
        compiler_params=pltpu.CompilerParams(
            collective_id=5, has_side_effects=True, vmem_limit_bytes=48 * 1024 * 1024
        ),
        cost_estimate=pl.CostEstimate(
            flops=5_000_000_000, bytes_accessed=10_000_000, transcendentals=1_000_000
        ),
    )(
        in_hbm(tile_feats),
        in_hbm(tile_pos),
        jnp.broadcast_to(slide_count[:, None], (1, 128)),
        in_hbm(w_proj),
        in_hbm(emb_grad),
        in_hbm(ln_gain),
        in_hbm(w_qkv),
        in_hbm(w_out),
    )
    return finish(emb, branch, summed.reshape(features, width))


def solution(mesh):
    in_specs = (
        P("dp", None),
        P("dp", None),
        P("dp"),
        P(None, "seq"),
        P("dp", "seq", None),
        P(),
        P("dp", None),
        P("dp", None),
    )
    out_specs = (P("dp", "seq", None), P("dp", "seq", None), P(None, "seq"))
    one_kernel = mesh.shape["dp"] == 16 and mesh.shape["seq"] == 2
    body = fused if one_kernel else local
    return jax.shard_map(body, mesh=mesh, in_specs=in_specs, out_specs=out_specs, check_vma=False)
```

```python
import functools

import jax
import jax.numpy as jnp
from jax import lax
from jax.experimental import pallas as pl
from jax.experimental.pallas import tpu as pltpu
from jax.sharding import PartitionSpec as P

D = 768
HEAD_COUNT = 12
HEAD_WIDTH = 64
DILATION_STEP = 4
NEGATIVE = -1e30
EPSILON = 1e-05
STEP_HEADS = 4

F32 = jnp.float32
BF16 = jnp.bfloat16
MESH = pl.DeviceIdType.MESH


def greet(dp_peers, seq_peers):
    barrier = pltpu.get_barrier_semaphore()
    dp_count, seq_count = lax.axis_size("dp"), lax.axis_size("seq")
    dp, seq = lax.axis_index("dp"), lax.axis_index("seq")
    if dp_peers:

        @pl.loop(1, dp_count)
        def _(t):
            pl.semaphore_signal(
                barrier, device_id=(lax.rem(dp + t, dp_count), seq), device_id_type=MESH
            )

    if seq_peers:

        @pl.loop(1, seq_count)
        def _(t):
            pl.semaphore_signal(
                barrier, device_id=(dp, lax.rem(seq + t, seq_count)), device_id_type=MESH
            )

    pl.semaphore_wait(
        barrier, (dp_count - 1 if dp_peers else 0) + (seq_count - 1 if seq_peers else 0)
    )


def remote(src, dst, send, recv, device):
    return pltpu.make_async_remote_copy(
        src_ref=src,
        dst_ref=dst,
        send_sem=send,
        recv_sem=recv,
        device_id=device,
        device_id_type=MESH,
    )


def dispatch_kernel(
    n, seq_count, pos, grad, emb, pos_out, emb_out, grad_out, grad_rows, picked, *sems
):
    ps, pr, xs, xr, es, er, gs, gr, fs, fr = sems
    dp, seq = lax.axis_index("dp"), lax.axis_index("seq")
    most = pos.shape[2]
    nearby, width = grad.shape[1:]
    greet(True, True)

    def column_copy(t):
        peer = lax.rem(seq + t, seq_count)
        return remote(grad.at[peer], grad_rows.at[seq], xs.at[t], xr.at[t], (dp, peer))

    def pos_copy(t):
        peer = lax.rem(dp + t, n)
        return remote(pos.at[peer], pos_out.at[dp], ps.at[t], pr.at[t], (peer, seq))

    def emb_copy(t):
        peer = lax.rem(dp + t, n)
        return remote(emb.at[peer], emb_out.at[seq, dp], es.at[t], er.at[t], (peer, seq))

    def grad_copy(t):
        peer = lax.rem(dp + t, n)
        return remote(picked.at[peer], grad_out.at[dp], gs.at[t], gr.at[t], (peer, seq))

    def forward(k, t):
        source = lax.rem(dp - t + n, n)
        peer = lax.rem(seq + k, seq_count)
        block = emb_out.at[seq, source]
        return remote(block, block, fs.at[k, t], fr.at[k, t], (dp, peer))

    @pl.loop(1, seq_count)
    def _(t):
        column_copy(t).start()

    @pl.loop(1, n)
    def _(t):
        pos_copy(t).start()

    @pl.loop(1, n)
    def _(t):
        emb_copy(t).start()

    pos_out[dp] = pos[dp]
    grad_rows[seq] = grad[seq]
    emb_out[seq, dp] = emb[dp]

    @pl.loop(1, n)
    def _(t):
        pos_copy(t).wait()

    @pl.loop(1, seq_count)
    def _(t):
        column_copy(t).wait()

    rows = jnp.concatenate([grad_rows[i] for i in range(seq_count)], axis=0)
    spot = lax.broadcasted_iota(jnp.int32, (nearby * seq_count, 1), 0)
    batch = 4
    for first in range(0, n, batch):
        at = jnp.concatenate([pos_out[first + i] for i in range(batch)], axis=1)
        hot = jnp.where(spot == at, 1.0, 0.0).astype(BF16)
        block = lax.dot_general(
            hot, rows, (((0,), (0,)), ((), ())), preferred_element_type=F32
        ).astype(BF16)
        for i in range(batch):
            picked[first + i] = block[i * most : (i + 1) * most]

    @pl.loop(1, n)
    def _(t):
        grad_copy(t).start()

    grad_out[dp] = picked[dp]
    for k in range(1, seq_count):
        forward(k, 0).start()

    @pl.loop(1, n)
    def _(t):
        emb_copy(t).wait_recv()
        for k in range(1, seq_count):
            forward(k, t).start()

    @pl.loop(1, n)
    def _(t):
        emb_copy(t).wait_send()
        grad_copy(t).wait()

    @pl.loop(0, n)
    def _(t):
        for k in range(1, seq_count):
            forward(k, t).wait()


def reduce_kernel(n, feats, slots, out, src, pair, cross, stage_b, stage_c, arrive, *sems):
    s1, r1, s2, r2, s3, r3, s4, r4, s5, r5, s6, r6 = sems
    dp, seq = lax.axis_index("dp"), lax.axis_index("seq")
    q = n // 4
    a, b, c = lax.rem(dp, 2), lax.rem(dp // 2, 2), dp // 4
    sibling = (dp + 1 - 2 * a, seq)
    across = (dp + 2 - 4 * b, seq)
    barrier = pltpu.get_barrier_semaphore()
    pl.semaphore_signal(barrier, device_id=sibling, device_id_type=MESH)
    pl.semaphore_signal(barrier, device_id=across, device_id_type=MESH)

    def ahead(t):
        return lax.rem(c + t, q)

    def behind(t):
        return lax.rem(c - t + q, q)

    def along(t):
        return (ahead(t) * 4 + b * 2 + a, seq)

    @pl.loop(1, q)
    def _(t):
        pl.semaphore_signal(barrier, device_id=along(t), device_id_type=MESH)

    rows = src.shape[3]
    tile = 512
    for first in range(0, n * rows, tile):
        product = lax.dot_general(
            feats[:, first : first + tile],
            slots[...],
            (((0,), (0,)), ((), ())),
            preferred_element_type=F32,
        ).astype(BF16)
        for i in range(tile // rows):
            k = first // rows + i
            src[k // (2 * q), k // q % 2, k % q] = product[i * rows : (i + 1) * rows]

    pl.semaphore_wait(barrier, q + 1)

    def side(i):
        return 1 - b if i == 0 else b

    def to_sibling(i, t):
        return remote(
            src.at[1 - a, side(i), ahead(t)], pair.at[i, t], s1.at[i, t], r1.at[i, t], sibling
        )

    def to_across(t):
        return remote(stage_b.at[t], cross.at[t], s2.at[t], r2.at[t], across)

    def to_owner(t):
        return remote(stage_c.at[t], arrive.at[t], s3.at[t], r3.at[t], along(t))

    def result_along(t):
        block = out.at[a, b, c]
        return remote(block, block, s4.at[t], r4.at[t], along(t))

    def result_across(t):
        block = out.at[a, b, behind(t)]
        return remote(block, block, s5.at[t], r5.at[t], across)

    def result_sibling(i, t):
        block = out.at[a, side(i), behind(t)]
        return remote(block, block, s6.at[i, t], r6.at[i, t], sibling)

    for i in (0, 1):

        @pl.loop(1, q + 1)
        def _(t):
            to_sibling(i, lax.rem(t, q)).start()

    @pl.loop(1, q + 1)
    def _(step):
        t = lax.rem(step, q)
        to_sibling(0, t).wait_recv()
        stage_b[t] = (src[a, 1 - b, ahead(t)].astype(F32) + pair[0, t].astype(F32)).astype(BF16)
        to_across(t).start()

    @pl.loop(1, q + 1)
    def _(step):
        t = lax.rem(step, q)
        to_sibling(1, t).wait_recv()
        to_across(t).wait_recv()
        stage_c[t] = (
            src[a, b, ahead(t)].astype(F32) + pair[1, t].astype(F32) + cross[t].astype(F32)
        ).astype(BF16)

        @pl.when(step < q)
        def _():
            to_owner(t).start()

    total = stage_c[0].astype(F32)
    for t in range(1, q):
        to_owner(t).wait_recv()
        total = total + arrive[t].astype(F32)
    out[a, b, c] = total.astype(BF16)

    @pl.loop(1, q)
    def _(t):
        result_along(t).start()

    result_across(0).start()
    result_sibling(1, 0).start()

    @pl.loop(1, q)
    def _(t):
        result_along(t).wait_recv()
        result_across(t).start()
        result_sibling(1, t).start()

    @pl.loop(0, q)
    def _(t):
        result_across(t).wait_recv()
        result_sibling(0, t).start()

    @pl.loop(1, q)
    def _(t):
        to_owner(t).wait_send()
        result_along(t).wait_send()

    for i in (0, 1):

        @pl.loop(0, q)
        def _(t):
            to_sibling(i, t).wait_send()
            result_sibling(i, t).wait()

    @pl.loop(0, q)
    def _(t):
        to_across(t).wait_send()
        result_across(t).wait_send()


VM = pl.BlockSpec(memory_space=pltpu.VMEM)
DMA = pltpu.SemaphoreType.DMA


def exchange(kernel, ident, outs, scratch, *operands):
    return pl.pallas_call(
        kernel,
        out_shape=tuple(jax.ShapeDtypeStruct(shape, kind) for shape, kind in outs),
        in_specs=[VM] * len(operands),
        out_specs=tuple([VM] * len(outs)),
        scratch_shapes=scratch,
        compiler_params=pltpu.CompilerParams(
            collective_id=ident, has_side_effects=True, vmem_limit_bytes=32 * 1024 * 1024
        ),
        cost_estimate=pl.CostEstimate(
            flops=10_000_000_000, bytes_accessed=10_000_000, transcendentals=0
        ),
    )(*operands)


def put_rows(whole, rows, low, high):
    pieces = [whole[:low]] if low else []
    pieces.append(rows)
    if high < whole.shape[0]:
        pieces.append(whole[high:])
    return jnp.concatenate(pieces, axis=0)


def attention_kernel(
    seq_count,
    nearby,
    meta_ref,
    rows_ref,
    gain_ref,
    wq_ref,
    wk_ref,
    wv_ref,
    wo_ref,
    emb_ref,
    branch_ref,
    normed,
    context,
):
    step = pl.program_id(0)
    me = meta_ref[0]
    count = meta_ref[1]
    part = nearby // DILATION_STEP
    own = pl.multiple_of(me * nearby, nearby)

    @pl.when(step == 0)
    def _():
        for block in range(seq_count):
            at = slice(block * nearby, (block + 1) * nearby)
            wide = jnp.concatenate(
                [rows_ref[c, at, :] for c in range(seq_count)], axis=-1
            ).astype(F32)
            center = jnp.mean(wide, axis=-1, keepdims=True)
            spread = jnp.mean(jnp.square(wide - center), axis=-1, keepdims=True)
            normed[at, :] = (
                (wide - center) * lax.rsqrt(spread + EPSILON) * gain_ref[...]
            ).astype(BF16)

    mine = normed[pl.ds(own, nearby), :]
    query = jnp.dot(mine, wq_ref[...], preferred_element_type=F32).astype(BF16)
    query = query * BF16(HEAD_WIDTH**-0.5)
    key = jnp.dot(mine, wk_ref[...], preferred_element_type=F32).astype(BF16)
    value = jnp.dot(mine, wv_ref[...], preferred_element_type=F32).astype(BF16)
    far_keys, far_values = [], []
    for other in range(1, seq_count):
        block = lax.rem(me + other, seq_count)
        start = pl.multiple_of(block * nearby, nearby)
        theirs = normed[pl.ds(start, nearby), :]
        far_keys.append(jnp.dot(theirs, wk_ref[...], preferred_element_type=F32).astype(BF16))
        far_values.append(jnp.dot(theirs, wv_ref[...], preferred_element_type=F32).astype(BF16))

    lane = lax.broadcasted_iota(jnp.int32, (1, nearby), 1)
    key_ok = own + (lane % part) * DILATION_STEP + lane // part < count
    row = lax.broadcasted_iota(jnp.int32, (nearby, 1), 0)
    query_ok = own + (row % part) * DILATION_STEP + row // part < count
    far_lane = lax.broadcasted_iota(jnp.int32, (1, part * (seq_count - 1)), 1)
    far_block = lax.rem(me + 1 + far_lane // part, seq_count)
    far_spot = far_block * nearby + far_lane % part * DILATION_STEP
    dims = (((1,), (1,)), ((), ()))
    outs = []
    for head in range(STEP_HEADS):
        shift = head % DILATION_STEP
        cols = slice(head * HEAD_WIDTH, (head + 1) * HEAD_WIDTH)
        low, high = shift * part, (shift + 1) * part
        q, k, v = query[:, cols], key[:, cols], value[:, cols]
        scores = lax.dot_general(q, k, dims, preferred_element_type=F32)
        scores = jnp.where(key_ok, scores, NEGATIVE)
        maximum = jnp.max(scores, axis=-1, keepdims=True)
        far_k = jnp.concatenate([x[low:high, cols] for x in far_keys], axis=0)
        far_v = jnp.concatenate([x[low:high, cols] for x in far_values], axis=0)
        far_ok = far_spot + shift < count
        far = lax.dot_general(q[low:high], far_k, dims, preferred_element_type=F32)
        far = jnp.where(far_ok, far, NEGATIVE)
        far_max = jnp.maximum(maximum[low:high], jnp.max(far, axis=-1, keepdims=True))
        maximum = put_rows(maximum, far_max, low, high)
        weight = jnp.exp(scores - maximum)
        in_lane = (lane >= low) & (lane < high)
        twice = jnp.where(in_lane, weight[low:high] * 2.0, weight[low:high])
        weight = put_rows(weight, twice, low, high)
        far_weight = jnp.exp(far - far_max)
        total = jnp.sum(weight, axis=-1, keepdims=True)
        far_total = jnp.sum(far_weight, axis=-1, keepdims=True)
        total = put_rows(total, total[low:high] + far_total, low, high)
        gathered = jnp.dot(weight.astype(BF16), v, preferred_element_type=F32)
        far_gathered = jnp.dot(far_weight.astype(BF16), far_v, preferred_element_type=F32)
        gathered = put_rows(gathered, gathered[low:high] + far_gathered, low, high)
        outs.append(jnp.where(query_ok, gathered / total, 0.0).astype(BF16))
    context[step] = jnp.concatenate(outs, axis=-1)

    @pl.when(step == pl.num_programs(0) - 1)
    def _():
        at_row = lax.broadcasted_iota(jnp.int32, (nearby, nearby), 0)
        at_lane = lax.broadcasted_iota(jnp.int32, (nearby, nearby), 1)
        natural = (at_lane % part) * DILATION_STEP + at_lane // part
        back = jnp.where(at_row == natural, 1.0, 0.0).astype(BF16)
        ordered = jnp.concatenate(
            [rows_ref[c, pl.ds(own, nearby), :] for c in range(seq_count)], axis=-1
        )
        emb_ref[...] = jnp.dot(back, ordered, preferred_element_type=F32).astype(BF16)
        whole = jnp.concatenate(
            [context[i] for i in range(HEAD_COUNT // STEP_HEADS)], axis=-1
        )
        whole = jnp.dot(back, whole, preferred_element_type=F32).astype(BF16)
        branch_ref[...] = jnp.dot(whole, wo_ref[...], preferred_element_type=F32).astype(BF16)


def attend(meta, rows, gain, weights, seq_count, nearby):
    width = STEP_HEADS * HEAD_WIDTH
    steps = HEAD_COUNT // STEP_HEADS
    slide_len = rows.shape[1]
    full = lambda *shape: pl.BlockSpec(shape, lambda i: (0,) * len(shape))
    out = jax.ShapeDtypeStruct((nearby, D), BF16)
    return pl.pallas_call(
        functools.partial(attention_kernel, seq_count, nearby),
        out_shape=(out, out),
        grid=(steps,),
        in_specs=[
            pl.BlockSpec(memory_space=pltpu.SMEM),
            full(*rows.shape),
            full(1, D),
            pl.BlockSpec((D, width), lambda i: (0, i)),
            pl.BlockSpec((D, width), lambda i: (0, steps + i)),
            pl.BlockSpec((D, width), lambda i: (0, 2 * steps + i)),
            pl.BlockSpec((D, D), lambda i: (0, 3)),
        ],
        out_specs=(full(nearby, D), full(nearby, D)),
        scratch_shapes=[
            pltpu.VMEM((slide_len, D), BF16),
            pltpu.VMEM((steps, nearby, width), BF16),
        ],
        compiler_params=pltpu.CompilerParams(vmem_limit_bytes=60 * 1024 * 1024),
        cost_estimate=pl.CostEstimate(
            flops=20_000_000_000, bytes_accessed=20_000_000, transcendentals=1_000_000
        ),
    )(meta, rows, gain, weights, weights, weights, weights)


def local(tile_feats, tile_pos, slide_count, w_proj, emb_grad, ln_gain, w_qkv, w_out):
    seq_count = lax.axis_size("seq")
    n = lax.axis_size("dp")
    seq_index = lax.axis_index("seq")
    slot_rows = tile_feats.shape[0]
    nearby = emb_grad.shape[1]
    slide_len = nearby * seq_count
    part = nearby // DILATION_STEP
    most = slot_rows // n
    width = w_proj.shape[1]
    weights = lax.all_gather(
        jnp.concatenate([w_qkv, w_out], axis=1), "dp", axis=0, tiled=True
    )
    emb_part = jnp.dot(tile_feats, w_proj, preferred_element_type=F32).astype(BF16)
    positions, arrived, slot_grad = exchange(
        functools.partial(dispatch_kernel, n, seq_count),
        1,
        [
            ((n, 1, most), jnp.int32),
            ((seq_count, n, most, width), BF16),
            ((n, most, width), BF16),
        ],
        [pltpu.VMEM((seq_count, nearby, width), BF16), pltpu.VMEM((n, most, width), BF16)]
        + [DMA((n,))] * 2
        + [DMA((seq_count,))] * 2
        + [DMA((n,))] * 4
        + [DMA((seq_count, n))] * 2,
        tile_pos.reshape(n, 1, most),
        emb_grad.reshape(nearby, seq_count, width).transpose(1, 0, 2),
        emb_part.reshape(n, most, width),
    )
    positions = positions.reshape(slot_rows)
    spot = jnp.arange(slide_len, dtype=jnp.int32)
    features = tile_feats.shape[1]
    quarter = n // 4
    shape = (2, 2, quarter, features // n, width)
    (summed,) = exchange(
        functools.partial(reduce_kernel, n),
        3,
        [(shape, BF16)],
        [pltpu.VMEM(shape, BF16), pltpu.VMEM(shape[1:], BF16)]
        + [pltpu.VMEM(shape[2:], BF16)] * 4
        + [DMA((2, quarter))] * 2
        + [DMA((quarter,))] * 8
        + [DMA((2, quarter))] * 2,
        tile_feats,
        slot_grad.reshape(slot_rows, width),
    )
    proj_grad = summed.reshape(features, width).astype(F32)

    inside = spot % nearby
    at_spot = spot - inside + (inside % part) * DILATION_STEP + inside // part
    hot_perm = (at_spot[:, None] == positions[None, :]).astype(BF16)
    rows = jnp.einsum(
        "ps,csw->cpw",
        hot_perm,
        arrived.reshape(seq_count, slot_rows, width),
        preferred_element_type=F32,
    ).astype(BF16)
    meta = jnp.stack([seq_index.astype(jnp.int32), slide_count[0]])
    local_emb, attn_branch = attend(
        meta, rows, ln_gain.reshape(1, D), weights, seq_count, nearby
    )
    return (local_emb[None], attn_branch[None], proj_grad)


SPLIT = 5
HBM = pl.BlockSpec(memory_space=pltpu.HBM)
NT = (((1,), (1,)), ((), ()))
TN = (((0,), (0,)), ((), ()))


def fused_kernel(
    n,
    feats_hbm,
    pos_hbm,
    slide_count,
    wproj_hbm,
    grad,
    gain_hbm,
    wqkv_hbm,
    wout_hbm,
    emb_ref,
    branch_ref,
    out,
    feats,
    wproj,
    pos,
    gain,
    wqkv,
    wout,
    emb,
    pos_in,
    pos_all,
    emb_all,
    grad_rows,
    picked,
    slots,
    wts,
    wts_x,
    normed,
    qkv,
    ctx_send,
    ctx_own,
    ctx_peer,
    src,
    pair,
    cross,
    stage_y,
    stage_za,
    stage_zb,
    in_za,
    in_zb,
    stage_yb,
    cross_b,
    local_sems,
    xs,
    xr,
    ps,
    pr,
    es,
    er,
    fs,
    fr,
    gs,
    gr,
    us,
    ur,
    ds_,
    dr,
    ys,
    yr,
    cs,
    cr,
    wxs,
    wxr,
    ks,
    kr,
    s1,
    r1,
    s2,
    r2,
    s3,
    r3,
    s4,
    r4,
    gus,
    gur,
    gds,
    gdr,
    gys,
    gyr,
    gbs,
    gbr,
    gcs,
    gcr,
    gxs,
    gxr,
):
    dp, seq = lax.axis_index("dp"), lax.axis_index("seq")
    q = n // 4
    a, b, c = lax.rem(dp, 2), lax.rem(dp // 2, 2), dp // 4
    x_peer = (dp, 1 - seq)
    sib_dp = dp + 1 - 2 * a
    y_dp = dp + 2 - 4 * b
    sibling, across = (sib_dp, seq), (y_dp, seq)
    most = pos_in.shape[2]
    slot_rows = feats.shape[0]
    nearby = grad.shape[1]
    width = wproj.shape[1]
    depth = wqkv.shape[0]
    part = nearby // DILATION_STEP
    inner = HEAD_COUNT * HEAD_WIDTH
    wide = 3 * width

    barrier = pltpu.get_barrier_semaphore()

    @pl.loop(1, n)
    def _(t):
        pl.semaphore_signal(barrier, device_id=(lax.rem(dp + t, n), seq), device_id_type=MESH)

    pl.semaphore_signal(barrier, device_id=x_peer, device_id_type=MESH)
    def feats_copy(step):
        which = lax.rem(c * 2 // q + 1 + step, 2)
        half_rows = slot_rows // 2
        at = pl.ds(pl.multiple_of(which * half_rows, half_rows), half_rows)
        return pltpu.make_async_copy(feats_hbm.at[at], feats.at[at], local_sems.at[7 + step])

    wproj_copy = pltpu.make_async_copy(wproj_hbm, wproj, local_sems.at[1])
    pos_load = pltpu.make_async_copy(pos_hbm, pos, local_sems.at[3])
    gain_load = pltpu.make_async_copy(gain_hbm, gain, local_sems.at[4])
    wqkv_load = pltpu.make_async_copy(wqkv_hbm, wqkv, local_sems.at[5])
    wout_load = pltpu.make_async_copy(wout_hbm, wout, local_sems.at[6])
    pos_load.start()
    wqkv_load.start()
    wout_load.start()
    gain_load.start()
    wproj_copy.start()
    feats_copy(0).start()
    feats_copy(1).start()
    pos_load.wait()
    for i in range(n):
        pos_in[i] = pos[:, i * most : (i + 1) * most]
    wqkv_load.wait()
    wout_load.wait()
    gain_load.wait()
    mine_w = pl.ds(pl.multiple_of(dp * depth, 16), depth)
    half = pl.multiple_of(seq * width, width)
    for i in range(3):
        wts[mine_w, i * width : (i + 1) * width] = wqkv[
            :, pl.ds(pl.multiple_of(i * inner + half, 128), width)
        ]
    wts[mine_w, wide:] = wout[:, pl.ds(half, width)]
    pos_all[dp] = pos_in[dp]

    def column_copy():
        block = grad.at[0, :, pl.ds(pl.multiple_of((1 - seq) * width, 128), width)]
        return remote(block, grad_rows.at[seq], xs.at[0], xr.at[0], x_peer)

    own_columns = pltpu.make_async_copy(
        grad.at[0, :, pl.ds(half, width)], grad_rows.at[seq], local_sems.at[2]
    )
    own_columns.start()

    def pos_copy(t):
        peer = lax.rem(dp + t, n)
        return remote(pos_in.at[peer], pos_all.at[dp], ps.at[t], pr.at[t], (peer, seq))

    def emb_copy(t):
        peer = lax.rem(dp + t, n)
        return remote(
            emb.at[pl.ds(pl.multiple_of(peer * most, most), most)],
            emb_all.at[seq, dp],
            es.at[t],
            er.at[t],
            (peer, seq),
        )

    def forward(t):
        block = emb_all.at[seq, lax.rem(dp - t + n, n)]
        return remote(block, block, fs.at[t], fr.at[t], x_peer)

    def grad_send(peer):
        return remote(picked.at[peer], slots.at[dp], gs.at[peer], gr.at[dp], (peer, seq))

    def grad_recv(source):
        return remote(picked.at[source], slots.at[source], gs.at[source], gr.at[source], sibling)

    def rows_of(who):
        return pl.ds(pl.multiple_of(who * depth, 16), depth)

    def z_block(z):
        return wts.at[rows_of(z * 4 + b * 2 + a)]

    def up(hop, z):
        return remote(z_block(z), z_block(z), us.at[hop], ur.at[hop], (lax.rem(dp + 4, n), seq))

    def down(hop, z):
        return remote(z_block(z), z_block(z), ds_.at[hop], dr.at[hop], (lax.rem(dp + n - 4, n), seq))

    def y_copy(z, back=False):
        who = z * 4 + (1 - b if back else b) * 2 + a
        block = wts.at[rows_of(who)]
        return remote(block, block, ys.at[z], yr.at[z], across)

    def c_copy(side, z, back=False):
        y = b if side == 0 else 1 - b
        who = z * 4 + y * 2 + (1 - a if back else a)
        block = wts.at[rows_of(who)]
        return remote(block, block, cs.at[side, z], cr.at[side, z], sibling)

    def w_start():
        @pl.when(c < q - 1)
        def _():
            up(1, c).start()

        @pl.when(c > 0)
        def _():
            down(1, c).start()

        y_copy(c).start()
        c_copy(0, c).start()

    def w_hop(hop):
        below, above = c - hop, c + hop

        @pl.when(below >= 0)
        def _():
            up(hop, below).wait_recv()

            @pl.when(c < q - 1)
            def _():
                up(hop + 1, below).start()

            y_copy(below).start()
            c_copy(0, below).start()

        @pl.when(above < q)
        def _():
            down(hop, above).wait_recv()

            @pl.when(c > 0)
            def _():
                down(hop + 1, above).start()

            y_copy(above).start()
            c_copy(0, above).start()

    def w_side():
        @pl.loop(0, q)
        def _(t):
            z = lax.rem(c + t, q)
            y_copy(z, True).wait_recv()
            c_copy(1, z).start()

    def wx_copy():
        return remote(wts.at[:, pl.ds(wide, width)], wts_x, wxs.at[0], wxr.at[0], x_peer)

    def w_gathered():
        @pl.loop(0, q)
        def _(z):
            c_copy(0, z, True).wait_recv()
            c_copy(1, z, True).wait_recv()

        wx_copy().start()

    def w_done():
        for hop in range(1, q):

            @pl.when((c - hop + 1 >= 0) & (c < q - 1))
            def _():
                up(hop, c - hop + 1).wait_send()

            @pl.when((c + hop - 1 < q) & (c > 0))
            def _():
                down(hop, c + hop - 1).wait_send()

        @pl.loop(0, q)
        def _(z):
            y_copy(z).wait_send()
            c_copy(0, z).wait_send()
            c_copy(1, z).wait_send()

        wx_copy().wait_send()

    spot = lax.broadcasted_iota(jnp.int32, (2 * nearby, 1), 0)

    @pl.when(c == 0)
    def _():
        in_za[0] = jnp.zeros_like(in_za[0])
        in_zb[0] = jnp.zeros_like(in_zb[0])

    @pl.when(c == q - 1)
    def _():
        in_za[1] = jnp.zeros_like(in_za[1])
        in_zb[1] = jnp.zeros_like(in_zb[1])

    def first_sends():
        pl.semaphore_wait(barrier, n)
        column_copy().start()

        @pl.loop(1, n)
        def _(t):
            pos_copy(t).start()

    def embed():
        wproj_copy.wait()
        group = n // 2

        @pl.loop(0, 2)
        def _(step):
            feats_copy(step).wait()
            which = lax.rem(c * 2 // q + 1 + step, 2)
            at = pl.ds(pl.multiple_of(which * group * most, group * most), group * most)
            emb[at, :] = jnp.dot(feats[at, :], wproj[...], preferred_element_type=F32).astype(
                BF16
            )

            @pl.loop(0, group)
            def _(i):
                t = lax.rem(which * group + i - dp + n, n)

                @pl.when(t > 0)
                def _():
                    emb_copy(t).start()

    def emb_sends():
        emb_all[seq, dp] = emb[pl.ds(pl.multiple_of(dp * most, most), most), :]
        forward(0).start()

    def emb_on(low, high):
        @pl.loop(low, high)
        def _(t):
            emb_copy(t).wait_recv()
            forward(t).start()

    def grad_sends():
        @pl.loop(1, n)
        def _(t):
            pos_copy(t).wait()

        own_columns.wait()
        column_copy().wait()
        rows = jnp.concatenate([grad_rows[0], grad_rows[1]], axis=0)
        batch = 4

        @pl.loop(1, q + 1)
        def _(step):
            first = lax.rem(c + step - 1, q) * batch
            at = jnp.concatenate([pos_all[first + i] for i in range(batch)], axis=1)
            hot = jnp.where(spot == at, 1.0, 0.0).astype(BF16)
            block = lax.dot_general(hot, rows, TN, preferred_element_type=F32).astype(BF16)
            for i in range(batch):
                picked[first + i] = block[i * most : (i + 1) * most]

                @pl.when(first + i != dp)
                def _():
                    grad_send(first + i).start()

                @pl.when(first + i == dp)
                def _():
                    slots[first + i] = block[i * most : (i + 1) * most]

    count = slide_count[:, 0:1]
    own = pl.multiple_of(seq * nearby, nearby)
    far_own = pl.multiple_of((1 - seq) * nearby, nearby)

    def natural_of(index, shift):
        return (index % part) * DILATION_STEP + lax.rem(index // part + 2 * shift, DILATION_STEP)

    def regroup():
        @pl.loop(0, n)
        def _(t):
            forward(t).wait_recv()

        positions = jnp.concatenate([pos_all[i] for i in range(n)], axis=1)
        inside = spot % nearby
        at_spot = spot - inside + natural_of(inside, seq)
        hot_perm = jnp.where(at_spot == positions, 1.0, 0.0).astype(BF16)
        own_spot = lax.broadcasted_iota(jnp.int32, (nearby, 1), 0) + seq * nearby
        hot_own = jnp.where(own_spot == positions, 1.0, 0.0).astype(BF16)
        blocks = [emb_all[i].reshape(slot_rows, width) for i in range(2)]
        for i in range(2):
            emb_ref[:, i * width : (i + 1) * width] = jnp.dot(
                hot_own, blocks[i], preferred_element_type=F32
            ).astype(BF16)
        for block in range(2):
            at = slice(block * nearby, (block + 1) * nearby)
            row = jnp.concatenate(
                [jnp.dot(hot_perm[at], blocks[i], preferred_element_type=F32) for i in range(2)],
                axis=-1,
            )
            center = jnp.mean(row, axis=-1, keepdims=True)
            spread = jnp.mean(jnp.square(row - center), axis=-1, keepdims=True)
            normed[at, :] = (
                (row - center) * lax.rsqrt(spread + EPSILON) * gain[...][None, :]
            ).astype(BF16)

    rows_each = src.shape[3]
    cut = rows_each * SPLIT // 8
    at_a, at_b = pl.ds(0, cut), pl.ds(cut, rows_each - cut)
    both = pl.ds(0, 2)

    def to_sibling(part, y, k):
        at = (at_a, at_b)[part]
        return remote(
            src.at[1 - a, y, k, at],
            pair.at[y, k, at],
            s1.at[part, y, k],
            r1.at[part, y, k],
            sibling,
        )

    def turn(j):
        return lax.select(c < q // 2, q - 1 - j, j)

    def send_pairs(y):
        for part in range(2):
            for j in range(q):
                to_sibling(part, y, turn(j)).start()

    def to_across(k):
        return remote(stage_y.at[k], cross.at[k], s2.at[k], r2.at[k], across)

    def to_z(part, d, k):
        stage, land = ((stage_za, in_za), (stage_zb, in_zb))[part]
        peer = lax.rem(dp + n + 4 - 8 * d, n)
        return remote(stage.at[k], land.at[d, k], s3.at[part, k], r3.at[part, d, k], (peer, seq))

    def to_across_b():
        return remote(stage_yb, cross_b, s4.at[0], r4.at[0], across)

    def block_of(part, k):
        return out.at[a, b, k, at_a] if part == 0 else out.at[a, both, k, at_b]

    def go_up(part, hop, k):
        block = block_of(part, k)
        device = (lax.rem(dp + 4, n), seq)
        return remote(block, block, gus.at[part, hop], gur.at[part, hop], device)

    def go_down(part, hop, k):
        block = block_of(part, k)
        device = (lax.rem(dp + n - 4, n), seq)
        return remote(block, block, gds.at[part, hop], gdr.at[part, hop], device)

    def go_across(k):
        block = out.at[a, b, k, at_a]
        return remote(block, block, gys.at[k], gyr.at[k], across)

    def go_across_b():
        block = out.at[a, b, c, at_b]
        return remote(block, block, gbs.at[0], gbr.at[0], across)

    def go_sibling(side, k):
        block = out.at[a, b if side == 0 else 1 - b, k, at_a]
        return remote(block, block, gcs.at[side, k], gcr.at[side, k], sibling)

    def go_sibling_b(k):
        block = out.at[a, both, k, at_b]
        return remote(block, block, gxs.at[k], gxr.at[k], sibling)

    def product():
        @pl.loop(0, n)
        def _(source):
            @pl.when(source != dp)
            def _():
                grad_recv(source).wait_recv()

        grads = slots[...].reshape(slot_rows, width)
        tile = q * rows_each

        @pl.loop(0, n // q)
        def _(step):
            core = lax.rem(1 - a + step // 2, 2)
            y = lax.rem(1 - b + step, 2)
            first = pl.multiple_of((core * 2 + y) * tile, tile)
            product = lax.dot_general(
                feats[:, pl.ds(first, tile)], grads, TN, preferred_element_type=F32
            ).astype(BF16)
            for i in range(q):
                src[core, y, i] = product[i * rows_each : (i + 1) * rows_each]

            @pl.when(step < 2)
            def _():
                send_pairs(y)

    def sum_y(j):
        k = turn(j)
        to_sibling(0, 1 - b, k).wait_recv()
        stage_y[k] = (
            src[a, 1 - b, k, at_a].astype(F32) + pair[1 - b, k, at_a].astype(F32)
        ).astype(BF16)
        to_across(k).start()

    def term_a(k):
        return (
            src[a, b, k, at_a].astype(F32)
            + pair[b, k, at_a].astype(F32)
            + cross[k].astype(F32)
        )

    def term_b(k):
        return src[a, both, k, at_b].astype(F32) + pair[both, k, at_b].astype(F32)

    def ready(part, k):
        if part == 0:
            to_sibling(0, b, k).wait_recv()
            to_across(k).wait_recv()
        else:
            to_sibling(1, 0, k).wait_recv()
            to_sibling(1, 1, k).wait_recv()

    def sum_z(part, j):
        k = turn(j)
        term, stage, land = ((term_a, stage_za, in_za), (term_b, stage_zb, in_zb))[part]
        ready(part, k)

        @pl.when(k > c)
        def _():
            @pl.when(c > 0)
            def _():
                to_z(part, 0, k).wait_recv()

            stage[k] = (term(k) + land[0, k].astype(F32)).astype(BF16)
            to_z(part, 0, k).start()

        @pl.when(k < c)
        def _():
            @pl.when(c < q - 1)
            def _():
                to_z(part, 1, k).wait_recv()

            stage[k] = (term(k) + land[1, k].astype(F32)).astype(BF16)
            to_z(part, 1, k).start()

    def own_in(part):
        @pl.when(c > 0)
        def _():
            to_z(part, 0, c).wait_recv()

        @pl.when(c < q - 1)
        def _():
            to_z(part, 1, c).wait_recv()

    def hand_on(part, k):
        if part == 0:
            go_across(k).start()
            go_sibling(0, k).start()
        else:
            go_sibling_b(k).start()

    def share(part):
        @pl.when(c < q - 1)
        def _():
            go_up(part, 1, c).start()

        @pl.when(c > 0)
        def _():
            go_down(part, 1, c).start()

        hand_on(part, c)

    def own_a():
        own_in(0)
        out[a, b, c, at_a] = (
            term_a(c) + in_za[0, c].astype(F32) + in_za[1, c].astype(F32)
        ).astype(BF16)
        share(0)

    def own_b():
        own_in(1)
        stage_yb[...] = (
            src[a, 1 - b, c, at_b].astype(F32)
            + pair[1 - b, c, at_b].astype(F32)
            + in_zb[0, c, 1 - b].astype(F32)
            + in_zb[1, c, 1 - b].astype(F32)
        ).astype(BF16)
        to_across_b().start()

    def whole_b():
        to_across_b().wait_recv()
        out[a, b, c, at_b] = (
            src[a, b, c, at_b].astype(F32)
            + pair[b, c, at_b].astype(F32)
            + in_zb[0, c, b].astype(F32)
            + in_zb[1, c, b].astype(F32)
            + cross_b[...].astype(F32)
        ).astype(BF16)
        go_across_b().start()

    def share_b():
        go_across_b().wait_recv()
        share(1)

    def result_hop(part, hop):
        below, above = c - hop, c + hop

        @pl.when(below >= 0)
        def _():
            go_up(part, hop, below).wait_recv()

            @pl.when(c < q - 1)
            def _():
                go_up(part, hop + 1, below).start()

            hand_on(part, below)

        @pl.when(above < q)
        def _():
            go_down(part, hop, above).wait_recv()

            @pl.when(c > 0)
            def _():
                go_down(part, hop + 1, above).start()

            hand_on(part, above)

    def result_over(j):
        k = lax.rem(c + j, q)
        go_across(k).wait_recv()
        go_sibling(1, k).start()

    def reduce_done():
        @pl.loop(0, q)
        def _(k):
            for y in range(2):
                for part in range(2):
                    to_sibling(part, y, k).wait_send()
                go_sibling(y, k).wait()
            to_across(k).wait_send()
            go_across(k).wait_send()
            go_sibling_b(k).wait()

            @pl.when(k != c)
            def _():
                for part in range(2):
                    to_z(part, 0, k).wait_send()

        to_across_b().wait_send()
        go_across_b().wait_send()
        for part in range(2):
            for hop in range(1, q):

                @pl.when((c - hop + 1 >= 0) & (c < q - 1))
                def _():
                    go_up(part, hop, c - hop + 1).wait_send()

                @pl.when((c + hop - 1 < q) & (c > 0))
                def _():
                    go_down(part, hop, c + hop - 1).wait_send()

    lane = lax.broadcasted_iota(jnp.int32, (1, nearby), 1)
    row_at = lax.broadcasted_iota(jnp.int32, (nearby, 1), 0)
    far_lane = lax.broadcasted_iota(jnp.int32, (1, part), 1)

    def project(which):
        cols = slice(which * width, (which + 1) * width)
        value = jnp.dot(normed[...], wts[:, cols], preferred_element_type=F32).astype(BF16)
        if which == 0:
            value = value * BF16(HEAD_WIDTH**-0.5)
        qkv[which] = value

    def attend_head(start, other, head):
        group = head % DILATION_STEP
        cols = slice(head * HEAD_WIDTH, (head + 1) * HEAD_WIDTH)
        low, high = group * part, (group + 1) * part
        key_ok = start + natural_of(lane, seq) < count
        query_ok = start + natural_of(row_at, seq) < count
        far_ok = (
            other + far_lane * DILATION_STEP + lax.rem(group + 2 * seq, DILATION_STEP) < count
        )
        here = pl.ds(start, nearby)
        there = pl.ds(pl.multiple_of(other + low, part), part)
        qh, kh, vh = (qkv[i, here, :][:, cols] for i in range(3))
        far_k, far_v = (qkv[i, there, :][:, cols] for i in (1, 2))
        scores = lax.dot_general(qh, kh, NT, preferred_element_type=F32)
        scores = jnp.where(key_ok, scores, NEGATIVE)
        maximum = jnp.max(scores, axis=-1, keepdims=True)
        far = lax.dot_general(qh[low:high], far_k, NT, preferred_element_type=F32)
        far = jnp.where(far_ok, far, NEGATIVE)
        far_max = jnp.maximum(maximum[low:high], jnp.max(far, axis=-1, keepdims=True))
        maximum = put_rows(maximum, far_max, low, high)
        weight = jnp.exp(scores - maximum)
        in_lane = (lane >= low) & (lane < high)
        twice = jnp.where(in_lane, weight[low:high] * 2.0, weight[low:high])
        weight = put_rows(weight, twice, low, high)
        far_weight = jnp.exp(far - far_max)
        total = jnp.sum(weight, axis=-1, keepdims=True)
        far_total = jnp.sum(far_weight, axis=-1, keepdims=True)
        total = put_rows(total, total[low:high] + far_total, low, high)
        gathered = jnp.dot(weight.astype(BF16), vh, preferred_element_type=F32)
        far_gathered = jnp.dot(far_weight.astype(BF16), far_v, preferred_element_type=F32)
        gathered = put_rows(gathered, gathered[low:high] + far_gathered, low, high)
        return jnp.where(query_ok, gathered / total, 0.0).astype(BF16)

    def ctx_copy(j):
        at = pl.ds(j * 128, 128)
        return remote(ctx_send.at[:, at], ctx_peer.at[:, at], ks.at[j], kr.at[j], x_peer)

    pairs = width // 128

    def heads(mine, j):
        start, other = (own, far_own) if mine else (far_own, own)
        block = jnp.concatenate(
            [attend_head(start, other, 2 * j + i) for i in range(2)], axis=-1
        )
        at = pl.ds(j * 128, 128)
        if mine:
            ctx_own[:, at] = block
        else:
            ctx_send[:, at] = block
            ctx_copy(j).start()

    def finish_branch():
        for j in range(pairs):
            ctx_copy(j).wait()
        wx_copy().wait_recv()
        at_row = lax.broadcasted_iota(jnp.int32, (nearby, nearby), 0)
        at_lane = lax.broadcasted_iota(jnp.int32, (nearby, nearby), 1)
        ordered = []
        for shift, ref in ((seq, ctx_own), (1 - seq, ctx_peer)):
            back = jnp.where(at_row == natural_of(at_lane, shift), 1.0, 0.0).astype(BF16)
            ordered.append(jnp.dot(back, ref[...], preferred_element_type=F32).astype(BF16))
        for cols, weight in ((seq, wts.at[:, pl.ds(wide, width)]), (1 - seq, wts_x)):
            total = None
            for value, owner in zip(ordered, (seq, 1 - seq)):
                at = pl.ds(pl.multiple_of(owner * width, width), width)
                term = jnp.dot(value, weight[at, :], preferred_element_type=F32)
                total = term if total is None else total + term
            branch_ref[:, pl.ds(pl.multiple_of(cols * width, width), width)] = total.astype(BF16)

    do = functools.partial

    sums = [do(sum_y, 0), do(sum_y, 1), do(sum_z, 1, 0), do(sum_y, 2), do(sum_y, 3)]
    for j in range(1, q):
        sums += [do(sum_z, 1, j), do(sum_z, 0, j - 1)]
    sums += [own_b, do(sum_z, 0, q - 1), whole_b, own_a, share_b]
    for hop in range(1, q):
        sums += [do(result_hop, 0, hop), do(result_hop, 1, hop)]
    sums += [do(result_over, j) for j in range(q)]

    def merge(jobs, others, tail=2):
        mixed, taken = [], 0
        for i, job in enumerate(jobs):
            until = (i + 1) * len(others) // (len(jobs) + tail)
            mixed += [job] + others[taken:until]
            taken = until
        return mixed + others[taken:]
    steps = [first_sends, embed, emb_sends, grad_sends, w_start, do(emb_on, 1, n), regroup, do(w_hop, 1), product]
    steps += sums[0:5] + [do(w_hop, 2)]
    steps += sums[5:8] + [do(w_hop, 3)]
    steps += sums[8:10] + [w_side]
    sums = sums[10:]
    work = [w_gathered]
    work += [do(project, i) for i in range(3)]
    work += [do(heads, False, j) for j in range(pairs)]
    work += [do(heads, True, j) for j in range(pairs)]
    work += [finish_branch]

    steps += merge(work, sums, 2)
    for step in steps:
        step()

    @pl.loop(1, n)
    def _(t):
        emb_copy(t).wait_send()

    @pl.loop(0, n)
    def _(t):
        forward(t).wait_send()

        @pl.when(t != dp)
        def _():
            grad_send(t).wait_send()

    w_done()
    reduce_done()


def finish_kernel(emb, branch, summed, emb_out, branch_out, grad_out, wide, sems):
    copies = [
        pltpu.make_async_copy(emb, emb_out.at[0], sems.at[0]),
        pltpu.make_async_copy(branch, branch_out.at[0], sems.at[1]),
    ]
    for copy in copies:
        copy.start()
    size = summed.shape[0] // 4
    for i in range(4):
        at = pl.ds(i * size, size)
        wide[at, :] = summed[at, :].astype(F32)
        copies.append(pltpu.make_async_copy(wide.at[at], grad_out.at[at], sems.at[2 + i]))
        copies[-1].start()
    for copy in copies:
        copy.wait()


def finish(emb, branch, summed):
    return pl.pallas_call(
        finish_kernel,
        out_shape=(
            jax.ShapeDtypeStruct((1, *emb.shape), BF16),
            jax.ShapeDtypeStruct((1, *branch.shape), BF16),
            jax.ShapeDtypeStruct(summed.shape, F32),
        ),
        in_specs=[VM] * 3,
        out_specs=(HBM,) * 3,
        scratch_shapes=[pltpu.VMEM(summed.shape, F32), DMA((6,))],
        compiler_params=pltpu.CompilerParams(vmem_limit_bytes=16 * 1024 * 1024),
        cost_estimate=pl.CostEstimate(flops=0, bytes_accessed=6_000_000, transcendentals=0),
    )(emb, branch, summed)


def in_hbm(operand):
    return pltpu.with_memory_space_constraint(operand, pltpu.HBM)


def fused(tile_feats, tile_pos, slide_count, w_proj, emb_grad, ln_gain, w_qkv, w_out):
    n = lax.axis_size("dp")
    slot_rows, features = tile_feats.shape
    nearby = emb_grad.shape[1]
    most = slot_rows // n
    width = w_proj.shape[1]
    q = n // 4
    shape = (2, 2, q, features // n, width)
    cut = features // n * SPLIT // 8
    part_a = (q, cut, width)
    part_b = (q, 2, features // n - cut, width)
    scratch = [
        pltpu.VMEM(tile_feats.shape, BF16),
        pltpu.VMEM(w_proj.shape, BF16),
        pltpu.VMEM(tile_pos.shape, jnp.int32),
        pltpu.VMEM(ln_gain.shape, F32),
        pltpu.VMEM(w_qkv.shape, BF16),
        pltpu.VMEM(w_out.shape, BF16),
        pltpu.VMEM((slot_rows, width), BF16),
        pltpu.VMEM((n, 1, most), jnp.int32),
        pltpu.VMEM((n, 1, most), jnp.int32),
        pltpu.VMEM((2, n, most, width), BF16),
        pltpu.VMEM((2, nearby, width), BF16),
        pltpu.VMEM((n, most, width), BF16),
        pltpu.VMEM((n, most, width), BF16),
        pltpu.VMEM((D, 4 * width), BF16),
        pltpu.VMEM((D, width), BF16),
        pltpu.VMEM((2 * nearby, D), BF16),
        pltpu.VMEM((3, 2 * nearby, width), BF16),
        pltpu.VMEM((nearby, width), BF16),
        pltpu.VMEM((nearby, width), BF16),
        pltpu.VMEM((nearby, width), BF16),
        pltpu.VMEM(shape, BF16),
        pltpu.VMEM(shape[1:], BF16),
        pltpu.VMEM(part_a, BF16),
        pltpu.VMEM(part_a, BF16),
        pltpu.VMEM(part_a, BF16),
        pltpu.VMEM(part_b, BF16),
        pltpu.VMEM((2, *part_a), BF16),
        pltpu.VMEM((2, *part_b), BF16),
        pltpu.VMEM(part_b[2:], BF16),
        pltpu.VMEM(part_b[2:], BF16),
        DMA((9,)),
    ]
    scratch += [DMA((1,))] * 2
    scratch += [DMA((n,))] * 8
    scratch += [DMA((q + 1,))] * 4
    scratch += [DMA((q,))] * 2
    scratch += [DMA((2, q))] * 2
    scratch += [DMA((1,))] * 2
    scratch += [DMA((width // 128,))] * 2
    scratch += [DMA((2, 2, q))] * 2
    scratch += [DMA((q,))] * 2
    scratch += [DMA((2, q)), DMA((2, 2, q))]
    scratch += [DMA((1,))] * 2
    scratch += [DMA((2, q + 1))] * 4
    scratch += [DMA((q,))] * 2
    scratch += [DMA((1,))] * 2
    scratch += [DMA((2, q))] * 2
    scratch += [DMA((q,))] * 2
    row = jax.ShapeDtypeStruct((nearby, D), BF16)
    emb, branch, summed = pl.pallas_call(
        functools.partial(fused_kernel, n),
        out_shape=(row, row, jax.ShapeDtypeStruct(shape, BF16)),
        in_specs=[HBM, HBM, VM, HBM, HBM, HBM, HBM, HBM],
        out_specs=(VM, VM, VM),
        scratch_shapes=scratch,
        compiler_params=pltpu.CompilerParams(
            collective_id=5, has_side_effects=True, vmem_limit_bytes=48 * 1024 * 1024
        ),
        cost_estimate=pl.CostEstimate(
            flops=5_000_000_000, bytes_accessed=10_000_000, transcendentals=1_000_000
        ),
    )(
        in_hbm(tile_feats),
        in_hbm(tile_pos),
        jnp.broadcast_to(slide_count[:, None], (1, 128)),
        in_hbm(w_proj),
        in_hbm(emb_grad),
        in_hbm(ln_gain),
        in_hbm(w_qkv),
        in_hbm(w_out),
    )
    return finish(emb, branch, summed.reshape(features, width))


def solution(mesh):
    in_specs = (
        P("dp", None),
        P("dp", None),
        P("dp"),
        P(None, "seq"),
        P("dp", "seq", None),
        P(),
        P("dp", None),
        P("dp", None),
    )
    out_specs = (P("dp", "seq", None), P("dp", "seq", None), P(None, "seq"))
    one_kernel = mesh.shape["dp"] == 16 and mesh.shape["seq"] == 2
    body = fused if one_kernel else local
    return jax.shard_map(body, mesh=mesh, in_specs=in_specs, out_specs=out_specs, check_vma=False)
```
